128 devices in a mesh: gx: 4 (over y), gy: 4 (over z), gz: 8 (over x, core).
Axes of the slice: x: 4, y: 4, z: 4, core: 2. Of those that a mesh axis runs over, the one named last changes fastest.
Arguments:
- initial: float32 [128, 128, 1024], P('gx', 'gy', 'gz'), may hold values from -6 to 6
- rhs: float32 [128, 128, 1024], P('gx', 'gy', 'gz'), may hold values from -6 to 6
- kappa: float32 [128, 128, 1024], P('gx', 'gy', 'gz'), may hold values from 0.5 to 2
- sigma: float32 [128, 128, 1024], P('gx', 'gy', 'gz'), may hold values from 0.005 to 0.05
Outputs:
- updated: float32 [128, 128, 1024], P('gx', 'gy', 'gz')
The draws below stay inside these ranges and needn't reach their ends.
All inputs are finite; a program needn't handle non-finite values.
Results may differ from the reference program's by a relative error of at most 0.00016.
Values sent between devices are 32-bit elements; how exact they have to be, the bound alone decides.
No kernel may reach another device: no remote copies, remote signals or barrier semaphores. Data moves between devices by JAX's collectives and lax.ppermute only.
A program may use at most 192 MiB of HBM per device.

```python
import math
import jax
import jax.numpy as jnp

COARSE_SWEEPS = 8
NX = 128
NY = 128
NZ = 1024


def level_of(stream_key, extent, pieces, smallest, high):
    def one(position, blocks):
        draws = jax.random.uniform(jax.random.fold_in(jax.random.fold_in(stream_key, 6), position), (blocks,), jnp.float32, smallest / len(pieces), high / len(pieces))
        return jnp.repeat(jnp.exp(draws), extent[position] // blocks).reshape((-1,) + (1,) * (len(extent) - position - 1))

    level = one(*pieces[0])
    for cut in pieces[1:]:
        level = level * one(*cut)
    return level


def bell_draw(own_key, dims, scale, bound, cuts=(), dtype=jnp.bfloat16):
    values = jax.random.normal(own_key, dims, jnp.float32) * scale
    if len(cuts) > 0:
        values = level_of(own_key, dims, cuts, -0.22, 0.18) * values
    return jnp.clip(values, min=-bound, max=bound).astype(dtype)


def setup_inputs(seed: int = 0) -> dict:
    seeds = jax.random.split(jax.random.key(seed), 5)
    return {
        "initial": bell_draw(seeds[0], (NX, NY, NZ), 1.0, 6.0, ((0, 4), (1, 4), (2, 8)), jnp.float32),
        "rhs": bell_draw(seeds[1], (NX, NY, NZ), 1.0, 6.0, ((0, 4), (1, 4), (2, 8)), jnp.float32),
        "kappa": jnp.clip(jnp.exp(math.log(2.0) - 1.3862944 * jax.random.uniform(seeds[2], (NX, NY, NZ), jnp.float32) ** level_of(seeds[2], (NX, NY, NZ), ((0, 4), (1, 4), (2, 8)), -0.2, 0.2)), 0.5, 2.0),
        "sigma": jnp.clip(jnp.exp(math.log(0.05) - 2.3025851 * jax.random.uniform(seeds[3], (NX, NY, NZ), jnp.float32) ** level_of(seeds[3], (NX, NY, NZ), ((0, 4), (1, 4), (2, 8)), -0.2, 0.2)), 0.005, 0.05),
    }


jacobi_weight = 0.8


def neighbours(padded):
    return [padded[2:, 1:-1, 1:-1], padded[:-2, 1:-1, 1:-1],
            padded[1:-1, 2:, 1:-1], padded[1:-1, :-2, 1:-1],
            padded[1:-1, 1:-1, 2:], padded[1:-1, 1:-1, :-2]]


def face_list(kappa_pad):
    center = kappa_pad[1:-1, 1:-1, 1:-1]
    return [0.5 * (center + other) for other in neighbours(kappa_pad)]


def operate(field_pad, faces, shift):
    center = field_pad[1:-1, 1:-1, 1:-1]
    total = shift * center
    for face, other in zip(faces, neighbours(field_pad)):
        total = total + face * (center - other)
    return total


def diagonal_of(faces, shift):
    total = shift
    for face in faces:
        total = total + face
    return total


def coarsen(field):
    sizes = field.shape
    blocks = field.reshape(sizes[0] // 2, 2, sizes[1] // 2, 2, sizes[2] // 2, 2)
    return blocks.mean(axis=(1, 3, 5))


def refine(field):
    return jnp.repeat(jnp.repeat(jnp.repeat(field, 2, 0), 2, 1), 2, 2)


def pad_wrap(field):
    return jnp.pad(field, 1, mode="wrap")


def smooth(source, faces, shift, sweeps):
    diagonal = diagonal_of(faces, shift)
    result = jacobi_weight * source / diagonal
    for sweep in range(sweeps - 1):
        result = result + jacobi_weight * (source - operate(pad_wrap(result), faces, shift)) / diagonal
    return result


def reference(initial, rhs, kappa, sigma):
    faces = face_list(pad_wrap(kappa))
    residual = rhs - operate(pad_wrap(initial), faces, sigma)
    rests = [residual]
    kappas = [kappa]
    shifts = [sigma]
    for level in range(5):
        rests.append(4.0 * coarsen(rests[-1]))
        kappas.append(coarsen(kappas[-1]))
        shifts.append(4.0 * coarsen(shifts[-1]))
    line_rest = jnp.mean(rests[-1], axis=2, keepdims=True)
    line_kappa = jnp.mean(kappas[-1], axis=2, keepdims=True)
    line_shift = jnp.mean(shifts[-1], axis=2, keepdims=True)
    total = smooth(line_rest, face_list(pad_wrap(line_kappa)), line_shift, COARSE_SWEEPS)
    for level in (5, 4, 3, 2, 1, 0):
        sweeps = 2 if level < 2 else COARSE_SWEEPS
        level_faces = faces if level == 0 else face_list(pad_wrap(kappas[level]))
        correction = smooth(rests[level], level_faces, shifts[level], sweeps)
        if level == 5:
            total = correction + jnp.broadcast_to(total, correction.shape)
        else:
            total = correction + refine(total)
    return initial + total
```

```python
import jax
import jax.numpy as jnp
from jax import lax
from jax.experimental import pallas as pl
from jax.experimental.pallas import tpu as pltpu
from jax.sharding import PartitionSpec as P

COARSE_SWEEPS = 8
WEIGHT = 0.8
LANES = 128
F32 = jnp.float32
BF16 = jnp.bfloat16

Z_FINE, Z_SEC, Z_ROWS = 72, 104, 120
W_SHIFT, W_FOUR, W_FIVE, W_SEC, W_ROWS = 64, 128, 144, 152, 168


def turn(value, shift, axis):
    size = value.shape[axis]
    if isinstance(shift, int):
        shift = shift % size
        if shift == 0:
            return value
    return pltpu.roll(value, shift, axis)


def lanes_of(shape):
    return lax.broadcasted_iota(jnp.int32, shape, len(shape) - 1)


def square(rule):
    row = lax.broadcasted_iota(jnp.int32, (LANES, LANES), 0)
    col = lax.broadcasted_iota(jnp.int32, (LANES, LANES), 1)
    return jnp.where(rule(row, col), 1.0, 0.0).astype(BF16)


def spread(value, chosen):
    total = None
    for part in range(3):
        piece = value.astype(BF16)
        term = jnp.dot(piece, chosen, preferred_element_type=F32)
        total = term if total is None else total + term
        if part < 2:
            value = value - piece.astype(F32)
    return total


def flat(value):
    return value.reshape(-1, LANES)


def faces_kernel(kappa, initial, xp, xm, yp, ym, zs):
    xp[0] = kappa[31]
    xp[1] = kappa[30]
    xp[2] = initial[31]
    xm[0] = kappa[0]
    xm[1] = kappa[1]
    xm[2] = initial[0]
    yp[0] = kappa[:, 31, :]
    yp[1] = kappa[:, 30, :]
    yp[2] = initial[:, 31, :]
    ym[0] = kappa[:, 0, :]
    ym[1] = kappa[:, 1, :]
    ym[2] = initial[:, 0, :]
    lane = lanes_of((32, LANES))

    def body(x, carry):
        first, second = carry
        mine = lane // 4 == x
        shift = 4 * x + 2
        first = jnp.where(mine, turn(kappa[x], shift, 1), first)
        second = jnp.where(mine, turn(initial[x], shift, 1), second)
        return first, second

    zero = jnp.zeros((32, LANES), F32)
    first, second = lax.fori_loop(0, 32, body, (zero, zero), unroll=4)
    zs[0] = first
    zs[1] = second


def z_sides(value, rim, x, lane, period):
    near = turn(rim, 126 - 4 * x, 1)
    if period < LANES:
        other = turn(rim, lax.rem(190 - 4 * x, 128), 1)
        near = jnp.where((lane >= 32) & (lane < 96), other, near)
    inside = lane % period
    above = turn(jnp.where(inside == 0, near, value), LANES - 1, 1)
    below = turn(jnp.where(inside == period - 1, near, value), 1, 1)
    return above, below


def residual_kernel(
    kappa, initial, rhs, sigma, xlo, xhi, ylo, yhi, zlo, zhi,
    kp, ck, scale, first, message, sides, kp2, ck2, scale2, first2, sides2,
    vp, pair_r, pair_k, pair_s, rims, small,
):
    lane = lanes_of((32, LANES))
    inner = pl.ds(8, 32)
    kp[0, inner] = xlo[0]
    kp[33, inner] = xhi[0]
    vp[0, inner] = xlo[2]
    vp[33, inner] = xhi[2]

    def fill(x, carry):
        one = pl.ds(x, 1)
        kp[x + 1, inner] = kappa[x]
        vp[x + 1, inner] = initial[x]
        kp[x + 1, 7:8] = ylo[0, one]
        kp[x + 1, 40:41] = yhi[0, one]
        vp[x + 1, 7:8] = ylo[2, one]
        vp[x + 1, 40:41] = yhi[2, one]
        return carry

    lax.fori_loop(0, 32, fill, 0, unroll=4)
    low_half = lane % 4 < 2
    rim_k = jnp.where(low_half, zlo[0], zhi[0])
    rim_v = jnp.where(low_half, zlo[1], zhi[1])
    ck[...] = rim_k

    def slab(x, packed):
        k = kp[x + 1, inner]
        v = vp[x + 1, inner]
        around = [
            (kp[x, inner], vp[x, inner]),
            (kp[x + 2, inner], vp[x + 2, inner]),
            (kp[x + 1, pl.ds(7, 32)], vp[x + 1, pl.ds(7, 32)]),
            (kp[x + 1, pl.ds(9, 32)], vp[x + 1, pl.ds(9, 32)]),
        ]
        k_up, k_down = z_sides(k, rim_k, x, lane, LANES)
        v_up, v_down = z_sides(v, rim_v, x, lane, LANES)
        around += [(k_up, v_up), (k_down, v_down)]
        k_sum = sum(kn for kn, _ in around)
        v_sum = sum(vn for _, vn in around)
        both = sum(kn * vn for kn, vn in around)
        s = sigma[x]
        diagonal = s + 3.0 * k + 0.5 * k_sum
        r = rhs[x] - diagonal * v + 0.5 * (k * v_sum + both)
        h = WEIGHT / diagonal
        e = h * r
        scale[x] = h
        first[x] = e
        packed = jnp.where(lane // 4 == x, turn(e, 4 * x + 2, 1), packed)
        return r, k, s, packed

    def two(i, packed):
        r0, k0, s0, packed = slab(2 * i, packed)
        r1, k1, s1, packed = slab(2 * i + 1, packed)
        pair_r[i] = r0 + r1
        pair_k[i] = k0 + k1
        pair_s[i] = s0 + s1
        return packed

    packed = lax.fori_loop(0, 16, two, jnp.zeros((32, LANES), F32))
    sides[0] = first[31]
    sides[1] = first[0]
    sides[2] = first[:, 31, :]
    sides[3] = first[:, 0, :]

    even, odd = pl.ds(0, 16, stride=2), pl.ds(1, 16, stride=2)
    to_two = square(lambda row, col: row // 2 == col % 64)

    def level_two(ref, weight):
        summed = ref[:, even, :] + ref[:, odd, :]
        return (spread(flat(summed), to_two) * weight).reshape(16, 16, LANES)

    r2 = level_two(pair_r, 0.5)
    k2 = level_two(pair_k, 0.125)
    s2 = level_two(pair_s, 0.5)
    rims[0] = xlo[0] + xlo[1]
    rims[1] = xhi[0] + xhi[1]
    rims[2] = ylo[0] + ylo[1]
    rims[3] = yhi[0] + yhi[1]
    halo = rims[:, even, :] + rims[:, odd, :]
    halo = (spread(flat(halo), to_two) * 0.125).reshape(4, 16, LANES)
    inner2 = pl.ds(8, 16)
    kp2[1:17, inner2] = k2
    kp2[0, inner2] = halo[0]
    kp2[17, inner2] = halo[1]
    for x in range(16):
        kp2[x + 1, 7:8] = halo[2, x : x + 1]
        kp2[x + 1, 24:25] = halo[3, x : x + 1]
    rims[0] = rim_k
    rim_pair = rims[0, even, :] + rims[0, odd, :]

    def rim_rule(row, col):
        low = (col % 4 == 1) & (row % 4 < 2)
        high = (col % 4 == 2) & (row % 4 >= 2)
        return (row // 8 == col // 4) & (low | high)

    rim_k2 = spread(rim_pair, square(rim_rule)) * 0.125
    ck2[...] = rim_k2
    lane2 = lanes_of((16, LANES))
    packed2 = jnp.zeros((16, LANES), F32)
    for x in range(16):
        k = k2[x]
        up, down = z_sides(k, rim_k2, x, lane2, 64)
        k_sum = (
            kp2[x, inner2] + kp2[x + 2, inner2]
            + kp2[x + 1, pl.ds(7, 16)] + kp2[x + 1, pl.ds(9, 16)] + up + down
        )
        h = WEIGHT / (s2[x] + 3.0 * k + 0.5 * k_sum)
        e = h * r2[x]
        scale2[x] = h
        first2[x] = e
        packed2 = jnp.where(lane2 // 4 == x, turn(e, 4 * x + 2, 1), packed2)
    sides2[0] = first2[15]
    sides2[1] = first2[0]
    sides2[2] = first2[:, 15, :]
    sides2[3] = first2[:, 0, :]

    even8, odd8 = pl.ds(0, 8, stride=2), pl.ds(1, 8, stride=2)

    def level_three(field, part, weight):
        halves = field.reshape(8, 2, 16, LANES)
        small[...] = halves[:, 0] + halves[:, 1]
        summed = small[:, even8, :] + small[:, odd8, :]
        rule = square(lambda row, col: (row < 64) & (row // 2 == col - 32 * part))
        return spread(flat(summed), rule) * weight

    three = level_three(r2, 0, 0.5) + level_three(k2, 1, 0.125) + level_three(s2, 2, 0.5)
    cubes = three.reshape(2, 4, 8, LANES)
    summed = cubes[:, 0] + cubes[:, 1] + cubes[:, 2] + cubes[:, 3]
    small[0:2, 0:8] = summed
    quads = [small[0:2, pl.ds(j, 2, stride=4), :] for j in range(4)]
    quad = quads[0] + quads[1] + quads[2] + quads[3]
    small[2, 0:8] = jnp.zeros((8, LANES), F32)
    small[2, 0:2] = quad[0]
    small[2, 2:4] = quad[1]
    five = spread(small[2, 0:8], square(lambda row, col: (row < 96) & (row // 4 == col)))
    lane8 = lanes_of((8, LANES))
    five = five * jnp.where((lane8 >= 8) & (lane8 < 16), 1.0 / 64.0, 0.25)
    for p in range(8):
        message[p, 0:64] = three
        message[p, 64:72] = five
        message[p, Z_FINE:Z_SEC] = packed
        message[p, Z_SEC:Z_ROWS] = packed2


def window_kernel(place, lines, sides, sides2, out, cf, cf2, small):
    gx, gy, gz = place[0], place[1], place[2]
    before, after = lax.rem(gz + 7, 8), lax.rem(gz + 1, 8)
    a, b, c = lines[before, 0:64], lines[gz, 0:64], lines[after, 0:64]
    lane = lanes_of((64, LANES))

    def join(pieces):
        total = pieces[-1][1]
        for stop, piece in reversed(pieces[:-1]):
            total = jnp.where(lane < stop, piece, total)
        return total

    both = join([
        (16, turn(a, -16, 1)), (48, turn(b, 16, 1)), (64, turn(c, 48, 1)),
        (80, turn(a, 16, 1)), (112, turn(b, 48, 1)), (128, turn(c, 80, 1)),
    ])
    shift = join([
        (16, turn(a, -80, 1)), (48, turn(b, -48, 1)), (64, turn(c, -16, 1)),
        (128, jnp.zeros((64, LANES), F32)),
    ])

    even, odd = pl.ds(0, 4, stride=2), pl.ds(1, 4, stride=2)

    def shrink(field):
        halves = field.reshape(4, 2, 8, LANES)
        small[0:4] = halves[:, 0] + halves[:, 1]
        summed = small[0:4, even, :] + small[0:4, odd, :]
        for i in range(4):
            small[4 + i // 2, 4 * (i % 2) : 4 * (i % 2) + 4] = summed[i]
        return flat(small[4:6])

    lane4 = lanes_of((16, LANES))
    four = spread(shrink(both), square(lambda row, col: row // 2 == col))
    four = four * jnp.where(lane4 < 32, 0.5, 0.125)
    four = four + 0.5 * spread(
        shrink(shift), square(lambda row, col: (row < 64) & (row // 2 + 64 == col))
    )

    lane8 = lanes_of((8, LANES))
    row8 = lax.broadcasted_iota(jnp.int32, (8, LANES), 0)
    five = jnp.zeros((8, LANES), F32)
    five_shift = jnp.zeros((8, LANES), F32)
    for p in range(8):
        piece = lines[p, 64:72]
        five = jnp.where(lane8 // 8 == p, turn(piece, 8 * p, 1), five)
        five = jnp.where(lane8 // 8 == p + 8, turn(piece, 56 + 8 * p, 1), five)
        five_shift = jnp.where(lane8 // 8 == p, turn(piece, 8 * p - 16, 1), five_shift)
    five = jnp.where(row8 < 4, five, turn(five_shift, 4, 0))

    for q in range(16):
        out[q, 0:64] = both
        out[q, W_SHIFT:W_FOUR] = shift
        out[q, W_FOUR:W_FIVE] = four
        out[q, W_FIVE:W_SEC] = five
        out[q, W_SEC:W_ROWS] = jnp.zeros((16, LANES), F32)
    lane32 = lanes_of((32, LANES))
    for side, (dx, dy) in enumerate(((1, 0), (3, 0), (0, 1), (0, 3))):
        q = 4 * lax.rem(gx + dx, 4) + lax.rem(gy + dy, 4)
        face = sides[side]
        low = lane32 < 64
        out[q, W_SHIFT : W_SHIFT + 32] = jnp.where(low, shift[0:32], turn(face, 64, 1))
        out[q, W_SHIFT + 32 : W_FOUR] = jnp.where(low, shift[32:64], face)
        out[q, W_SEC:W_ROWS] = sides2[side]
    cf[...] = jnp.where(
        lane32 % 4 < 2, lines[before, Z_FINE:Z_SEC], lines[after, Z_FINE:Z_SEC]
    )
    cf2[...] = jnp.where(lane4 % 4 < 2, lines[before, Z_SEC:Z_ROWS], lines[after, Z_SEC:Z_ROWS])


def wrapped(value):
    last = value.shape[0] - 1
    return [
        jnp.concatenate([value[1:], value[:1]], 0),
        jnp.concatenate([value[last:], value[:last]], 0),
        turn(value, -1, 1),
        turn(value, 1, 1),
        turn(value, -1, 2),
        turn(value, 1, 2),
    ]


def periodic_setup(r, k, s, coefs):
    near = wrapped(k)
    diagonal = s + 3.0 * k + 0.5 * sum(near)
    h = WEIGHT / diagonal
    half = 0.5 * h
    for n in range(6):
        coefs[n] = half * (k + near[n])
    start = h * r
    coefs[6] = start
    return start


def periodic_sweep(e, coefs):
    total = 0.2 * e + coefs[6]
    for n, other in enumerate(wrapped(e)):
        total = total + coefs[n] * other
    return total


def cycle_kernel(
    place, columns, initial, kp, ck, scale, first, cf, kp2, ck2, scale2, first2, cf2,
    out,
    fp, fp2, rk3, s3, k3, c3, ea, eb, l4, l5, s5, l6, c4, c5, c6, c7, w4, w3, w2, up,
):
    gx, gy, gz = place[0], place[1], place[2]

    def slot(dx, dy):
        return 4 * lax.rem(gx + dx, 4) + lax.rem(gy + dy, 4)

    for ix, dx in enumerate((3, 0, 1)):
        for iy, dy in enumerate((3, 0, 1)):
            q = slot(dx, dy)
            for i in range(8):
                piece = columns[q, 8 * i : 8 * i + 8]
                rk3[8 * ix + i, 8 * iy : 8 * iy + 8] = piece
                s3[8 * ix + i, 8 * iy : 8 * iy + 8] = columns[
                    q, W_SHIFT + 8 * i : W_SHIFT + 8 * i + 8
                ]
                k3[8 * ix + i, 8 + 8 * iy : 16 + 8 * iy] = turn(piece, 64, 1)
    rim = jnp.zeros((24, 8, LANES), F32)
    for ref in (k3, ea, eb):
        ref[:, 0:8] = rim
        ref[:, 32:40] = rim
    mid = pl.ds(8, 24)

    def setup3(x, carry):
        k = k3[x, mid]
        near = [
            k3[x + 1, mid], k3[x - 1, mid], k3[x, pl.ds(9, 24)], k3[x, pl.ds(7, 24)],
            turn(k, -1, 1), turn(k, 1, 1),
        ]
        h = WEIGHT / (s3[x] + 3.0 * k + 0.5 * sum(near))
        half = 0.5 * h
        for n in range(6):
            c3[n, x] = half * (k + near[n])
        g = h * rk3[x]
        c3[6, x] = g
        ea[x, mid] = g
        return carry

    lax.fori_loop(1, 23, setup3, 0)

    for qx in range(4):
        for qy in range(4):
            q = 4 * qx + qy
            for i in range(4):
                l4[4 * qx + i, 4 * qy : 4 * qy + 4] = columns[
                    q, W_FOUR + 4 * i : W_FOUR + 4 * i + 4
                ]
            for i in range(2):
                base = W_FIVE + 2 * i
                l5[2 * qx + i, 2 * qy : 2 * qy + 2] = columns[q, base : base + 2]
                s5[2 * qx + i, 2 * qy : 2 * qy + 2] = columns[q, base + 4 : base + 6]
    r4 = l4[...]
    e4 = periodic_setup(r4, turn(r4, 96, 2), turn(r4, 64, 2), c4)
    lane5 = lanes_of((8, 8, LANES))
    both5 = l5[...]
    swapped = turn(both5, 64, 2)
    shift5 = s5[...]
    r5 = jnp.where(lane5 < 64, both5, swapped)
    k5 = jnp.where(lane5 < 64, swapped, both5)
    sh5 = jnp.where(lane5 < 64, shift5, turn(shift5, 64, 2))
    e5 = periodic_setup(r5, k5, sh5, c5)
    to_six = square(lambda row, col: (row < 64) & (row // 2 == col % 32))

    def level_six(field, weight):
        halves = field.reshape(4, 2, 8, LANES)
        l6[...] = halves[:, 0] + halves[:, 1]
        summed = l6[:, pl.ds(0, 4, stride=2), :] + l6[:, pl.ds(1, 4, stride=2), :]
        l6[:, 0:4] = summed
        l6[:, 4:8] = summed
        return spread(flat(l6[...]), to_six) * weight

    r6, k6, sh6 = level_six(r5, 0.5), level_six(k5, 0.125), level_six(sh5, 0.5)
    mean = square(lambda row, col: row < 32)

    def cube(value):
        return value.reshape(4, 8, LANES)

    r7, k7, sh7 = [cube(spread(f, mean) * (1.0 / 32.0)) for f in (r6, k6, sh6)]
    e6 = periodic_setup(cube(r6), cube(k6), cube(sh6), c6)
    e7 = periodic_setup(r7, k7, sh7, c7)

    def sweep(_, carry):
        a, b, c, d = carry
        return (
            periodic_sweep(a, c4), periodic_sweep(b, c5), periodic_sweep(c, c6),
            periodic_sweep(d, c7),
        )

    e4, e5, e6, e7 = lax.fori_loop(0, COARSE_SWEEPS - 1, sweep, (e4, e5, e6, e7))

    source, target = ea, eb
    for step in range(2, COARSE_SWEEPS + 1):

        def sweep3(x, carry, source=source, target=target):
            e = source[x, mid]
            near = [
                source[x + 1, mid], source[x - 1, mid],
                source[x, pl.ds(9, 24)], source[x, pl.ds(7, 24)],
                turn(e, -1, 1), turn(e, 1, 1),
            ]
            total = 0.2 * e + c3[6, x]
            for n in range(6):
                total = total + c3[n, x] * near[n]
            target[x, mid] = total
            return carry

        lax.fori_loop(step, 24 - step, sweep3, 0)
        source, target = target, source

    lane16 = lanes_of((16, LANES))
    lane8 = lanes_of((8, LANES))
    l6[...] = e6 + e7
    six = turn(l6[gx, pl.ds(gy, 1)] + jnp.zeros((8, LANES), F32), 128 - 4 * gz, 1)
    six = spread(six, square(lambda row, col: row == col // 32))
    l5[...] = e5
    w4[...] = jnp.zeros((16, LANES), F32)
    w4[0:2] = l5[2 * gx, pl.ds(2 * gy, 2)]
    w4[2:4] = l5[2 * gx + 1, pl.ds(2 * gy, 2)]
    five = spread(turn(w4[0:8], 128 - 8 * gz, 1), square(lambda row, col: row == col // 16))
    five = five + six
    l4[...] = e4
    for i in range(4):
        w4[4 * i : 4 * i + 4] = l4[4 * gx + i, pl.ds(4 * gy, 4)]
    four = jnp.where((lane16 >= 8) & (lane16 < 24), w4[...], 0.0)
    four = spread(four, square(lambda row, col: row == 8 + col // 8))
    for i in range(4):
        for j in range(2):
            row = 2 * (i // 2) + j
            w4[4 * i + 2 * j : 4 * i + 2 * j + 2] = jnp.broadcast_to(
                five[row : row + 1], (2, LANES)
            )
    four = four + w4[...]
    own = source[8:16, 16:24]
    lane3 = lanes_of((8, 8, LANES))
    three = flat(jnp.where((lane3 >= 16) & (lane3 < 48), own, 0.0))
    three = spread(three, square(lambda row, col: row == 16 + col // 4))
    for i in range(8):
        block = four[4 * (i // 2) : 4 * (i // 2) + 4]
        w3[i, pl.ds(0, 4, stride=2), :] = block
        w3[i, pl.ds(1, 4, stride=2), :] = block
    three = three + flat(w3[...])

    inner2 = pl.ds(8, 16)
    lane2 = lanes_of((16, LANES))
    lane32 = lanes_of((32, LANES))
    sides = [slot(3, 0), slot(1, 0), slot(0, 3), slot(0, 1)]
    fp2[1:17, inner2] = first2[...]
    fp2[0, inner2] = columns[sides[0], W_SEC:W_ROWS]
    fp2[17, inner2] = columns[sides[1], W_SEC:W_ROWS]
    for x in range(16):
        fp2[x + 1, 7:8] = columns[sides[2], W_SEC + x : W_SEC + x + 1]
        fp2[x + 1, 24:25] = columns[sides[3], W_SEC + x : W_SEC + x + 1]
    rim_k2 = ck2[...]
    rim_f2 = cf2[...]
    for x in range(16):
        k = kp2[x + 1, inner2]
        e = fp2[x + 1, inner2]
        k_up, k_down = z_sides(k, rim_k2, x, lane2, 64)
        e_up, e_down = z_sides(e, rim_f2, x, lane2, 64)
        around = [
            (kp2[x, inner2], fp2[x, inner2]),
            (kp2[x + 2, inner2], fp2[x + 2, inner2]),
            (kp2[x + 1, pl.ds(7, 16)], fp2[x + 1, pl.ds(7, 16)]),
            (kp2[x + 1, pl.ds(9, 16)], fp2[x + 1, pl.ds(9, 16)]),
            (k_up, e_up),
            (k_down, e_down),
        ]
        total = k * sum(en for _, en in around) + sum(kn * en for kn, en in around)
        w2[x] = 1.2 * e + 0.5 * scale2[x] * total
    two = spread(flat(w2[...]), square(lambda row, col: row == col // 2))
    even8, odd8 = pl.ds(0, 8, stride=2), pl.ds(1, 8, stride=2)
    for i in range(16):
        block = three[8 * (i // 2) : 8 * (i // 2) + 8]
        w2[i, even8, :] = block
        w2[i, odd8, :] = block
    two = two.reshape(16, 16, LANES) + w2[...]
    up[:, pl.ds(0, 16, stride=2), :] = two
    up[:, pl.ds(1, 16, stride=2), :] = two

    inner = pl.ds(8, 32)

    def face_of(q):
        low = columns[q, W_SHIFT : W_SHIFT + 32]
        return jnp.where(lane32 < 64, turn(low, 64, 1), columns[q, W_SHIFT + 32 : W_FOUR])

    fp[0, inner] = face_of(sides[0])
    fp[33, inner] = face_of(sides[1])
    w2[0:2] = face_of(sides[2]).reshape(2, 16, LANES)
    w2[2:4] = face_of(sides[3]).reshape(2, 16, LANES)

    def fill(x, carry):
        fp[x + 1, inner] = first[x]
        row = pl.ds(lax.rem(x, 16), 1)
        fp[x + 1, 7:8] = w2[x // 16, row]
        fp[x + 1, 40:41] = w2[2 + x // 16, row]
        return carry

    lax.fori_loop(0, 32, fill, 0, unroll=4)
    rim_k = ck[...]
    rim_f = cf[...]

    def slab(x, carry):
        k = kp[x + 1, inner]
        e = fp[x + 1, inner]
        k_up, k_down = z_sides(k, rim_k, x, lane32, LANES)
        e_up, e_down = z_sides(e, rim_f, x, lane32, LANES)
        around = [
            (kp[x, inner], fp[x, inner]),
            (kp[x + 2, inner], fp[x + 2, inner]),
            (kp[x + 1, pl.ds(7, 32)], fp[x + 1, pl.ds(7, 32)]),
            (kp[x + 1, pl.ds(9, 32)], fp[x + 1, pl.ds(9, 32)]),
            (k_up, e_up),
            (k_down, e_down),
        ]
        total = k * sum(en for _, en in around) + sum(kn * en for kn, en in around)
        out[x] = initial[x] + (1.2 * e + 0.5 * scale[x] * total + up[x // 2])
        return carry

    lax.fori_loop(0, 32, slab, 0)


VM = pl.BlockSpec(memory_space=pltpu.VMEM)
SM = pl.BlockSpec(memory_space=pltpu.SMEM)


def shape(*dims):
    return jax.ShapeDtypeStruct(dims, F32)


def local(kernel, outs, ins, scratch, name):
    return pl.pallas_call(
        kernel,
        out_shape=outs,
        in_specs=ins,
        out_specs=[VM] * len(outs),
        scratch_shapes=[pltpu.VMEM(dims, F32) for dims in scratch],
        compiler_params=pltpu.CompilerParams(vmem_limit_bytes=40 * 1024 * 1024),
        name=name,
    )


def on_device(initial, rhs, kappa, sigma):
    place = jnp.stack([lax.axis_index(axis) for axis in ("gx", "gy", "gz")]).astype(jnp.int32)

    def passed(value, axis, step):
        count = lax.axis_size(axis)
        return lax.ppermute(value, axis, [(i, (i + step) % count) for i in range(count)])

    edge = shape(3, 32, LANES)
    xp, xm, yp, ym, zs = local(
        faces_kernel, [edge, edge, edge, edge, shape(2, 32, LANES)], [VM] * 2, [], "faces"
    )(kappa, initial)
    xlo, xhi = passed(xp, "gx", 1), passed(xm, "gx", -1)
    ylo, yhi = passed(yp, "gy", 1), passed(ym, "gy", -1)
    zlo, zhi = passed(zs, "gz", 1), passed(zs, "gz", -1)
    block = (32, 32, LANES)
    block2 = (16, 16, LANES)
    kp, ck, scale, first, message, sides, kp2, ck2, scale2, first2, sides2 = local(
        residual_kernel,
        [
            shape(34, 48, LANES), shape(32, LANES), shape(*block), shape(*block),
            shape(8, Z_ROWS, LANES), shape(4, 32, LANES), shape(18, 32, LANES),
            shape(16, LANES), shape(*block2), shape(*block2), shape(4, 16, LANES),
        ],
        [VM] * 10,
        [
            (34, 48, LANES), (16, 32, LANES), (16, 32, LANES), (16, 32, LANES),
            (4, 32, LANES), (8, 16, LANES),
        ],
        "residual",
    )(kappa, initial, rhs, sigma, xlo, xhi, ylo, yhi, zlo, zhi)
    lines = lax.all_to_all(message, "gz", 0, 0)
    windows, cf, cf2 = local(
        window_kernel,
        [shape(16, W_ROWS, LANES), shape(32, LANES), shape(16, LANES)],
        [SM] + [VM] * 3,
        [(8, 8, LANES)],
        "window",
    )(place, lines, sides, sides2)
    columns = lax.all_to_all(windows, ("gx", "gy"), 0, 0)
    padded3 = (24, 40, LANES)
    block3 = (24, 24, LANES)
    return local(
        cycle_kernel,
        [shape(*block)],
        [SM] + [VM] * 12,
        [
            (34, 48, LANES), (18, 32, LANES), block3, block3, padded3, (7,) + block3,
            padded3, padded3, block2, (8, 8, LANES), (8, 8, LANES), (4, 8, LANES),
            (7,) + block2, (7, 8, 8, LANES), (7, 4, 8, LANES), (7, 4, 8, LANES),
            (16, LANES), (8, 8, LANES), block2, (16, 32, LANES),
        ],
        "cycle",
    )(
        place, columns, initial, kp, ck, scale, first, cf, kp2, ck2, scale2, first2, cf2
    )[0]


def solution(mesh):
    spec = P("gx", "gy", "gz")
    return jax.shard_map(
        on_device, mesh=mesh, in_specs=(spec,) * 4, out_specs=spec, check_vma=False
    )
```

```python
import jax
import jax.numpy as jnp
from jax import lax
from jax.experimental import pallas as pl
from jax.experimental.pallas import tpu as pltpu
from jax.sharding import PartitionSpec as P

COARSE_SWEEPS = 8
WEIGHT = 0.8
LANES = 128
F32 = jnp.float32
BF16 = jnp.bfloat16

Z_FINE, Z_SEC, Z_ROWS = 72, 104, 120
W_SHIFT, W_FOUR, W_FIVE, W_SEC, W_ROWS = 64, 128, 144, 152, 168


def turn(value, shift, axis):
    size = value.shape[axis]
    if isinstance(shift, int):
        shift = shift % size
        if shift == 0:
            return value
    return pltpu.roll(value, shift, axis)


def lanes_of(shape):
    return lax.broadcasted_iota(jnp.int32, shape, len(shape) - 1)


def square(rule):
    row = lax.broadcasted_iota(jnp.int32, (LANES, LANES), 0)
    col = lax.broadcasted_iota(jnp.int32, (LANES, LANES), 1)
    return jnp.where(rule(row, col), 1.0, 0.0).astype(BF16)


def spread(value, chosen):
    total = None
    for part in range(3):
        piece = value.astype(BF16)
        term = jnp.dot(piece, chosen, preferred_element_type=F32)
        total = term if total is None else total + term
        if part < 2:
            value = value - piece.astype(F32)
    return total


def flat(value):
    return value.reshape(-1, LANES)


def faces_kernel(kappa, initial, xp, xm, yp, ym, zs):
    xp[0] = kappa[31]
    xp[1] = kappa[30]
    xp[2] = initial[31]
    xm[0] = kappa[0]
    xm[1] = kappa[1]
    xm[2] = initial[0]
    yp[0] = kappa[:, 31, :]
    yp[1] = kappa[:, 30, :]
    yp[2] = initial[:, 31, :]
    ym[0] = kappa[:, 0, :]
    ym[1] = kappa[:, 1, :]
    ym[2] = initial[:, 0, :]
    lane = lanes_of((32, LANES))

    def body(x, carry):
        first, second = carry
        mine = lane // 4 == x
        shift = 4 * x + 2
        first = jnp.where(mine, turn(kappa[x], shift, 1), first)
        second = jnp.where(mine, turn(initial[x], shift, 1), second)
        return first, second

    zero = jnp.zeros((32, LANES), F32)
    first, second = lax.fori_loop(0, 32, body, (zero, zero), unroll=4)
    zs[0] = first
    zs[1] = second


def z_sides(value, rim, x, lane, period):
    near = turn(rim, 126 - 4 * x, 1)
    if period < LANES:
        other = turn(rim, lax.rem(190 - 4 * x, 128), 1)
        near = jnp.where((lane >= 32) & (lane < 96), other, near)
    inside = lane % period
    above = turn(jnp.where(inside == 0, near, value), LANES - 1, 1)
    below = turn(jnp.where(inside == period - 1, near, value), 1, 1)
    return above, below


def residual_kernel(
    kappa, initial, rhs, sigma, xlo, xhi, ylo, yhi, zlo, zhi,
    kp, ck, scale, first, message, sides, kp2, ck2, scale2, first2, sides2,
    vp, pair_r, pair_k, pair_s, rims, small,
):
    lane = lanes_of((32, LANES))
    inner = pl.ds(8, 32)
    kp[0, inner] = xlo[0]
    kp[33, inner] = xhi[0]
    vp[0, inner] = xlo[2]
    vp[33, inner] = xhi[2]

    def fill(x, carry):
        one = pl.ds(x, 1)
        kp[x + 1, inner] = kappa[x]
        vp[x + 1, inner] = initial[x]
        kp[x + 1, 7:8] = ylo[0, one]
        kp[x + 1, 40:41] = yhi[0, one]
        vp[x + 1, 7:8] = ylo[2, one]
        vp[x + 1, 40:41] = yhi[2, one]
        return carry

    lax.fori_loop(0, 32, fill, 0, unroll=4)
    low_half = lane % 4 < 2
    rim_k = jnp.where(low_half, zlo[0], zhi[0])
    rim_v = jnp.where(low_half, zlo[1], zhi[1])
    ck[...] = rim_k

    def slab(x, packed):
        k = kp[x + 1, inner]
        v = vp[x + 1, inner]
        around = [
            (kp[x, inner], vp[x, inner]),
            (kp[x + 2, inner], vp[x + 2, inner]),
            (kp[x + 1, pl.ds(7, 32)], vp[x + 1, pl.ds(7, 32)]),
            (kp[x + 1, pl.ds(9, 32)], vp[x + 1, pl.ds(9, 32)]),
        ]
        k_up, k_down = z_sides(k, rim_k, x, lane, LANES)
        v_up, v_down = z_sides(v, rim_v, x, lane, LANES)
        around += [(k_up, v_up), (k_down, v_down)]
        k_sum = sum(kn for kn, _ in around)
        v_sum = sum(vn for _, vn in around)
        both = sum(kn * vn for kn, vn in around)
        s = sigma[x]
        diagonal = s + 3.0 * k + 0.5 * k_sum
        r = rhs[x] - diagonal * v + 0.5 * (k * v_sum + both)
        h = WEIGHT / diagonal
        e = h * r
        scale[x] = h
        first[x] = e
        packed = jnp.where(lane // 4 == x, turn(e, 4 * x + 2, 1), packed)
        return r, k, s, packed

    def two(i, packed):
        r0, k0, s0, packed = slab(2 * i, packed)
        r1, k1, s1, packed = slab(2 * i + 1, packed)
        pair_r[i] = r0 + r1
        pair_k[i] = k0 + k1
        pair_s[i] = s0 + s1
        return packed

    packed = lax.fori_loop(0, 16, two, jnp.zeros((32, LANES), F32), unroll=2)
    sides[0] = first[31]
    sides[1] = first[0]
    sides[2] = first[:, 31, :]
    sides[3] = first[:, 0, :]

    even, odd = pl.ds(0, 16, stride=2), pl.ds(1, 16, stride=2)
    to_two = square(lambda row, col: row // 2 == col % 64)

    def level_two(ref, weight):
        summed = ref[:, even, :] + ref[:, odd, :]
        return (spread(flat(summed), to_two) * weight).reshape(16, 16, LANES)

    r2 = level_two(pair_r, 0.5)
    k2 = level_two(pair_k, 0.125)
    s2 = level_two(pair_s, 0.5)
    rims[0] = xlo[0] + xlo[1]
    rims[1] = xhi[0] + xhi[1]
    rims[2] = ylo[0] + ylo[1]
    rims[3] = yhi[0] + yhi[1]
    halo = rims[:, even, :] + rims[:, odd, :]
    halo = (spread(flat(halo), to_two) * 0.125).reshape(4, 16, LANES)
    inner2 = pl.ds(8, 16)
    kp2[1:17, inner2] = k2
    kp2[0, inner2] = halo[0]
    kp2[17, inner2] = halo[1]
    for x in range(16):
        kp2[x + 1, 7:8] = halo[2, x : x + 1]
        kp2[x + 1, 24:25] = halo[3, x : x + 1]
    rims[0] = rim_k
    rim_pair = rims[0, even, :] + rims[0, odd, :]

    def rim_rule(row, col):
        low = (col % 4 == 1) & (row % 4 < 2)
        high = (col % 4 == 2) & (row % 4 >= 2)
        return (row // 8 == col // 4) & (low | high)

    rim_k2 = spread(rim_pair, square(rim_rule)) * 0.125
    ck2[...] = rim_k2
    lane2 = lanes_of((16, LANES))
    packed2 = jnp.zeros((16, LANES), F32)
    for x in range(16):
        k = k2[x]
        up, down = z_sides(k, rim_k2, x, lane2, 64)
        k_sum = (
            kp2[x, inner2] + kp2[x + 2, inner2]
            + kp2[x + 1, pl.ds(7, 16)] + kp2[x + 1, pl.ds(9, 16)] + up + down
        )
        h = WEIGHT / (s2[x] + 3.0 * k + 0.5 * k_sum)
        e = h * r2[x]
        scale2[x] = h
        first2[x] = e
        packed2 = jnp.where(lane2 // 4 == x, turn(e, 4 * x + 2, 1), packed2)
    sides2[0] = first2[15]
    sides2[1] = first2[0]
    sides2[2] = first2[:, 15, :]
    sides2[3] = first2[:, 0, :]

    even8, odd8 = pl.ds(0, 8, stride=2), pl.ds(1, 8, stride=2)

    def level_three(field, part, weight):
        halves = field.reshape(8, 2, 16, LANES)
        small[...] = halves[:, 0] + halves[:, 1]
        summed = small[:, even8, :] + small[:, odd8, :]
        rule = square(lambda row, col: (row < 64) & (row // 2 == col - 32 * part))
        return spread(flat(summed), rule) * weight

    three = level_three(r2, 0, 0.5) + level_three(k2, 1, 0.125) + level_three(s2, 2, 0.5)
    cubes = three.reshape(2, 4, 8, LANES)
    summed = cubes[:, 0] + cubes[:, 1] + cubes[:, 2] + cubes[:, 3]
    small[0:2, 0:8] = summed
    quads = [small[0:2, pl.ds(j, 2, stride=4), :] for j in range(4)]
    quad = quads[0] + quads[1] + quads[2] + quads[3]
    small[2, 0:8] = jnp.zeros((8, LANES), F32)
    small[2, 0:2] = quad[0]
    small[2, 2:4] = quad[1]
    five = spread(small[2, 0:8], square(lambda row, col: (row < 96) & (row // 4 == col)))
    lane8 = lanes_of((8, LANES))
    five = five * jnp.where((lane8 >= 8) & (lane8 < 16), 1.0 / 64.0, 0.25)
    for p in range(8):
        message[p, 0:64] = three
        message[p, 64:72] = five
        message[p, Z_FINE:Z_SEC] = packed
        message[p, Z_SEC:Z_ROWS] = packed2


def window_kernel(place, lines, sides, sides2, out, cf, cf2, small):
    gx, gy, gz = place[0], place[1], place[2]
    before, after = lax.rem(gz + 7, 8), lax.rem(gz + 1, 8)
    a, b, c = lines[before, 0:64], lines[gz, 0:64], lines[after, 0:64]
    lane = lanes_of((64, LANES))

    def join(pieces):
        total = pieces[-1][1]
        for stop, piece in reversed(pieces[:-1]):
            total = jnp.where(lane < stop, piece, total)
        return total

    both = join([
        (16, turn(a, -16, 1)), (48, turn(b, 16, 1)), (64, turn(c, 48, 1)),
        (80, turn(a, 16, 1)), (112, turn(b, 48, 1)), (128, turn(c, 80, 1)),
    ])
    shift = join([
        (16, turn(a, -80, 1)), (48, turn(b, -48, 1)), (64, turn(c, -16, 1)),
        (128, jnp.zeros((64, LANES), F32)),
    ])

    even, odd = pl.ds(0, 4, stride=2), pl.ds(1, 4, stride=2)

    def shrink(field):
        halves = field.reshape(4, 2, 8, LANES)
        small[0:4] = halves[:, 0] + halves[:, 1]
        summed = small[0:4, even, :] + small[0:4, odd, :]
        for i in range(4):
            small[4 + i // 2, 4 * (i % 2) : 4 * (i % 2) + 4] = summed[i]
        return flat(small[4:6])

    lane4 = lanes_of((16, LANES))
    four = spread(shrink(both), square(lambda row, col: row // 2 == col))
    four = four * jnp.where(lane4 < 32, 0.5, 0.125)
    four = four + 0.5 * spread(
        shrink(shift), square(lambda row, col: (row < 64) & (row // 2 + 64 == col))
    )

    lane8 = lanes_of((8, LANES))
    row8 = lax.broadcasted_iota(jnp.int32, (8, LANES), 0)
    five = jnp.zeros((8, LANES), F32)
    five_shift = jnp.zeros((8, LANES), F32)
    for p in range(8):
        piece = lines[p, 64:72]
        five = jnp.where(lane8 // 8 == p, turn(piece, 8 * p, 1), five)
        five = jnp.where(lane8 // 8 == p + 8, turn(piece, 56 + 8 * p, 1), five)
        five_shift = jnp.where(lane8 // 8 == p, turn(piece, 8 * p - 16, 1), five_shift)
    five = jnp.where(row8 < 4, five, turn(five_shift, 4, 0))

    for q in range(16):
        out[q, 0:64] = both
        out[q, W_SHIFT:W_FOUR] = shift
        out[q, W_FOUR:W_FIVE] = four
        out[q, W_FIVE:W_SEC] = five
        out[q, W_SEC:W_ROWS] = jnp.zeros((16, LANES), F32)
    lane32 = lanes_of((32, LANES))
    for side, (dx, dy) in enumerate(((1, 0), (3, 0), (0, 1), (0, 3))):
        q = 4 * lax.rem(gx + dx, 4) + lax.rem(gy + dy, 4)
        face = sides[side]
        low = lane32 < 64
        out[q, W_SHIFT : W_SHIFT + 32] = jnp.where(low, shift[0:32], turn(face, 64, 1))
        out[q, W_SHIFT + 32 : W_FOUR] = jnp.where(low, shift[32:64], face)
        out[q, W_SEC:W_ROWS] = sides2[side]
    cf[...] = jnp.where(
        lane32 % 4 < 2, lines[before, Z_FINE:Z_SEC], lines[after, Z_FINE:Z_SEC]
    )
    cf2[...] = jnp.where(lane4 % 4 < 2, lines[before, Z_SEC:Z_ROWS], lines[after, Z_SEC:Z_ROWS])


def wrapped(value):
    last = value.shape[0] - 1
    return [
        jnp.concatenate([value[1:], value[:1]], 0),
        jnp.concatenate([value[last:], value[:last]], 0),
        turn(value, -1, 1),
        turn(value, 1, 1),
        turn(value, -1, 2),
        turn(value, 1, 2),
    ]


def periodic_setup(r, k, s, coefs):
    near = wrapped(k)
    diagonal = s + 3.0 * k + 0.5 * sum(near)
    h = WEIGHT / diagonal
    half = 0.5 * h
    for n in range(6):
        coefs[n] = half * (k + near[n])
    start = h * r
    coefs[6] = start
    return start


def periodic_sweep(e, coefs):
    total = 0.2 * e + coefs[6]
    for n, other in enumerate(wrapped(e)):
        total = total + coefs[n] * other
    return total


def cycle_kernel(
    place, columns, initial, kp, ck, scale, first, cf, kp2, ck2, scale2, first2, cf2,
    out,
    fp, fp2, rk3, s3, k3, c3, ea, eb, l4, l5, s5, l6, c4, c5, c6, c7, w4, w3, w2, up,
):
    gx, gy, gz = place[0], place[1], place[2]

    def slot(dx, dy):
        return 4 * lax.rem(gx + dx, 4) + lax.rem(gy + dy, 4)

    for ix, dx in enumerate((3, 0, 1)):
        for iy, dy in enumerate((3, 0, 1)):
            q = slot(dx, dy)
            for i in range(8):
                piece = columns[q, 8 * i : 8 * i + 8]
                rk3[8 * ix + i, 8 * iy : 8 * iy + 8] = piece
                s3[8 * ix + i, 8 * iy : 8 * iy + 8] = columns[
                    q, W_SHIFT + 8 * i : W_SHIFT + 8 * i + 8
                ]
                k3[8 * ix + i, 8 + 8 * iy : 16 + 8 * iy] = turn(piece, 64, 1)
    rim = jnp.zeros((24, 8, LANES), F32)
    for ref in (k3, ea, eb):
        ref[:, 0:8] = rim
        ref[:, 32:40] = rim
    mid = pl.ds(8, 24)

    def setup3(x, carry):
        k = k3[x, mid]
        near = [
            k3[x + 1, mid], k3[x - 1, mid], k3[x, pl.ds(9, 24)], k3[x, pl.ds(7, 24)],
            turn(k, -1, 1), turn(k, 1, 1),
        ]
        h = WEIGHT / (s3[x] + 3.0 * k + 0.5 * sum(near))
        half = 0.5 * h
        for n in range(6):
            c3[n, x] = half * (k + near[n])
        g = h * rk3[x]
        c3[6, x] = g
        ea[x, mid] = g
        return carry

    lax.fori_loop(1, 23, setup3, 0, unroll=True)

    for qx in range(4):
        for qy in range(4):
            q = 4 * qx + qy
            for i in range(4):
                l4[4 * qx + i, 4 * qy : 4 * qy + 4] = columns[
                    q, W_FOUR + 4 * i : W_FOUR + 4 * i + 4
                ]
            for i in range(2):
                base = W_FIVE + 2 * i
                l5[2 * qx + i, 2 * qy : 2 * qy + 2] = columns[q, base : base + 2]
                s5[2 * qx + i, 2 * qy : 2 * qy + 2] = columns[q, base + 4 : base + 6]
    r4 = l4[...]
    e4 = periodic_setup(r4, turn(r4, 96, 2), turn(r4, 64, 2), c4)
    lane5 = lanes_of((8, 8, LANES))
    both5 = l5[...]
    swapped = turn(both5, 64, 2)
    shift5 = s5[...]
    r5 = jnp.where(lane5 < 64, both5, swapped)
    k5 = jnp.where(lane5 < 64, swapped, both5)
    sh5 = jnp.where(lane5 < 64, shift5, turn(shift5, 64, 2))
    e5 = periodic_setup(r5, k5, sh5, c5)
    to_six = square(lambda row, col: (row < 64) & (row // 2 == col % 32))

    def level_six(field, weight):
        halves = field.reshape(4, 2, 8, LANES)
        l6[...] = halves[:, 0] + halves[:, 1]
        summed = l6[:, pl.ds(0, 4, stride=2), :] + l6[:, pl.ds(1, 4, stride=2), :]
        l6[:, 0:4] = summed
        l6[:, 4:8] = summed
        return spread(flat(l6[...]), to_six) * weight

    r6, k6, sh6 = level_six(r5, 0.5), level_six(k5, 0.125), level_six(sh5, 0.5)
    mean = square(lambda row, col: row < 32)

    def cube(value):
        return value.reshape(4, 8, LANES)

    r7, k7, sh7 = [cube(spread(f, mean) * (1.0 / 32.0)) for f in (r6, k6, sh6)]
    e6 = periodic_setup(cube(r6), cube(k6), cube(sh6), c6)
    e7 = periodic_setup(r7, k7, sh7, c7)

    def sweep(_, carry):
        a, b, c, d = carry
        return (
            periodic_sweep(a, c4), periodic_sweep(b, c5), periodic_sweep(c, c6),
            periodic_sweep(d, c7),
        )

    e4, e5, e6, e7 = lax.fori_loop(0, COARSE_SWEEPS - 1, sweep, (e4, e5, e6, e7))

    source, target = ea, eb
    for step in range(2, COARSE_SWEEPS + 1):

        def sweep3(x, carry, source=source, target=target):
            e = source[x, mid]
            near = [
                source[x + 1, mid], source[x - 1, mid],
                source[x, pl.ds(9, 24)], source[x, pl.ds(7, 24)],
                turn(e, -1, 1), turn(e, 1, 1),
            ]
            total = 0.2 * e + c3[6, x]
            for n in range(6):
                total = total + c3[n, x] * near[n]
            target[x, mid] = total
            return carry

        lax.fori_loop(step, 24 - step, sweep3, 0, unroll=True)
        source, target = target, source

    lane16 = lanes_of((16, LANES))
    lane8 = lanes_of((8, LANES))
    l6[...] = e6 + e7
    six = turn(l6[gx, pl.ds(gy, 1)] + jnp.zeros((8, LANES), F32), 128 - 4 * gz, 1)
    six = spread(six, square(lambda row, col: row == col // 32))
    l5[...] = e5
    w4[...] = jnp.zeros((16, LANES), F32)
    w4[0:2] = l5[2 * gx, pl.ds(2 * gy, 2)]
    w4[2:4] = l5[2 * gx + 1, pl.ds(2 * gy, 2)]
    five = spread(turn(w4[0:8], 128 - 8 * gz, 1), square(lambda row, col: row == col // 16))
    five = five + six
    l4[...] = e4
    for i in range(4):
        w4[4 * i : 4 * i + 4] = l4[4 * gx + i, pl.ds(4 * gy, 4)]
    four = jnp.where((lane16 >= 8) & (lane16 < 24), w4[...], 0.0)
    four = spread(four, square(lambda row, col: row == 8 + col // 8))
    for i in range(4):
        for j in range(2):
            row = 2 * (i // 2) + j
            w4[4 * i + 2 * j : 4 * i + 2 * j + 2] = jnp.broadcast_to(
                five[row : row + 1], (2, LANES)
            )
    four = four + w4[...]
    own = source[8:16, 16:24]
    lane3 = lanes_of((8, 8, LANES))
    three = flat(jnp.where((lane3 >= 16) & (lane3 < 48), own, 0.0))
    three = spread(three, square(lambda row, col: row == 16 + col // 4))
    for i in range(8):
        block = four[4 * (i // 2) : 4 * (i // 2) + 4]
        w3[i, pl.ds(0, 4, stride=2), :] = block
        w3[i, pl.ds(1, 4, stride=2), :] = block
    three = three + flat(w3[...])

    inner2 = pl.ds(8, 16)
    lane2 = lanes_of((16, LANES))
    lane32 = lanes_of((32, LANES))
    sides = [slot(3, 0), slot(1, 0), slot(0, 3), slot(0, 1)]
    fp2[1:17, inner2] = first2[...]
    fp2[0, inner2] = columns[sides[0], W_SEC:W_ROWS]
    fp2[17, inner2] = columns[sides[1], W_SEC:W_ROWS]
    for x in range(16):
        fp2[x + 1, 7:8] = columns[sides[2], W_SEC + x : W_SEC + x + 1]
        fp2[x + 1, 24:25] = columns[sides[3], W_SEC + x : W_SEC + x + 1]
    rim_k2 = ck2[...]
    rim_f2 = cf2[...]
    for x in range(16):
        k = kp2[x + 1, inner2]
        e = fp2[x + 1, inner2]
        k_up, k_down = z_sides(k, rim_k2, x, lane2, 64)
        e_up, e_down = z_sides(e, rim_f2, x, lane2, 64)
        around = [
            (kp2[x, inner2], fp2[x, inner2]),
            (kp2[x + 2, inner2], fp2[x + 2, inner2]),
            (kp2[x + 1, pl.ds(7, 16)], fp2[x + 1, pl.ds(7, 16)]),
            (kp2[x + 1, pl.ds(9, 16)], fp2[x + 1, pl.ds(9, 16)]),
            (k_up, e_up),
            (k_down, e_down),
        ]
        total = k * sum(en for _, en in around) + sum(kn * en for kn, en in around)
        w2[x] = 1.2 * e + 0.5 * scale2[x] * total
    two = spread(flat(w2[...]), square(lambda row, col: row == col // 2))
    even8, odd8 = pl.ds(0, 8, stride=2), pl.ds(1, 8, stride=2)
    for i in range(16):
        block = three[8 * (i // 2) : 8 * (i // 2) + 8]
        w2[i, even8, :] = block
        w2[i, odd8, :] = block
    two = two.reshape(16, 16, LANES) + w2[...]
    up[:, pl.ds(0, 16, stride=2), :] = two
    up[:, pl.ds(1, 16, stride=2), :] = two

    inner = pl.ds(8, 32)

    def face_of(q):
        low = columns[q, W_SHIFT : W_SHIFT + 32]
        return jnp.where(lane32 < 64, turn(low, 64, 1), columns[q, W_SHIFT + 32 : W_FOUR])

    fp[0, inner] = face_of(sides[0])
    fp[33, inner] = face_of(sides[1])
    w2[0:2] = face_of(sides[2]).reshape(2, 16, LANES)
    w2[2:4] = face_of(sides[3]).reshape(2, 16, LANES)

    def fill(x, carry):
        fp[x + 1, inner] = first[x]
        row = pl.ds(lax.rem(x, 16), 1)
        fp[x + 1, 7:8] = w2[x // 16, row]
        fp[x + 1, 40:41] = w2[2 + x // 16, row]
        return carry

    lax.fori_loop(0, 32, fill, 0, unroll=4)
    rim_k = ck[...]
    rim_f = cf[...]

    def slab(x, carry):
        k = kp[x + 1, inner]
        e = fp[x + 1, inner]
        k_up, k_down = z_sides(k, rim_k, x, lane32, LANES)
        e_up, e_down = z_sides(e, rim_f, x, lane32, LANES)
        around = [
            (kp[x, inner], fp[x, inner]),
            (kp[x + 2, inner], fp[x + 2, inner]),
            (kp[x + 1, pl.ds(7, 32)], fp[x + 1, pl.ds(7, 32)]),
            (kp[x + 1, pl.ds(9, 32)], fp[x + 1, pl.ds(9, 32)]),
            (k_up, e_up),
            (k_down, e_down),
        ]
        total = k * sum(en for _, en in around) + sum(kn * en for kn, en in around)
        out[x] = initial[x] + (1.2 * e + 0.5 * scale[x] * total + up[x // 2])
        return carry

    lax.fori_loop(0, 32, slab, 0, unroll=4)


VM = pl.BlockSpec(memory_space=pltpu.VMEM)
SM = pl.BlockSpec(memory_space=pltpu.SMEM)


def shape(*dims):
    return jax.ShapeDtypeStruct(dims, F32)


def local(kernel, outs, ins, scratch, name):
    return pl.pallas_call(
        kernel,
        out_shape=outs,
        in_specs=ins,
        out_specs=[VM] * len(outs),
        scratch_shapes=[pltpu.VMEM(dims, F32) for dims in scratch],
        compiler_params=pltpu.CompilerParams(vmem_limit_bytes=40 * 1024 * 1024),
        name=name,
    )


def on_device(initial, rhs, kappa, sigma):
    place = jnp.stack([lax.axis_index(axis) for axis in ("gx", "gy", "gz")]).astype(jnp.int32)

    def passed(value, axis, step):
        count = lax.axis_size(axis)
        return lax.ppermute(value, axis, [(i, (i + step) % count) for i in range(count)])

    edge = shape(3, 32, LANES)
    xp, xm, yp, ym, zs = local(
        faces_kernel, [edge, edge, edge, edge, shape(2, 32, LANES)], [VM] * 2, [], "faces"
    )(kappa, initial)
    xlo, xhi = passed(xp, "gx", 1), passed(xm, "gx", -1)
    ylo, yhi = passed(yp, "gy", 1), passed(ym, "gy", -1)
    zlo, zhi = passed(zs, "gz", 1), passed(zs, "gz", -1)
    block = (32, 32, LANES)
    block2 = (16, 16, LANES)
    kp, ck, scale, first, message, sides, kp2, ck2, scale2, first2, sides2 = local(
        residual_kernel,
        [
            shape(34, 48, LANES), shape(32, LANES), shape(*block), shape(*block),
            shape(8, Z_ROWS, LANES), shape(4, 32, LANES), shape(18, 32, LANES),
            shape(16, LANES), shape(*block2), shape(*block2), shape(4, 16, LANES),
        ],
        [VM] * 10,
        [
            (34, 48, LANES), (16, 32, LANES), (16, 32, LANES), (16, 32, LANES),
            (4, 32, LANES), (8, 16, LANES),
        ],
        "residual",
    )(kappa, initial, rhs, sigma, xlo, xhi, ylo, yhi, zlo, zhi)
    lines = lax.all_to_all(message, "gz", 0, 0)
    windows, cf, cf2 = local(
        window_kernel,
        [shape(16, W_ROWS, LANES), shape(32, LANES), shape(16, LANES)],
        [SM] + [VM] * 3,
        [(8, 8, LANES)],
        "window",
    )(place, lines, sides, sides2)
    columns = lax.all_to_all(windows, ("gx", "gy"), 0, 0)
    padded3 = (24, 40, LANES)
    block3 = (24, 24, LANES)
    return local(
        cycle_kernel,
        [shape(*block)],
        [SM] + [VM] * 12,
        [
            (34, 48, LANES), (18, 32, LANES), block3, block3, padded3, (7,) + block3,
            padded3, padded3, block2, (8, 8, LANES), (8, 8, LANES), (4, 8, LANES),
            (7,) + block2, (7, 8, 8, LANES), (7, 4, 8, LANES), (7, 4, 8, LANES),
            (16, LANES), (8, 8, LANES), block2, (16, 32, LANES),
        ],
        "cycle",
    )(
        place, columns, initial, kp, ck, scale, first, cf, kp2, ck2, scale2, first2, cf2
    )[0]


def solution(mesh):
    spec = P("gx", "gy", "gz")
    return jax.shard_map(
        on_device, mesh=mesh, in_specs=(spec,) * 4, out_specs=spec, check_vma=False
    )
```

```python
import jax
import jax.numpy as jnp
from jax import lax
from jax.experimental import pallas as pl
from jax.experimental.pallas import tpu as pltpu
from jax.sharding import PartitionSpec as P

COARSE_SWEEPS = 8
WEIGHT = 0.8
LANES = 128
F32 = jnp.float32
BF16 = jnp.bfloat16

Z_SMALL, Z_ROWS = 32, 40
W_FACE, W_FOUR, W_SEC, W_FIVE, W_ROWS = 64, 96, 112, 120, 128
BASE = 5


def turn(value, shift, axis):
    size = value.shape[axis]
    if isinstance(shift, int):
        shift = shift % size
        if shift == 0:
            return value
    return pltpu.roll(value, shift, axis)


def lanes_of(shape):
    return lax.broadcasted_iota(jnp.int32, shape, len(shape) - 1)


def square(rule):
    row = lax.broadcasted_iota(jnp.int32, (LANES, LANES), 0)
    col = lax.broadcasted_iota(jnp.int32, (LANES, LANES), 1)
    return jnp.where(rule(row, col), 1.0, 0.0).astype(BF16)


def spread(value, chosen):
    total = None
    for part in range(3):
        piece = value.astype(BF16)
        term = jnp.dot(piece, chosen, preferred_element_type=F32)
        total = term if total is None else total + term
        if part < 2:
            value = value - piece.astype(F32)
    return total


def flat(value):
    return value.reshape(-1, LANES)


def faces_kernel(kappa, initial, xp, xm, yp, ym, zs):
    xp[0] = kappa[31]
    xp[1] = kappa[30]
    xp[2] = initial[31]
    xm[0] = kappa[0]
    xm[1] = kappa[1]
    xm[2] = initial[0]
    yp[0] = kappa[:, 31, :]
    yp[1] = kappa[:, 30, :]
    yp[2] = initial[:, 31, :]
    ym[0] = kappa[:, 0, :]
    ym[1] = kappa[:, 1, :]
    ym[2] = initial[:, 0, :]
    lane = lanes_of((32, LANES))

    def body(x, carry):
        first, second = carry
        mine = lane // 4 == x
        shift = 4 * x + 2
        first = jnp.where(mine, turn(kappa[x], shift, 1), first)
        second = jnp.where(mine, turn(initial[x], shift, 1), second)
        return first, second

    zero = jnp.zeros((32, LANES), F32)
    first, second = lax.fori_loop(0, 32, body, (zero, zero), unroll=4)
    zs[0] = first
    zs[1] = second


def z_sides(value, rim, x, lane, period):
    near = turn(rim, 126 - 4 * x, 1)
    if period < LANES:
        other = turn(rim, lax.rem(190 - 4 * x, 128), 1)
        near = jnp.where((lane >= 32) & (lane < 96), other, near)
    inside = lane % period
    above = turn(jnp.where(inside == 0, near, value), LANES - 1, 1)
    below = turn(jnp.where(inside == period - 1, near, value), 1, 1)
    return above, below


def residual_kernel(
    place, kappa, initial, rhs, sigma, xlo, xhi, ylo, yhi, zlo, zhi,
    kp, ck, scale, first, message, whole, sides, kp2, ck2, scale2, first2, sides2,
    vp, pair_r, pair_k, pair_s, rims, small,
):
    lane = lanes_of((32, LANES))
    inner = pl.ds(8, 32)
    kp[0, inner] = xlo[0]
    kp[33, inner] = xhi[0]
    vp[0, inner] = xlo[2]
    vp[33, inner] = xhi[2]

    def fill(x, carry):
        one = pl.ds(x, 1)
        kp[x + 1, inner] = kappa[x]
        vp[x + 1, inner] = initial[x]
        kp[x + 1, 7:8] = ylo[0, one]
        kp[x + 1, 40:41] = yhi[0, one]
        vp[x + 1, 7:8] = ylo[2, one]
        vp[x + 1, 40:41] = yhi[2, one]
        return carry

    lax.fori_loop(0, 32, fill, 0, unroll=4)
    low_half = lane % 4 < 2
    rim_k = jnp.where(low_half, zlo[0], zhi[0])
    rim_v = jnp.where(low_half, zlo[1], zhi[1])
    ck[...] = rim_k

    def slab(x, packed):
        k = kp[x + 1, inner]
        v = vp[x + 1, inner]
        around = [
            (kp[x, inner], vp[x, inner]),
            (kp[x + 2, inner], vp[x + 2, inner]),
            (kp[x + 1, pl.ds(7, 32)], vp[x + 1, pl.ds(7, 32)]),
            (kp[x + 1, pl.ds(9, 32)], vp[x + 1, pl.ds(9, 32)]),
        ]
        k_up, k_down = z_sides(k, rim_k, x, lane, LANES)
        v_up, v_down = z_sides(v, rim_v, x, lane, LANES)
        around += [(k_up, v_up), (k_down, v_down)]
        k_sum = sum(kn for kn, _ in around)
        v_sum = sum(vn for _, vn in around)
        both = sum(kn * vn for kn, vn in around)
        s = sigma[x]
        diagonal = s + 3.0 * k + 0.5 * k_sum
        r = rhs[x] - diagonal * v + 0.5 * (k * v_sum + both)
        h = WEIGHT / diagonal
        e = h * r
        scale[x] = h
        first[x] = e
        packed = jnp.where(lane // 4 == x, turn(e, 4 * x + 2, 1), packed)
        return r, k, s, packed

    def two(i, packed):
        r0, k0, s0, packed = slab(2 * i, packed)
        r1, k1, s1, packed = slab(2 * i + 1, packed)
        pair_r[i] = r0 + r1
        pair_k[i] = k0 + k1
        pair_s[i] = s0 + s1
        return packed

    packed = lax.fori_loop(0, 16, two, jnp.zeros((32, LANES), F32), unroll=2)
    sides[0] = first[31]
    sides[1] = first[0]
    sides[2] = first[:, 31, :]
    sides[3] = first[:, 0, :]

    even, odd = pl.ds(0, 16, stride=2), pl.ds(1, 16, stride=2)
    to_two = square(lambda row, col: row // 2 == col % 64)

    def level_two(ref, weight):
        summed = ref[:, even, :] + ref[:, odd, :]
        return (spread(flat(summed), to_two) * weight).reshape(16, 16, LANES)

    r2 = level_two(pair_r, 0.5)
    k2 = level_two(pair_k, 0.125)
    s2 = level_two(pair_s, 0.5)
    rims[0] = xlo[0] + xlo[1]
    rims[1] = xhi[0] + xhi[1]
    rims[2] = ylo[0] + ylo[1]
    rims[3] = yhi[0] + yhi[1]
    halo = rims[:, even, :] + rims[:, odd, :]
    halo = (spread(flat(halo), to_two) * 0.125).reshape(4, 16, LANES)
    inner2 = pl.ds(8, 16)
    kp2[1:17, inner2] = k2
    kp2[0, inner2] = halo[0]
    kp2[17, inner2] = halo[1]
    for x in range(16):
        kp2[x + 1, 7:8] = halo[2, x : x + 1]
        kp2[x + 1, 24:25] = halo[3, x : x + 1]
    rims[0] = rim_k
    rim_pair = rims[0, even, :] + rims[0, odd, :]

    def rim_rule(row, col):
        low = (col % 4 == 1) & (row % 4 < 2)
        high = (col % 4 == 2) & (row % 4 >= 2)
        return (row // 8 == col // 4) & (low | high)

    rim_k2 = spread(rim_pair, square(rim_rule)) * 0.125
    ck2[...] = rim_k2
    lane2 = lanes_of((16, LANES))
    packed2 = jnp.zeros((16, LANES), F32)
    for x in range(16):
        k = k2[x]
        up, down = z_sides(k, rim_k2, x, lane2, 64)
        k_sum = (
            kp2[x, inner2] + kp2[x + 2, inner2]
            + kp2[x + 1, pl.ds(7, 16)] + kp2[x + 1, pl.ds(9, 16)] + up + down
        )
        h = WEIGHT / (s2[x] + 3.0 * k + 0.5 * k_sum)
        e = h * r2[x]
        scale2[x] = h
        first2[x] = e
        packed2 = jnp.where(lane2 // 4 == x, turn(e, 4 * x + 2, 1), packed2)
    sides2[0] = first2[15]
    sides2[1] = first2[0]
    sides2[2] = first2[:, 15, :]
    sides2[3] = first2[:, 0, :]

    even8, odd8 = pl.ds(0, 8, stride=2), pl.ds(1, 8, stride=2)

    def level_three(field, part, weight):
        halves = field.reshape(8, 2, 16, LANES)
        small[...] = halves[:, 0] + halves[:, 1]
        summed = small[:, even8, :] + small[:, odd8, :]
        rule = square(lambda row, col: (row < 64) & (row // 2 == col - 32 * part))
        return spread(flat(summed), rule) * weight

    three = level_three(r2, 0, 0.5) + level_three(k2, 1, 0.125) + level_three(s2, 2, 0.5)
    cubes = three.reshape(2, 4, 8, LANES)
    summed = cubes[:, 0] + cubes[:, 1] + cubes[:, 2] + cubes[:, 3]
    small[0:2, 0:8] = summed
    quads = [small[0:2, pl.ds(j, 2, stride=4), :] for j in range(4)]
    quad = quads[0] + quads[1] + quads[2] + quads[3]
    small[2, 0:8] = jnp.zeros((8, LANES), F32)
    small[2, 0:2] = quad[0]
    small[2, 2:4] = quad[1]
    five = spread(small[2, 0:8], square(lambda row, col: (row < 96) & (row // 4 == col)))
    lane8 = lanes_of((8, LANES))
    five = five * jnp.where((lane8 >= 8) & (lane8 < 16), 1.0 / 64.0, 0.25)
    whole[...] = three
    five = turn(jnp.where(lane8 < 24, five, 0.0), 64, 1)
    blank = jnp.zeros((32, LANES), F32)
    for p in range(8):
        message[p, 0:Z_SMALL] = blank
        message[p, Z_SMALL:Z_ROWS] = five
    gz = place[2]
    for step, start, tag in ((1, 16, 1), (7, 0, 2)):
        p = lax.rem(gz + step, 8)
        half = spread(
            three,
            square(
                lambda row, col, start=start: (col < 48)
                & (row == 32 * (col // 16) + start + col % 16)
            ),
        )
        face = spread(packed, square(lambda row, col, tag=tag: row == 4 * (col - 96) + tag))
        message[p, 0:Z_SMALL] = half[0:32] + turn(half[32:64], 48, 1) + face
        face2 = spread(
            packed2, square(lambda row, col, tag=tag: (col < 16) & (row == 4 * col + tag))
        )
        message[p, Z_SMALL:Z_ROWS] = face2[0:8] + turn(face2[8:16], 16, 1) + five


def window_kernel(place, lines, whole, sides, sides2, out, own, cf, cf2, small):
    gx, gy, gz = place[0], place[1], place[2]
    before, after = lax.rem(gz + 7, 8), lax.rem(gz + 1, 8)
    lane = lanes_of((64, LANES))
    a_half, c_half = lines[before, 0:Z_SMALL], lines[after, 0:Z_SMALL]
    a = jnp.concatenate([a_half, turn(a_half, -48, 1)], 0)
    b = whole[...]
    c = jnp.concatenate([c_half, turn(c_half, -48, 1)], 0)

    def window(part):
        low = turn(a, BASE - 16 - 16 * part, 1)
        mid = turn(b, BASE - 32 * part, 1)
        high = turn(c, BASE + 32 - 16 * part, 1)
        value = jnp.where((lane < BASE) | (lane >= 112 + BASE), low, mid)
        value = jnp.where((lane >= BASE + 32) & (lane < BASE + 48), high, value)
        return jnp.where((lane >= BASE + 48) & (lane < 112 + BASE), 0.0, value)

    r, k, s = window(0), window(1), window(2)
    own[0], own[1], own[2] = r, k, s
    main = jnp.where(lane < 42, r, jnp.where(lane < 86, turn(k, 43, 1), turn(s, 86, 1)))
    low = jnp.where(lane == 127, r, jnp.where(lane == 126, k, turn(s, -2, 1)))
    high = jnp.where(lane == 42, r, jnp.where(lane == 43, k, turn(s, 2, 1)))
    ends = jnp.where(lane >= 64, low, turn(high, 86, 1))

    even, odd = pl.ds(0, 4, stride=2), pl.ds(1, 4, stride=2)

    def shrink(field, part, weight):
        halves = field.reshape(4, 2, 8, LANES)
        small[0:4] = halves[:, 0] + halves[:, 1]
        summed = small[0:4, even, :] + small[0:4, odd, :]
        for i in range(4):
            small[4 + i // 2, 4 * (i % 2) : 4 * (i % 2) + 4] = summed[i]

        def rule(row, col):
            cell = (row + 16 - BASE) % LANES
            return (cell < 64) & (cell // 2 == col - 32 * part)

        return spread(flat(small[4:6]), square(rule)) * weight

    four = shrink(r, 0, 0.5) + shrink(k, 1, 0.125) + shrink(s, 2, 0.5)
    lane8 = lanes_of((8, LANES))
    for i in range(8):
        start = 96 + 6 * (i % 4)
        moved = turn(ends[8 * i : 8 * i + 8], start - 125, 1)
        kept = jnp.where((lane8 >= start) & (lane8 < start + 6), moved, 0.0)
        extra = kept if i % 4 == 0 else extra + kept
        if i % 4 == 3:
            small[i // 4] = extra
    four = four + flat(small[0:2])

    row8 = lax.broadcasted_iota(jnp.int32, (8, LANES), 0)
    five = jnp.zeros((8, LANES), F32)
    five_shift = jnp.zeros((8, LANES), F32)
    for p in range(8):
        piece = lines[p, Z_SMALL:Z_ROWS]
        five = jnp.where(lane8 // 8 == p, turn(piece, 8 * p - 64, 1), five)
        five = jnp.where(lane8 // 8 == p + 8, turn(piece, 8 * p - 8, 1), five)
        five_shift = jnp.where(lane8 // 8 == p, turn(piece, 8 * p - 80, 1), five_shift)
    five = jnp.where(row8 < 4, five, turn(five_shift, 4, 0))

    for q in range(16):
        out[q, 0:W_FACE] = main
        out[q, W_FACE:W_FOUR] = jnp.zeros((32, LANES), F32)
        out[q, W_FOUR:W_SEC] = four
        out[q, W_SEC:W_FIVE] = jnp.zeros((8, LANES), F32)
        out[q, W_FIVE:W_ROWS] = five
    for side, (dx, dy) in enumerate(((1, 0), (3, 0), (0, 1), (0, 3))):
        q = 4 * lax.rem(gx + dx, 4) + lax.rem(gy + dy, 4)
        out[q, W_FACE:W_FOUR] = sides[side]
        face2 = sides2[side]
        out[q, W_SEC:W_FIVE] = jnp.where(lane8 < 64, face2[0:8], face2[8:16])

    def rim(low, high, ready):
        below = spread(low, square(lambda row, col: ready(row) & (col == 4 * (row % 32) + 1)))
        above = spread(high, square(lambda row, col: ready(row) & (col == 4 * (row % 32) + 2)))
        return below + above

    cf[...] = rim(a_half, c_half, lambda row: row >= 96)

    def unfold(half):
        return jnp.concatenate([half, turn(half, -16, 1)], 0)

    cf2[...] = rim(
        unfold(lines[before, Z_SMALL:Z_ROWS]),
        unfold(lines[after, Z_SMALL:Z_ROWS]),
        lambda row: row < 16,
    )


def wrapped(value):
    last = value.shape[0] - 1
    return [
        jnp.concatenate([value[1:], value[:1]], 0),
        jnp.concatenate([value[last:], value[:last]], 0),
        turn(value, -1, 1),
        turn(value, 1, 1),
        turn(value, -1, 2),
        turn(value, 1, 2),
    ]


def periodic_setup(r, k, s, coefs):
    near = wrapped(k)
    diagonal = s + 3.0 * k + 0.5 * sum(near)
    h = WEIGHT / diagonal
    half = 0.5 * h
    for n in range(6):
        coefs[n] = half * (k + near[n])
    start = h * r
    coefs[6] = start
    return start


def periodic_sweep(e, coefs):
    total = 0.2 * e + coefs[6]
    for n, other in enumerate(wrapped(e)):
        total = total + coefs[n] * other
    return total


def cycle_kernel(
    place, columns, own, initial, kp, ck, scale, first, cf, kp2, ck2, scale2, first2, cf2,
    out,
    fp, fp2, r3, s3, k3, c3, ea, eb, l4, l5, s5, l6, c4, c5, c6, c7, w4, w3, w2, up,
):
    gx, gy, gz = place[0], place[1], place[2]

    def slot(dx, dy):
        return 4 * lax.rem(gx + dx, 4) + lax.rem(gy + dy, 4)

    lane8 = lanes_of((8, LANES))
    for ix, dx in enumerate((3, 0, 1)):
        for iy, dy in enumerate((3, 0, 1)):
            q = slot(dx, dy)
            for i in range(8):
                if dx == 0 and dy == 0:
                    r, k, s = [own[f, 8 * i : 8 * i + 8] for f in range(3)]
                else:
                    r = columns[q, 8 * i : 8 * i + 8]
                    k = turn(r, -43, 1)
                    s = turn(r, -86, 1)
                    beside = (dx == 3 and i == 7) or (dx == 1 and i == 0) or dx == 0
                    if beside and (dx == 0 or dy == 0):
                        base = W_FOUR + 8 * (i // 4)
                        low = turn(columns[q, base : base + 8], 29 - 6 * (i % 4), 1)
                        high = turn(low, 42, 1)
                        r = jnp.where(lane8 == 127, low, jnp.where(lane8 == 42, high, r))
                        k = jnp.where(lane8 == 126, low, jnp.where(lane8 == 43, high, k))
                        low, high = turn(low, 2, 1), turn(high, -2, 1)
                        s = jnp.where(lane8 == 127, low, jnp.where(lane8 == 42, high, s))
                x, y = 8 * ix + i, 8 * iy
                r3[x, y : y + 8] = r
                k3[x, y + 8 : y + 16] = k
                s3[x, y : y + 8] = s
    rim = jnp.zeros((24, 8, LANES), F32)
    for ref in (k3, ea, eb):
        ref[:, 0:8] = rim
        ref[:, 32:40] = rim
    mid = pl.ds(8, 24)

    def setup3(x, carry):
        k = k3[x, mid]
        near = [
            k3[x + 1, mid], k3[x - 1, mid], k3[x, pl.ds(9, 24)], k3[x, pl.ds(7, 24)],
            turn(k, -1, 1), turn(k, 1, 1),
        ]
        h = WEIGHT / (s3[x] + 3.0 * k + 0.5 * sum(near))
        half = 0.5 * h
        for n in range(6):
            c3[n, x] = half * (k + near[n])
        g = h * r3[x]
        c3[6, x] = g
        ea[x, mid] = g
        return carry

    lax.fori_loop(1, 23, setup3, 0, unroll=True)

    for qx in range(4):
        for qy in range(4):
            q = 4 * qx + qy
            for i in range(4):
                l4[4 * qx + i, 4 * qy : 4 * qy + 4] = columns[
                    q, W_FOUR + 4 * i : W_FOUR + 4 * i + 4
                ]
            for i in range(2):
                base = W_FIVE + 2 * i
                l5[2 * qx + i, 2 * qy : 2 * qy + 2] = columns[q, base : base + 2]
                s5[2 * qx + i, 2 * qy : 2 * qy + 2] = columns[q, base + 4 : base + 6]
    r4 = l4[...]
    e4 = periodic_setup(r4, turn(r4, 96, 2), turn(r4, 64, 2), c4)
    lane5 = lanes_of((8, 8, LANES))
    both5 = l5[...]
    swapped = turn(both5, 64, 2)
    shift5 = s5[...]
    r5 = jnp.where(lane5 < 64, both5, swapped)
    k5 = jnp.where(lane5 < 64, swapped, both5)
    sh5 = jnp.where(lane5 < 64, shift5, turn(shift5, 64, 2))
    e5 = periodic_setup(r5, k5, sh5, c5)
    to_six = square(lambda row, col: (row < 64) & (row // 2 == col % 32))

    def level_six(field, weight):
        halves = field.reshape(4, 2, 8, LANES)
        l6[...] = halves[:, 0] + halves[:, 1]
        summed = l6[:, pl.ds(0, 4, stride=2), :] + l6[:, pl.ds(1, 4, stride=2), :]
        l6[:, 0:4] = summed
        l6[:, 4:8] = summed
        return spread(flat(l6[...]), to_six) * weight

    r6, k6, sh6 = level_six(r5, 0.5), level_six(k5, 0.125), level_six(sh5, 0.5)
    mean = square(lambda row, col: row < 32)

    def cube(value):
        return value.reshape(4, 8, LANES)

    r7, k7, sh7 = [cube(spread(f, mean) * (1.0 / 32.0)) for f in (r6, k6, sh6)]
    e6 = periodic_setup(cube(r6), cube(k6), cube(sh6), c6)
    e7 = periodic_setup(r7, k7, sh7, c7)

    def sweep(_, carry):
        a, b, c, d = carry
        return (
            periodic_sweep(a, c4), periodic_sweep(b, c5), periodic_sweep(c, c6),
            periodic_sweep(d, c7),
        )

    e4, e5, e6, e7 = lax.fori_loop(0, COARSE_SWEEPS - 1, sweep, (e4, e5, e6, e7))

    source, target = ea, eb
    for step in range(2, COARSE_SWEEPS + 1):

        def sweep3(x, carry, source=source, target=target):
            e = source[x, mid]
            near = [
                source[x + 1, mid], source[x - 1, mid],
                source[x, pl.ds(9, 24)], source[x, pl.ds(7, 24)],
                turn(e, -1, 1), turn(e, 1, 1),
            ]
            total = 0.2 * e + c3[6, x]
            for n in range(6):
                total = total + c3[n, x] * near[n]
            target[x, mid] = total
            return carry

        lax.fori_loop(step, 24 - step, sweep3, 0, unroll=True)
        source, target = target, source

    lane16 = lanes_of((16, LANES))
    l6[...] = e6 + e7
    six = turn(l6[gx, pl.ds(gy, 1)] + jnp.zeros((8, LANES), F32), 128 - 4 * gz, 1)
    six = spread(six, square(lambda row, col: row == col // 32))
    l5[...] = e5
    w4[...] = jnp.zeros((16, LANES), F32)
    w4[0:2] = l5[2 * gx, pl.ds(2 * gy, 2)]
    w4[2:4] = l5[2 * gx + 1, pl.ds(2 * gy, 2)]
    five = spread(turn(w4[0:8], 128 - 8 * gz, 1), square(lambda row, col: row == col // 16))
    five = five + six
    l4[...] = e4
    for i in range(4):
        w4[4 * i : 4 * i + 4] = l4[4 * gx + i, pl.ds(4 * gy, 4)]
    four = jnp.where((lane16 >= 8) & (lane16 < 24), w4[...], 0.0)
    four = spread(four, square(lambda row, col: row == 8 + col // 8))
    for i in range(4):
        for j in range(2):
            row = 2 * (i // 2) + j
            w4[4 * i + 2 * j : 4 * i + 2 * j + 2] = jnp.broadcast_to(
                five[row : row + 1], (2, LANES)
            )
    four = four + w4[...]
    mine = source[8:16, 16:24]
    lane3 = lanes_of((8, 8, LANES))
    three = flat(jnp.where((lane3 >= BASE) & (lane3 < BASE + 32), mine, 0.0))
    three = spread(three, square(lambda row, col: row == BASE + col // 4))
    for i in range(8):
        block = four[4 * (i // 2) : 4 * (i // 2) + 4]
        w3[i, pl.ds(0, 4, stride=2), :] = block
        w3[i, pl.ds(1, 4, stride=2), :] = block
    three = three + flat(w3[...])

    inner2 = pl.ds(8, 16)
    lane2 = lanes_of((16, LANES))
    lane32 = lanes_of((32, LANES))
    sides = [slot(3, 0), slot(1, 0), slot(0, 3), slot(0, 1)]
    fp2[1:17, inner2] = first2[...]

    def face2_of(q):
        half = columns[q, W_SEC:W_FIVE]
        other = turn(half, 64, 1)
        return [jnp.where(lane8 < 64, half, other), jnp.where(lane8 < 64, other, half)]

    fp2[0, pl.ds(8, 8)], fp2[0, pl.ds(16, 8)] = face2_of(sides[0])
    fp2[17, pl.ds(8, 8)], fp2[17, pl.ds(16, 8)] = face2_of(sides[1])
    low2, high2 = face2_of(sides[2]), face2_of(sides[3])
    for x in range(16):
        row = slice(x % 8, x % 8 + 1)
        fp2[x + 1, 7:8] = low2[x // 8][row]
        fp2[x + 1, 24:25] = high2[x // 8][row]
    rim_k2 = ck2[...]
    rim_f2 = cf2[...]
    for x in range(16):
        k = kp2[x + 1, inner2]
        e = fp2[x + 1, inner2]
        k_up, k_down = z_sides(k, rim_k2, x, lane2, 64)
        e_up, e_down = z_sides(e, rim_f2, x, lane2, 64)
        around = [
            (kp2[x, inner2], fp2[x, inner2]),
            (kp2[x + 2, inner2], fp2[x + 2, inner2]),
            (kp2[x + 1, pl.ds(7, 16)], fp2[x + 1, pl.ds(7, 16)]),
            (kp2[x + 1, pl.ds(9, 16)], fp2[x + 1, pl.ds(9, 16)]),
            (k_up, e_up),
            (k_down, e_down),
        ]
        total = k * sum(en for _, en in around) + sum(kn * en for kn, en in around)
        w2[x] = 1.2 * e + 0.5 * scale2[x] * total
    two = spread(flat(w2[...]), square(lambda row, col: row == col // 2))
    even8, odd8 = pl.ds(0, 8, stride=2), pl.ds(1, 8, stride=2)
    for i in range(16):
        block = three[8 * (i // 2) : 8 * (i // 2) + 8]
        w2[i, even8, :] = block
        w2[i, odd8, :] = block
    two = two.reshape(16, 16, LANES) + w2[...]
    up[:, pl.ds(0, 16, stride=2), :] = two
    up[:, pl.ds(1, 16, stride=2), :] = two

    inner = pl.ds(8, 32)

    fp[0, inner] = columns[sides[0], W_FACE:W_FOUR]
    fp[33, inner] = columns[sides[1], W_FACE:W_FOUR]

    def fill(x, carry):
        fp[x + 1, inner] = first[x]
        row = pl.ds(W_FACE + x, 1)
        fp[x + 1, 7:8] = columns[sides[2], row]
        fp[x + 1, 40:41] = columns[sides[3], row]
        return carry

    lax.fori_loop(0, 32, fill, 0, unroll=4)
    rim_k = ck[...]
    rim_f = cf[...]

    def slab(x, carry):
        k = kp[x + 1, inner]
        e = fp[x + 1, inner]
        k_up, k_down = z_sides(k, rim_k, x, lane32, LANES)
        e_up, e_down = z_sides(e, rim_f, x, lane32, LANES)
        around = [
            (kp[x, inner], fp[x, inner]),
            (kp[x + 2, inner], fp[x + 2, inner]),
            (kp[x + 1, pl.ds(7, 32)], fp[x + 1, pl.ds(7, 32)]),
            (kp[x + 1, pl.ds(9, 32)], fp[x + 1, pl.ds(9, 32)]),
            (k_up, e_up),
            (k_down, e_down),
        ]
        total = k * sum(en for _, en in around) + sum(kn * en for kn, en in around)
        out[x] = initial[x] + (1.2 * e + 0.5 * scale[x] * total + up[x // 2])
        return carry

    lax.fori_loop(0, 32, slab, 0, unroll=4)


VM = pl.BlockSpec(memory_space=pltpu.VMEM)
SM = pl.BlockSpec(memory_space=pltpu.SMEM)


def shape(*dims):
    return jax.ShapeDtypeStruct(dims, F32)


def local(kernel, outs, ins, scratch, name):
    return pl.pallas_call(
        kernel,
        out_shape=outs,
        in_specs=ins,
        out_specs=[VM] * len(outs),
        scratch_shapes=[pltpu.VMEM(dims, F32) for dims in scratch],
        compiler_params=pltpu.CompilerParams(vmem_limit_bytes=40 * 1024 * 1024),
        name=name,
    )


def on_device(initial, rhs, kappa, sigma):
    place = jnp.stack([lax.axis_index(axis) for axis in ("gx", "gy", "gz")]).astype(jnp.int32)

    def passed(value, axis, step):
        count = lax.axis_size(axis)
        return lax.ppermute(value, axis, [(i, (i + step) % count) for i in range(count)])

    edge = shape(3, 32, LANES)
    xp, xm, yp, ym, zs = local(
        faces_kernel, [edge, edge, edge, edge, shape(2, 32, LANES)], [VM] * 2, [], "faces"
    )(kappa, initial)
    xlo, xhi = passed(xp, "gx", 1), passed(xm, "gx", -1)
    ylo, yhi = passed(yp, "gy", 1), passed(ym, "gy", -1)
    zlo, zhi = passed(zs, "gz", 1), passed(zs, "gz", -1)
    block = (32, 32, LANES)
    block2 = (16, 16, LANES)
    kp, ck, scale, first, message, whole, sides, kp2, ck2, scale2, first2, sides2 = local(
        residual_kernel,
        [
            shape(34, 48, LANES), shape(32, LANES), shape(*block), shape(*block),
            shape(8, Z_ROWS, LANES), shape(64, LANES), shape(4, 32, LANES), shape(18, 32, LANES),
            shape(16, LANES), shape(*block2), shape(*block2), shape(4, 16, LANES),
        ],
        [SM] + [VM] * 10,
        [
            (34, 48, LANES), (16, 32, LANES), (16, 32, LANES), (16, 32, LANES),
            (4, 32, LANES), (8, 16, LANES),
        ],
        "residual",
    )(place, kappa, initial, rhs, sigma, xlo, xhi, ylo, yhi, zlo, zhi)
    lines = lax.all_to_all(message, "gz", 0, 0)
    windows, own, cf, cf2 = local(
        window_kernel,
        [shape(16, W_ROWS, LANES), shape(3, 64, LANES), shape(32, LANES), shape(16, LANES)],
        [SM] + [VM] * 4,
        [(8, 8, LANES)],
        "window",
    )(place, lines, whole, sides, sides2)
    columns = lax.all_to_all(windows, ("gx", "gy"), 0, 0)
    padded3 = (24, 40, LANES)
    block3 = (24, 24, LANES)
    return local(
        cycle_kernel,
        [shape(*block)],
        [SM] + [VM] * 13,
        [
            (34, 48, LANES), (18, 32, LANES), block3, block3, padded3, (7,) + block3,
            padded3, padded3, block2, (8, 8, LANES), (8, 8, LANES), (4, 8, LANES),
            (7,) + block2, (7, 8, 8, LANES), (7, 4, 8, LANES), (7, 4, 8, LANES),
            (16, LANES), (8, 8, LANES), block2, (16, 32, LANES),
        ],
        "cycle",
    )(
        place, columns, own, initial, kp, ck, scale, first, cf, kp2, ck2, scale2, first2, cf2
    )[0]


def solution(mesh):
    spec = P("gx", "gy", "gz")
    return jax.shard_map(
        on_device, mesh=mesh, in_specs=(spec,) * 4, out_specs=spec, check_vma=False
    )
```

```python
import jax
import jax.numpy as jnp
from jax import lax
from jax.experimental import pallas as pl
from jax.experimental.pallas import tpu as pltpu
from jax.sharding import PartitionSpec as P

COARSE_SWEEPS = 8
WEIGHT = 0.8
LANES = 128
F32 = jnp.float32
BF16 = jnp.bfloat16

Z_SMALL, Z_ROWS = 32, 40
X_FACE, X_SEC, X_ENDS, X_ROWS = 64, 96, 104, 112
Y_FACE, Y_SEC, Y_ENDS, Y_ROWS = 192, 224, 232, 240
CHUNKS = 4
BASE = 5


def turn(value, shift, axis):
    size = value.shape[axis]
    if isinstance(shift, int):
        shift = shift % size
        if shift == 0:
            return value
    return pltpu.roll(value, shift, axis)


def lanes_of(shape):
    return lax.broadcasted_iota(jnp.int32, shape, len(shape) - 1)


def square(rule):
    row = lax.broadcasted_iota(jnp.int32, (LANES, LANES), 0)
    col = lax.broadcasted_iota(jnp.int32, (LANES, LANES), 1)
    return jnp.where(rule(row, col), 1.0, 0.0).astype(BF16)


def spread(value, chosen):
    total = None
    for part in range(3):
        piece = value.astype(BF16)
        term = jnp.dot(piece, chosen, preferred_element_type=F32)
        total = term if total is None else total + term
        if part < 2:
            value = value - piece.astype(F32)
    return total


def rows_of(x, shift, pitch, count):
    start = pitch * x + 8
    return pl.ds(start + shift if shift else pl.multiple_of(start, 8), count)


def flat(value):
    return value.reshape(-1, LANES)


def fetch(pairs, sems):
    depth = pairs[0][0].shape[0] // CHUNKS
    copies = []
    for c in range(CHUNKS):
        part = pl.ds(c * depth, depth)
        for n, (far, near) in enumerate(pairs):
            copy = pltpu.make_async_copy(far.at[part], near.at[part], sems.at[n, c])
            copy.start()
            copies.append(copy)
    return copies


def load_kernel(rhs_far, sigma_far, edge, rhs, sigma, sems):
    for copy in fetch(((rhs_far, rhs), (sigma_far, sigma)), sems):
        copy.wait()


def faces_kernel(kappa_far, initial_far, xp, xm, yp, ym, zs, kappa, initial, sems):
    depth = 32 // CHUNKS
    copies = fetch(((kappa_far, kappa), (initial_far, initial)), sems)
    lane = lanes_of((32, LANES))
    first = second = jnp.zeros((32, LANES), F32)

    def body(x, carry):
        first, second = carry
        mine = lane // 4 == x
        shift = 4 * x + 2
        first = jnp.where(mine, turn(kappa[x], shift, 1), first)
        second = jnp.where(mine, turn(initial[x], shift, 1), second)
        return first, second

    for c in range(CHUNKS):
        copies[2 * c].wait()
        copies[2 * c + 1].wait()
        first, second = lax.fori_loop(
            c * depth, (c + 1) * depth, body, (first, second), unroll=True
        )
    zs[0] = first
    zs[1] = second
    xp[0] = kappa[31]
    xp[1] = kappa[30]
    xp[2] = initial[31]
    xm[0] = kappa[0]
    xm[1] = kappa[1]
    xm[2] = initial[0]
    yp[0] = kappa[:, 31, :]
    yp[1] = kappa[:, 30, :]
    yp[2] = initial[:, 31, :]
    ym[0] = kappa[:, 0, :]
    ym[1] = kappa[:, 1, :]
    ym[2] = initial[:, 0, :]


def z_sides(value, rim, x, lane, period):
    near = turn(rim, 126 - 4 * x, 1)
    if period < LANES:
        other = turn(rim, lax.rem(190 - 4 * x, 128), 1)
        near = jnp.where((lane >= 32) & (lane < 96), other, near)
    inside = lane % period
    above = turn(jnp.where(inside == 0, near, value), LANES - 1, 1)
    below = turn(jnp.where(inside == period - 1, near, value), 1, 1)
    return above, below


def residual_kernel(
    kappa, initial, rhs, sigma, xlo, xhi, ylo, yhi, zlo, zhi,
    kp, ck, scale, first, zp, zm, whole, sides, kp2, ck2, scale2, first2, sides2,
    vp, pair_r, pair_k, pair_s, rims, small,
):
    lane = lanes_of((32, LANES))
    inner = pl.ds(8, 32)
    kp[rows_of(0, 0, 40, 32)] = xlo[0]
    kp[rows_of(33, 0, 40, 32)] = xhi[0]
    vp[0, inner] = xlo[2]
    vp[33, inner] = xhi[2]

    def fill(x, carry):
        one = pl.ds(x, 1)
        kp[rows_of(x + 1, 0, 40, 32)] = kappa[x]
        vp[x + 1, inner] = initial[x]
        kp[rows_of(x + 1, -1, 40, 1)] = ylo[0, one]
        kp[rows_of(x + 1, 32, 40, 1)] = yhi[0, one]
        vp[x + 1, 7:8] = ylo[2, one]
        vp[x + 1, 40:41] = yhi[2, one]
        return carry

    lax.fori_loop(0, 32, fill, 0, unroll=4)
    low_half = lane % 4 < 2
    rim_k = jnp.where(low_half, zlo[0], zhi[0])
    rim_v = jnp.where(low_half, zlo[1], zhi[1])
    ck[...] = rim_k

    def slab(x, packed):
        k = kappa[x]
        v = vp[x + 1, inner]
        around = [
            (kp[rows_of(x, 0, 40, 32)], vp[x, inner]),
            (kp[rows_of(x + 2, 0, 40, 32)], vp[x + 2, inner]),
            (kp[rows_of(x + 1, -1, 40, 32)], vp[x + 1, pl.ds(7, 32)]),
            (kp[rows_of(x + 1, 1, 40, 32)], vp[x + 1, pl.ds(9, 32)]),
        ]
        k_up, k_down = z_sides(k, rim_k, x, lane, LANES)
        v_up, v_down = z_sides(v, rim_v, x, lane, LANES)
        around += [(k_up, v_up), (k_down, v_down)]
        k_sum = sum(kn for kn, _ in around)
        v_sum = sum(vn for _, vn in around)
        both = sum(kn * vn for kn, vn in around)
        s = sigma[x]
        diagonal = s + 3.0 * k + 0.5 * k_sum
        r = rhs[x] - diagonal * v + 0.5 * (k * v_sum + both)
        h = WEIGHT / diagonal
        e = h * r
        scale[x] = h
        first[x] = e
        packed = jnp.where(lane // 4 == x, turn(e, 4 * x + 2, 1), packed)
        return r, k, s, packed

    def two(i, packed):
        r0, k0, s0, packed = slab(2 * i, packed)
        r1, k1, s1, packed = slab(2 * i + 1, packed)
        pair_r[i] = r0 + r1
        pair_k[i] = k0 + k1
        pair_s[i] = s0 + s1
        return packed

    packed = lax.fori_loop(0, 16, two, jnp.zeros((32, LANES), F32), unroll=2)
    sides[0] = first[31]
    sides[1] = first[0]
    sides[2] = first[:, 31, :]
    sides[3] = first[:, 0, :]

    even, odd = pl.ds(0, 16, stride=2), pl.ds(1, 16, stride=2)
    to_two = square(lambda row, col: row // 2 == col % 64)

    def level_two(ref, weight):
        summed = ref[:, even, :] + ref[:, odd, :]
        return (spread(flat(summed), to_two) * weight).reshape(16, 16, LANES)

    r2 = level_two(pair_r, 0.5)
    k2 = level_two(pair_k, 0.125)
    s2 = level_two(pair_s, 0.5)
    rims[0] = xlo[0] + xlo[1]
    rims[1] = xhi[0] + xhi[1]
    rims[2] = ylo[0] + ylo[1]
    rims[3] = yhi[0] + yhi[1]
    halo = rims[:, even, :] + rims[:, odd, :]
    halo = (spread(flat(halo), to_two) * 0.125).reshape(4, 16, LANES)
    kp2[rows_of(0, 0, 24, 16)] = halo[0]
    kp2[rows_of(17, 0, 24, 16)] = halo[1]
    for x in range(16):
        kp2[rows_of(x + 1, 0, 24, 16)] = k2[x]
        kp2[rows_of(x + 1, -1, 24, 1)] = halo[2, x : x + 1]
        kp2[rows_of(x + 1, 16, 24, 1)] = halo[3, x : x + 1]
    rims[0] = rim_k
    rim_pair = rims[0, even, :] + rims[0, odd, :]

    def rim_rule(row, col):
        low = (col % 4 == 1) & (row % 4 < 2)
        high = (col % 4 == 2) & (row % 4 >= 2)
        return (row // 8 == col // 4) & (low | high)

    rim_k2 = spread(rim_pair, square(rim_rule)) * 0.125
    ck2[...] = rim_k2
    lane2 = lanes_of((16, LANES))
    packed2 = jnp.zeros((16, LANES), F32)
    for x in range(16):
        k = k2[x]
        up, down = z_sides(k, rim_k2, x, lane2, 64)
        k_sum = (
            kp2[rows_of(x, 0, 24, 16)] + kp2[rows_of(x + 2, 0, 24, 16)]
            + kp2[rows_of(x + 1, -1, 24, 16)] + kp2[rows_of(x + 1, 1, 24, 16)] + up + down
        )
        h = WEIGHT / (s2[x] + 3.0 * k + 0.5 * k_sum)
        e = h * r2[x]
        scale2[x] = h
        first2[x] = e
        packed2 = jnp.where(lane2 // 4 == x, turn(e, 4 * x + 2, 1), packed2)
    sides2[0] = first2[15]
    sides2[1] = first2[0]
    sides2[2] = first2[:, 15, :]
    sides2[3] = first2[:, 0, :]

    even8, odd8 = pl.ds(0, 8, stride=2), pl.ds(1, 8, stride=2)

    def level_three(field, part, weight):
        halves = field.reshape(8, 2, 16, LANES)
        small[...] = halves[:, 0] + halves[:, 1]
        summed = small[:, even8, :] + small[:, odd8, :]
        rule = square(lambda row, col: (row < 64) & (row // 2 == col - 32 * part))
        return spread(flat(summed), rule) * weight

    three = level_three(r2, 0, 0.5) + level_three(k2, 1, 0.125) + level_three(s2, 2, 0.5)
    whole[...] = three
    for out, start, tag in ((zp, 16, 1), (zm, 0, 2)):
        half = spread(
            three,
            square(
                lambda row, col, start=start: (col < 48)
                & (row == 32 * (col // 16) + start + col % 16)
            ),
        )
        face = spread(packed, square(lambda row, col, tag=tag: row == 4 * (col - 96) + tag))
        out[0:Z_SMALL] = half[0:32] + turn(half[32:64], 48, 1) + face
        face2 = spread(
            packed2, square(lambda row, col, tag=tag: (col < 16) & (row == 4 * col + tag))
        )
        out[Z_SMALL:Z_ROWS] = face2[0:8] + turn(face2[8:16], 16, 1)


def block_kernel(whole, block, small):
    three = whole[...]
    halves = three.reshape(4, 2, 8, LANES)
    small[0:4, 0:8] = halves[:, 0] + halves[:, 1]
    summed = small[0:4, pl.ds(0, 4, stride=2), :] + small[0:4, pl.ds(1, 4, stride=2), :]
    for i in range(4):
        small[4, 4 * i : 4 * i + 4] = summed[i]
    four = small[4]

    def pick(part, start):
        rule = square(
            lambda row, col: (row // 32 == part)
            & (col >= start) & (col < start + 16) & (row % 32 // 2 == col - start)
        )
        return spread(four, rule)

    both = 0.5 * pick(0, 0) + 0.125 * pick(1, 64)
    below = 0.5 * pick(2, 0)
    for i in range(4):
        rows = slice(4 * i, 4 * i + 4)
        upper = turn(both[rows], 16 * i, 1) if i == 0 else upper + turn(both[rows], 16 * i, 1)
        lower = turn(below[rows], 16 * i, 1) if i == 0 else lower + turn(below[rows], 16 * i, 1)
    small[5, 0:4] = upper
    small[5, 4:8] = lower
    block[...] = small[5, 0:8]


def window_kernel(
    zlo, zhi, whole, sides, sides2, block, own, xp, xm, ye, cf, cf2, blocks, small
):
    value = block[...]
    for p in range(128):
        blocks[p] = value
    lane = lanes_of((64, LANES))
    a_half, c_half = zlo[0:Z_SMALL], zhi[0:Z_SMALL]
    a = jnp.concatenate([a_half, turn(a_half, -48, 1)], 0)
    b = whole[...]
    c = jnp.concatenate([c_half, turn(c_half, -48, 1)], 0)

    def window(part):
        low = turn(a, BASE - 16 - 16 * part, 1)
        mid = turn(b, BASE - 32 * part, 1)
        high = turn(c, BASE + 32 - 16 * part, 1)
        value = jnp.where((lane < BASE) | (lane >= 112 + BASE), low, mid)
        value = jnp.where((lane >= BASE + 32) & (lane < BASE + 48), high, value)
        return jnp.where((lane >= BASE + 48) & (lane < 112 + BASE), 0.0, value)

    r, k, s = window(0), window(1), window(2)
    own[0], own[1], own[2] = r, k, s
    main = jnp.where(lane < 42, r, jnp.where(lane < 86, turn(k, 43, 1), turn(s, 86, 1)))
    low = jnp.where(lane == 127, r, jnp.where(lane == 126, k, turn(s, -2, 1)))
    high = jnp.where(lane == 42, r, jnp.where(lane == 43, k, turn(s, 2, 1)))
    ends = jnp.where(lane >= 64, low, turn(high, 86, 1))
    small[...] = ends.reshape(8, 8, LANES)
    ye[0] = small[:, 7, :]
    ye[1] = small[:, 0, :]
    lane8 = lanes_of((8, LANES))
    for side, out, i in ((0, xp, 7), (1, xm, 0)):
        out[0:X_FACE] = main
        out[X_FACE:X_SEC] = sides[side]
        out[X_SEC:X_ENDS] = jnp.where(lane8 < 64, sides2[side, 0:8], sides2[side, 8:16])
        out[X_ENDS:X_ROWS] = ends[8 * i : 8 * i + 8]

    def rim(low, high, ready):
        below = spread(low, square(lambda row, col: ready(row) & (col == 4 * (row % 32) + 1)))
        above = spread(high, square(lambda row, col: ready(row) & (col == 4 * (row % 32) + 2)))
        return below + above

    cf[...] = rim(a_half, c_half, lambda row: row >= 96)

    def unfold(half):
        return jnp.concatenate([half, turn(half, -16, 1)], 0)

    cf2[...] = rim(
        unfold(zlo[Z_SMALL:Z_ROWS]), unfold(zhi[Z_SMALL:Z_ROWS]), lambda row: row < 16
    )


def columns_kernel(xlo, xhi, xp, sides, sides2, ye, after, yp, ym):
    lane8 = lanes_of((8, LANES))
    for side, out in ((0, yp), (1, ym)):
        out[0:64] = xlo[0:64]
        out[64:128] = xp[0:64]
        out[128:192] = xhi[0:64]
        out[Y_FACE:Y_SEC] = sides[2 + side]
        face = sides2.at[2 + side]
        out[Y_SEC:Y_ENDS] = jnp.where(lane8 < 64, face[0:8], face[8:16])
        out[Y_ENDS:Y_ROWS] = ye[side]


def wrapped(value):
    last = value.shape[0] - 1
    return [
        jnp.concatenate([value[1:], value[:1]], 0),
        jnp.concatenate([value[last:], value[:last]], 0),
        turn(value, -1, 1),
        turn(value, 1, 1),
        turn(value, -1, 2),
        turn(value, 1, 2),
    ]


def periodic_setup(r, k, s, coefs):
    near = wrapped(k)
    diagonal = s + 3.0 * k + 0.5 * sum(near)
    h = WEIGHT / diagonal
    half = 0.5 * h
    for n in range(6):
        coefs[n] = half * (k + near[n])
    start = h * r
    coefs[6] = start
    return start


def periodic_sweep(e, coefs):
    total = 0.2 * e + coefs[6]
    for n, other in enumerate(wrapped(e)):
        total = total + coefs[n] * other
    return total


def planes_kernel(
    place, blocks_far, four_out,
    r4, k4, s4, half, l5, l6, c4, c5, c6, c7, w4, blocks, sems,
):
    copies = fetch(((blocks_far, blocks),), sems)
    gx, gy, gz = place[0], place[1], place[2]
    lane8 = lanes_of((8, LANES))
    group = lane8 // 16

    def assemble(q, carry):
        pieces = [blocks[8 * q + g] for g in range(8)]
        for i in range(4):
            straight = crossed = jnp.zeros((8, LANES), F32)
            for g in range(8):
                moved = turn(pieces[g], 16 * (g - i), 1)
                straight = jnp.where(group == g, moved, straight)
                crossed = jnp.where(group == (g + 4) % 8, moved, crossed)
            x = 4 * (q // 4) + i
            rows = pl.ds(pl.multiple_of(4 * (q % 4), 4), 4)
            r4[x, rows] = straight[0:4]
            s4[x, rows] = straight[4:8]
            k4[x, rows] = turn(crossed, 64, 1)[0:4]
        return carry

    for c in range(CHUNKS):
        copies[c].wait()
        lax.fori_loop(4 * c, 4 * c + 4, assemble, 0, unroll=True)
    fields4 = r4[...], k4[...], s4[...]
    e4 = periodic_setup(*fields4, c4)
    to_five = square(lambda row, col: row // 2 == col % 64)
    to_six = square(lambda row, col: (row < 64) & (row // 2 == col % 32))
    mean = square(lambda row, col: row < 32)

    def level_five(field, weight):
        pairs = field.reshape(8, 2, 16, LANES)
        half[...] = pairs[:, 0] + pairs[:, 1]
        summed = half[:, pl.ds(0, 8, stride=2), :] + half[:, pl.ds(1, 8, stride=2), :]
        return (spread(flat(summed), to_five) * weight).reshape(8, 8, LANES)

    def level_six(field, weight):
        pairs = field.reshape(4, 2, 8, LANES)
        l6[...] = pairs[:, 0] + pairs[:, 1]
        summed = l6[:, pl.ds(0, 4, stride=2), :] + l6[:, pl.ds(1, 4, stride=2), :]
        l6[:, 0:4] = summed
        l6[:, 4:8] = summed
        return (spread(flat(l6[...]), to_six) * weight).reshape(4, 8, LANES)

    def level_seven(field):
        return (spread(flat(field), mean) * (1.0 / 32.0)).reshape(4, 8, LANES)

    weights = (0.5, 0.125, 0.5)
    fields5 = [level_five(f, w) for f, w in zip(fields4, weights)]
    e5 = periodic_setup(*fields5, c5)
    fields6 = [level_six(f, w) for f, w in zip(fields5, weights)]
    e6 = periodic_setup(*fields6, c6)
    e7 = periodic_setup(*[level_seven(f) for f in fields6], c7)

    def sweep(_, carry):
        a, b, c, d = carry
        return (
            periodic_sweep(a, c4), periodic_sweep(b, c5), periodic_sweep(c, c6),
            periodic_sweep(d, c7),
        )

    e4, e5, e6, e7 = lax.fori_loop(0, COARSE_SWEEPS - 1, sweep, (e4, e5, e6, e7))

    l6[...] = e6 + e7
    six = turn(l6[gx, pl.ds(gy, 1)] + jnp.zeros((8, LANES), F32), 128 - 4 * gz, 1)
    six = spread(six, square(lambda row, col: row == col // 32))
    l5[...] = e5
    w4[...] = jnp.zeros((16, LANES), F32)
    w4[0:2] = l5[2 * gx, pl.ds(2 * gy, 2)]
    w4[2:4] = l5[2 * gx + 1, pl.ds(2 * gy, 2)]
    five = spread(turn(w4[0:8], 128 - 8 * gz, 1), square(lambda row, col: row == col // 16))
    five = five + six
    r4[...] = e4
    for i in range(4):
        w4[4 * i : 4 * i + 4] = r4[4 * gx + i, pl.ds(4 * gy, 4)]
    four = turn(w4[...], lax.rem(128 - 16 * gz, 128), 1)
    four = spread(four, square(lambda row, col: row == col // 8))
    for i in range(4):
        for j in range(2):
            row = 2 * (i // 2) + j
            w4[4 * i + 2 * j : 4 * i + 2 * j + 2] = jnp.broadcast_to(
                five[row : row + 1], (2, LANES)
            )
    four_out[...] = four + w4[...]


def fine_kernel(
    kp, ck, scale, first, cf, kp2, ck2, scale2, first2, cf2,
    base, base2, edge, edge2, fp, fp2,
):
    inner, inner2 = pl.ds(8, 32), pl.ds(8, 16)
    lane2, lane32 = [lanes_of((rows, LANES)) for rows in (16, 32)]
    fp2[1:17, inner2] = first2[...]
    for x in (0, 17):
        fp2[x, inner2] = jnp.zeros((16, LANES), F32)
    fp2[:, 0:8] = jnp.zeros((18, 8, LANES), F32)
    fp2[:, 24:32] = jnp.zeros((18, 8, LANES), F32)

    def second(k_ref, f_ref, x, rows, k_rim, f_rim, lane, period, h):
        inside, pitch = pl.ds(8, rows), rows + 8
        k, e = k_ref[rows_of(x + 1, 0, pitch, rows)], f_ref[x + 1, inside]
        k_up, k_down = z_sides(k, k_rim, x, lane, period)
        e_up, e_down = z_sides(e, f_rim, x, lane, period)
        around = [
            (k_ref[rows_of(x, 0, pitch, rows)], f_ref[x, inside]),
            (k_ref[rows_of(x + 2, 0, pitch, rows)], f_ref[x + 2, inside]),
            (k_ref[rows_of(x + 1, -1, pitch, rows)], f_ref[x + 1, pl.ds(7, rows)]),
            (k_ref[rows_of(x + 1, 1, pitch, rows)], f_ref[x + 1, pl.ds(9, rows)]),
            (k_up, e_up),
            (k_down, e_down),
        ]
        total = k * sum(en for _, en in around) + sum(kn * en for kn, en in around)
        return 1.2 * e + 0.5 * h * total

    rim_k2, rim_f2 = ck2[...], cf2[...]
    for x in range(16):
        base2[x] = second(kp2, fp2, x, 16, rim_k2, rim_f2, lane2, 64, scale2[x])

    for x in (0, 33):
        fp[x, inner] = jnp.zeros((32, LANES), F32)
    blank = jnp.zeros((8, LANES), F32)

    def fill(x, carry):
        fp[x + 1, inner] = first[x]
        fp[x + 1, 0:8] = blank
        fp[x + 1, 40:48] = blank
        return carry

    lax.fori_loop(0, 32, fill, 0, unroll=4)
    rim_k, rim_f = ck[...], cf[...]

    def slab(x, carry):
        base[x] = second(kp, fp, x, 32, rim_k, rim_f, lane32, LANES, scale[x])
        return carry

    lax.fori_loop(0, 32, slab, 0, unroll=4)
    for n, (x, step) in enumerate(((0, -1), (31, 1))):
        k = kp[rows_of(x + 1, 0, 40, 32)] + kp[rows_of(x + 1 + step, 0, 40, 32)]
        edge[n] = 0.5 * scale[x] * k
    for n, (x, step) in enumerate(((0, -1), (15, 1))):
        k = kp2[rows_of(x + 1, 0, 24, 16)] + kp2[rows_of(x + 1 + step, 0, 24, 16)]
        edge2[n] = 0.5 * scale2[x] * k
    for n, (y, step) in enumerate(((0, -1), (31, 1))):
        k = kp[pl.ds(48 + y, 32, stride=40), :] + kp[pl.ds(48 + y + step, 32, stride=40), :]
        edge[2 + n] = 0.5 * scale[:, y, :] * k
    for n, (y, step) in enumerate(((0, -1), (15, 1))):
        k = kp2[pl.ds(32 + y, 16, stride=24), :] + kp2[pl.ds(32 + y + step, 16, stride=24), :]
        edge2[2 + n] = 0.5 * scale2[:, y, :] * k


def finish_kernel(
    initial_far, own, xlo, xhi, ylo, yhi, four_in, base, base2, edge, edge2,
    out_far,
    r3, s3, k3, c3, ea, eb, w3, w2, w32, up, out, initial, sems,
):
    inputs = fetch(((initial_far, initial),), sems)
    lane8 = lanes_of((8, LANES))
    for ix in range(3):
        for iy, y_ref in enumerate((ylo, None, yhi)):
            for i in range(8):
                if ix == 1 and iy == 1:
                    r, k, s = [own[f, 8 * i : 8 * i + 8] for f in range(3)]
                else:
                    if iy == 1:
                        r = (xlo if ix == 0 else xhi)[8 * i : 8 * i + 8]
                    else:
                        r = y_ref[64 * ix + 8 * i : 64 * ix + 8 * i + 8]
                    k = turn(r, -43, 1)
                    s = turn(r, -86, 1)
                    if iy == 1 and ((ix == 0 and i == 7) or (ix == 2 and i == 0)):
                        low = (xlo if ix == 0 else xhi)[X_ENDS:X_ROWS]
                        high = turn(low, 42, 1)
                        r = jnp.where(lane8 == 127, low, jnp.where(lane8 == 42, high, r))
                        k = jnp.where(lane8 == 126, low, jnp.where(lane8 == 43, high, k))
                        low, high = turn(low, 2, 1), turn(high, -2, 1)
                        s = jnp.where(lane8 == 127, low, jnp.where(lane8 == 42, high, s))
                x, y = 8 * ix + i, 8 * iy
                r3[x, y : y + 8] = r
                k3[x, y + 8 : y + 16] = k
                s3[x, y : y + 8] = s
    lane1 = lanes_of((1, LANES))
    for y, y_ref in ((7, ylo), (16, yhi)):
        low = y_ref[Y_ENDS:Y_ROWS]
        high = turn(low, 42, 1)
        low_s, high_s = turn(low, 2, 1), turn(high, -2, 1)
        for i in range(8):
            row = slice(i, i + 1)

            def patch(ref, at, below, above, low_lane, high_lane):
                kept = jnp.where(lane1 == high_lane, above[row], ref[8 + i, at : at + 1])
                ref[8 + i, at : at + 1] = jnp.where(lane1 == low_lane, below[row], kept)

            patch(r3, y, low, high, 127, 42)
            patch(k3, y + 8, low, high, 126, 43)
            patch(s3, y, low_s, high_s, 127, 42)
    rim = jnp.zeros((24, 8, LANES), F32)
    for ref in (k3, ea, eb):
        ref[:, 0:8] = rim
        ref[:, 32:40] = rim
    mid = pl.ds(8, 24)

    def setup3(x, carry):
        k = k3[x, mid]
        near = [
            k3[x + 1, mid], k3[x - 1, mid], k3[x, pl.ds(9, 24)], k3[x, pl.ds(7, 24)],
            turn(k, -1, 1), turn(k, 1, 1),
        ]
        h = WEIGHT / (s3[x] + 3.0 * k + 0.5 * sum(near))
        half = 0.5 * h
        for n in range(6):
            c3[n, x] = half * (k + near[n])
        g = h * r3[x]
        c3[6, x] = g
        ea[x, mid] = g
        return carry

    lax.fori_loop(1, 23, setup3, 0, unroll=True)
    source, target = ea, eb
    for step in range(2, COARSE_SWEEPS + 1):

        def sweep3(x, carry, source=source, target=target):
            e = source[x, mid]
            near = [
                source[x + 1, mid], source[x - 1, mid],
                source[x, pl.ds(9, 24)], source[x, pl.ds(7, 24)],
                turn(e, -1, 1), turn(e, 1, 1),
            ]
            total = 0.2 * e + c3[6, x]
            for n in range(6):
                total = total + c3[n, x] * near[n]
            target[x, mid] = total
            return carry

        lax.fori_loop(step, 24 - step, sweep3, 0, unroll=True)
        source, target = target, source

    mine = source[8:16, 16:24]
    lane3 = lanes_of((8, 8, LANES))
    three = flat(jnp.where((lane3 >= BASE) & (lane3 < BASE + 32), mine, 0.0))
    three = spread(three, square(lambda row, col: row == BASE + col // 4))
    four = four_in[...]
    for i in range(8):
        block = four[4 * (i // 2) : 4 * (i // 2) + 4]
        w3[i, pl.ds(0, 4, stride=2), :] = block
        w3[i, pl.ds(1, 4, stride=2), :] = block
    three = three + flat(w3[...])

    def beyond(ref, start):
        half = ref[start : start + 8]
        other = turn(half, 64, 1)
        return jnp.concatenate(
            [jnp.where(lane8 < 64, half, other), jnp.where(lane8 < 64, other, half)], 0
        )

    w2[...] = base2[...]
    for n, (x, ref) in enumerate(((0, xlo), (15, xhi))):
        w2[x] = w2[x] + edge2[n] * beyond(ref, X_SEC)
    for n, (y, ref) in enumerate(((0, ylo), (15, yhi))):
        w2[:, y, :] = w2[:, y, :] + edge2[2 + n] * beyond(ref, Y_SEC)
    two = spread(flat(w2[...]), square(lambda row, col: row == col // 2))
    even8, odd8 = pl.ds(0, 8, stride=2), pl.ds(1, 8, stride=2)
    for i in range(16):
        block = three[8 * (i // 2) : 8 * (i // 2) + 8]
        w32[i, even8, :] = block
        w32[i, odd8, :] = block
    two = two.reshape(16, 16, LANES) + w32[...]
    up[:, pl.ds(0, 16, stride=2), :] = two
    up[:, pl.ds(1, 16, stride=2), :] = two

    depth = 32 // CHUNKS
    copies = []
    for c in range(CHUNKS):
        part = pl.ds(c * depth, depth)
        inputs[c].wait()
        for x in range(c * depth, (c + 1) * depth):
            total = initial[x] + (base[x] + up[x // 2])
            if x in (0, 31):
                face = (xhi if x else xlo)[X_FACE:X_SEC]
                total = total + edge[1 if x else 0] * face
            out[x] = total
        for n, (y, ref) in enumerate(((0, ylo), (31, yhi))):
            face = ref[pl.ds(Y_FACE + c * depth, depth)]
            out[part, y, :] = out[part, y, :] + edge[2 + n, part] * face
        copy = pltpu.make_async_copy(out.at[part], out_far.at[part], sems.at[1, c])
        copy.start()
        copies.append(copy)
    for copy in copies:
        copy.wait()


VM = pl.BlockSpec(memory_space=pltpu.VMEM)
SM = pl.BlockSpec(memory_space=pltpu.SMEM)
FAR = pl.BlockSpec(memory_space=pltpu.HBM)


def shape(*dims):
    return pltpu.VMEM(dims, F32)


def local(kernel, outs, ins, scratch, name, sems=None, out_spec=VM):
    scratch = [pltpu.VMEM(dims, F32) for dims in scratch]
    if sems is not None:
        scratch.append(pltpu.SemaphoreType.DMA(sems))
    return pl.pallas_call(
        kernel,
        out_shape=outs,
        in_specs=ins,
        out_specs=[out_spec] * len(outs),
        scratch_shapes=scratch,
        compiler_params=pltpu.CompilerParams(vmem_limit_bytes=24 * 1024 * 1024),
        name=name,
    )


def on_device(initial, rhs, kappa, sigma):
    place = jnp.stack([lax.axis_index(axis) for axis in ("gx", "gy", "gz")]).astype(jnp.int32)

    def passed(value, axis, step):
        count = lax.axis_size(axis)
        return lax.ppermute(value, axis, [(i, (i + step) % count) for i in range(count)])

    block = (32, 32, LANES)
    block2 = (16, 16, LANES)
    edge = shape(3, 32, LANES)
    far = [
        pltpu.with_memory_space_constraint(value, pltpu.HBM)
        for value in (kappa, initial, rhs, sigma)
    ]
    xp, xm, yp, ym, zs, kappa, initial = local(
        faces_kernel,
        [edge, edge, edge, edge, shape(2, 32, LANES)] + [shape(*block)] * 2,
        [FAR] * 2, [], "faces", sems=(2, CHUNKS),
    )(*far[:2])
    rhs, sigma = local(
        load_kernel, [shape(*block)] * 2, [FAR, FAR, VM], [], "load", sems=(2, CHUNKS)
    )(*far[2:], zs)
    zlo, zhi = passed(zs, "gz", 1), passed(zs, "gz", -1)
    xlo, xhi = passed(xp, "gx", 1), passed(xm, "gx", -1)
    ylo, yhi = passed(yp, "gy", 1), passed(ym, "gy", -1)
    kp, ck, scale, first, zp, zm, whole, sides, kp2, ck2, scale2, first2, sides2 = local(
        residual_kernel,
        [
            shape(1368, LANES), shape(32, LANES), shape(*block), shape(*block),
            shape(Z_ROWS, LANES), shape(Z_ROWS, LANES),
            shape(64, LANES), shape(4, 32, LANES), shape(440, LANES),
            shape(16, LANES), shape(*block2), shape(*block2), shape(4, 16, LANES),
        ],
        [VM] * 10,
        [
            (34, 48, LANES), (16, 32, LANES), (16, 32, LANES), (16, 32, LANES),
            (4, 32, LANES), (8, 16, LANES),
        ],
        "residual",
    )(kappa, initial, rhs, sigma, xlo, xhi, ylo, yhi, zlo, zhi)

    (level4,) = local(block_kernel, [shape(8, LANES)], [VM], [(8, 16, LANES)], "block")(whole)
    zlo, zhi = passed(zp, "gz", 1), passed(zm, "gz", -1)
    own, xp, xm, ye, cf, cf2, blocks = local(
        window_kernel,
        [
            shape(3, 64, LANES), shape(X_ROWS, LANES), shape(X_ROWS, LANES),
            shape(2, 8, LANES), shape(32, LANES), shape(16, LANES),
            pltpu.HBM((128, 8, LANES), F32),
        ],
        [VM] * 6, [(8, 8, LANES)], "window",
    )(zlo, zhi, whole, sides, sides2, level4)
    xlo, xhi = passed(xp, "gx", 1), passed(xm, "gx", -1)
    planes = lax.all_to_all(blocks, ("gx", "gy", "gz"), 0, 0)
    base, base2, edge, edge2 = local(
        fine_kernel,
        [shape(*block), shape(*block2), shape(4, 32, LANES), shape(4, 16, LANES)],
        [VM] * 10, [(34, 48, LANES), (18, 32, LANES)], "fine",
    )(kp, ck, scale, first, cf, kp2, ck2, scale2, first2, cf2)
    yp, ym = local(
        columns_kernel, [shape(Y_ROWS, LANES)] * 2, [VM] * 7, [], "columns"
    )(xlo, xhi, xp, sides, sides2, ye, edge2)
    ylo, yhi = passed(yp, "gy", 1), passed(ym, "gy", -1)
    (four,) = local(
        planes_kernel, [shape(16, LANES)], [SM, FAR],
        [
            block2, block2, block2, (8, 16, LANES), (8, 8, LANES), (4, 8, LANES),
            (7,) + block2, (7, 8, 8, LANES), (7, 4, 8, LANES), (7, 4, 8, LANES), (16, LANES),
            (128, 8, LANES),
        ],
        "planes", sems=(1, CHUNKS),
    )(place, pltpu.with_memory_space_constraint(planes, pltpu.HBM))
    padded3 = (24, 40, LANES)
    block3 = (24, 24, LANES)
    return local(
        finish_kernel, [pltpu.HBM(block, F32)], [FAR] + [VM] * 10,
        [
            block3, block3, padded3, (7,) + block3, padded3, padded3,
            (8, 8, LANES), block2, block2, (16, 32, LANES), block, block,
        ],
        "finish", sems=(2, CHUNKS), out_spec=FAR,
    )(far[1], own, xlo, xhi, ylo, yhi, four, base, base2, edge, edge2)[0]


def solution(mesh):
    spec = P("gx", "gy", "gz")
    return jax.shard_map(
        on_device, mesh=mesh, in_specs=(spec,) * 4, out_specs=spec, check_vma=False
    )
```

```python
import jax
import jax.numpy as jnp
from jax import lax
from jax.experimental import pallas as pl
from jax.experimental.pallas import tpu as pltpu
from jax.sharding import PartitionSpec as P

COARSE_SWEEPS = 8
WEIGHT = 0.8
LANES = 128
F32 = jnp.float32
BF16 = jnp.bfloat16

Z_SMALL, Z_ROWS = 32, 40
X_FACE, X_SEC, X_ENDS, X_ROWS = 64, 96, 104, 112
Y_FACE, Y_SEC, Y_ENDS, Y_ROWS = 192, 224, 232, 240
CHUNKS = 4
BASE = 5


def turn(value, shift, axis):
    size = value.shape[axis]
    if isinstance(shift, int):
        shift = shift % size
        if shift == 0:
            return value
    return pltpu.roll(value, shift, axis)


def lanes_of(shape):
    return lax.broadcasted_iota(jnp.int32, shape, len(shape) - 1)


def square(rule):
    row = lax.broadcasted_iota(jnp.int32, (LANES, LANES), 0)
    col = lax.broadcasted_iota(jnp.int32, (LANES, LANES), 1)
    return jnp.where(rule(row, col), 1.0, 0.0).astype(BF16)


def spread(value, chosen):
    total = None
    for part in range(3):
        piece = value.astype(BF16)
        term = jnp.dot(piece, chosen, preferred_element_type=F32)
        total = term if total is None else total + term
        if part < 2:
            value = value - piece.astype(F32)
    return total


def rows_of(x, shift, pitch, count):
    start = pitch * x + 8
    return pl.ds(start + shift if shift else pl.multiple_of(start, 8), count)


def flat(value):
    return value.reshape(-1, LANES)


def fetch(pairs, sems):
    depth = pairs[0][0].shape[0] // CHUNKS
    copies = []
    for c in range(CHUNKS):
        part = pl.ds(c * depth, depth)
        for n, (far, near) in enumerate(pairs):
            copy = pltpu.make_async_copy(far.at[part], near.at[part], sems.at[n, c])
            copy.start()
            copies.append(copy)
    return copies


def load_kernel(rhs_far, sigma_far, edge, rhs, sigma, sems):
    for copy in fetch(((rhs_far, rhs), (sigma_far, sigma)), sems):
        copy.wait()


def faces_kernel(kappa_far, initial_far, xp, xm, yp, ym, zs, kappa, initial, sems):
    depth = 32 // CHUNKS
    copies = fetch(((kappa_far, kappa), (initial_far, initial)), sems)
    lane = lanes_of((32, LANES))
    first = second = jnp.zeros((32, LANES), F32)

    def body(x, carry):
        first, second = carry
        mine = lane // 4 == x
        shift = 4 * x + 2
        first = jnp.where(mine, turn(kappa[x], shift, 1), first)
        second = jnp.where(mine, turn(initial[x], shift, 1), second)
        return first, second

    for c in range(CHUNKS):
        copies[2 * c].wait()
        copies[2 * c + 1].wait()
        first, second = lax.fori_loop(
            c * depth, (c + 1) * depth, body, (first, second), unroll=True
        )
    zs[0] = first
    zs[1] = second
    xp[0] = kappa[31]
    xp[1] = kappa[30]
    xp[2] = initial[31]
    xm[0] = kappa[0]
    xm[1] = kappa[1]
    xm[2] = initial[0]
    yp[0] = kappa[:, 31, :]
    yp[1] = kappa[:, 30, :]
    yp[2] = initial[:, 31, :]
    ym[0] = kappa[:, 0, :]
    ym[1] = kappa[:, 1, :]
    ym[2] = initial[:, 0, :]


def z_sides(value, rim, x, lane, period):
    near = turn(rim, 126 - 4 * x, 1)
    if period < LANES:
        other = turn(rim, lax.rem(190 - 4 * x, 128), 1)
        near = jnp.where((lane >= 32) & (lane < 96), other, near)
    inside = lane % period
    above = turn(jnp.where(inside == 0, near, value), LANES - 1, 1)
    below = turn(jnp.where(inside == period - 1, near, value), 1, 1)
    return above, below


def residual_kernel(
    kappa, initial, rhs, sigma, xlo, xhi, ylo, yhi, zlo, zhi,
    kp, ck, scale, first, zp, zm, whole, sides, kp2, ck2, scale2, first2, sides2,
    vp, pair_r, pair_k, pair_s, rims, small,
):
    lane = lanes_of((32, LANES))
    inner = pl.ds(8, 32)
    kp[rows_of(0, 0, 40, 32)] = xlo[0]
    kp[rows_of(33, 0, 40, 32)] = xhi[0]
    vp[0, inner] = xlo[2]
    vp[33, inner] = xhi[2]

    def fill(x, carry):
        one = pl.ds(x, 1)
        kp[rows_of(x + 1, 0, 40, 32)] = kappa[x]
        vp[x + 1, inner] = initial[x]
        kp[rows_of(x + 1, -1, 40, 1)] = ylo[0, one]
        kp[rows_of(x + 1, 32, 40, 1)] = yhi[0, one]
        vp[x + 1, 7:8] = ylo[2, one]
        vp[x + 1, 40:41] = yhi[2, one]
        return carry

    lax.fori_loop(0, 32, fill, 0, unroll=4)
    low_half = lane % 4 < 2
    rim_k = jnp.where(low_half, zlo[0], zhi[0])
    rim_v = jnp.where(low_half, zlo[1], zhi[1])
    ck[...] = rim_k

    def slab(x, packed):
        k = kappa[x]
        v = vp[x + 1, inner]
        around = [
            (kp[rows_of(x, 0, 40, 32)], vp[x, inner]),
            (kp[rows_of(x + 2, 0, 40, 32)], vp[x + 2, inner]),
            (kp[rows_of(x + 1, -1, 40, 32)], vp[x + 1, pl.ds(7, 32)]),
            (kp[rows_of(x + 1, 1, 40, 32)], vp[x + 1, pl.ds(9, 32)]),
        ]
        k_up, k_down = z_sides(k, rim_k, x, lane, LANES)
        v_up, v_down = z_sides(v, rim_v, x, lane, LANES)
        around += [(k_up, v_up), (k_down, v_down)]
        k_sum = sum(kn for kn, _ in around)
        v_sum = sum(vn for _, vn in around)
        both = sum(kn * vn for kn, vn in around)
        s = sigma[x]
        diagonal = s + 3.0 * k + 0.5 * k_sum
        r = rhs[x] - diagonal * v + 0.5 * (k * v_sum + both)
        h = WEIGHT / diagonal
        e = h * r
        scale[x] = h
        first[x] = e
        packed = jnp.where(lane // 4 == x, turn(e, 4 * x + 2, 1), packed)
        return r, k, s, packed

    def two(i, packed):
        r0, k0, s0, packed = slab(2 * i, packed)
        r1, k1, s1, packed = slab(2 * i + 1, packed)
        pair_r[i] = r0 + r1
        pair_k[i] = k0 + k1
        pair_s[i] = s0 + s1
        return packed

    packed = lax.fori_loop(0, 16, two, jnp.zeros((32, LANES), F32), unroll=2)
    sides[0] = first[31]
    sides[1] = first[0]
    sides[2] = first[:, 31, :]
    sides[3] = first[:, 0, :]

    even, odd = pl.ds(0, 16, stride=2), pl.ds(1, 16, stride=2)
    to_two = square(lambda row, col: row // 2 == col % 64)

    def level_two(ref, weight):
        summed = ref[:, even, :] + ref[:, odd, :]
        return (spread(flat(summed), to_two) * weight).reshape(16, 16, LANES)

    r2 = level_two(pair_r, 0.5)
    k2 = level_two(pair_k, 0.125)
    s2 = level_two(pair_s, 0.5)
    rims[0] = xlo[0] + xlo[1]
    rims[1] = xhi[0] + xhi[1]
    rims[2] = ylo[0] + ylo[1]
    rims[3] = yhi[0] + yhi[1]
    halo = rims[:, even, :] + rims[:, odd, :]
    halo = (spread(flat(halo), to_two) * 0.125).reshape(4, 16, LANES)
    kp2[rows_of(0, 0, 24, 16)] = halo[0]
    kp2[rows_of(17, 0, 24, 16)] = halo[1]
    for x in range(16):
        kp2[rows_of(x + 1, 0, 24, 16)] = k2[x]
        kp2[rows_of(x + 1, -1, 24, 1)] = halo[2, x : x + 1]
        kp2[rows_of(x + 1, 16, 24, 1)] = halo[3, x : x + 1]
    rims[0] = rim_k
    rim_pair = rims[0, even, :] + rims[0, odd, :]

    def rim_rule(row, col):
        low = (col % 4 == 1) & (row % 4 < 2)
        high = (col % 4 == 2) & (row % 4 >= 2)
        return (row // 8 == col // 4) & (low | high)

    rim_k2 = spread(rim_pair, square(rim_rule)) * 0.125
    ck2[...] = rim_k2
    lane2 = lanes_of((16, LANES))
    packed2 = jnp.zeros((16, LANES), F32)
    for x in range(16):
        k = k2[x]
        up, down = z_sides(k, rim_k2, x, lane2, 64)
        k_sum = (
            kp2[rows_of(x, 0, 24, 16)] + kp2[rows_of(x + 2, 0, 24, 16)]
            + kp2[rows_of(x + 1, -1, 24, 16)] + kp2[rows_of(x + 1, 1, 24, 16)] + up + down
        )
        h = WEIGHT / (s2[x] + 3.0 * k + 0.5 * k_sum)
        e = h * r2[x]
        scale2[x] = h
        first2[x] = e
        packed2 = jnp.where(lane2 // 4 == x, turn(e, 4 * x + 2, 1), packed2)
    sides2[0] = first2[15]
    sides2[1] = first2[0]
    sides2[2] = first2[:, 15, :]
    sides2[3] = first2[:, 0, :]

    even8, odd8 = pl.ds(0, 8, stride=2), pl.ds(1, 8, stride=2)

    def level_three(field, part, weight):
        halves = field.reshape(8, 2, 16, LANES)
        small[...] = halves[:, 0] + halves[:, 1]
        summed = small[:, even8, :] + small[:, odd8, :]
        rule = square(lambda row, col: (row < 64) & (row // 2 == col - 32 * part))
        return spread(flat(summed), rule) * weight

    three = level_three(r2, 0, 0.5) + level_three(k2, 1, 0.125) + level_three(s2, 2, 0.5)
    whole[...] = three
    cubes = three.reshape(2, 4, 8, LANES)
    small[0:2, 0:8] = cubes[:, 0] + cubes[:, 1] + cubes[:, 2] + cubes[:, 3]
    quads = [small[0:2, pl.ds(j, 2, stride=4), :] for j in range(4)]
    quad = quads[0] + quads[1] + quads[2] + quads[3]
    small[2, 0:8] = jnp.zeros((8, LANES), F32)
    small[2, 0:2] = quad[0]
    small[2, 2:4] = quad[1]
    five = spread(small[2, 0:8], square(lambda row, col: (row < 96) & (row // 4 == col - 64)))
    lane8 = lanes_of((8, LANES))
    five = five * jnp.where((lane8 >= 72) & (lane8 < 80), 1.0 / 64.0, 0.25)
    for out, start, tag in ((zp, 16, 1), (zm, 0, 2)):
        half = spread(
            three,
            square(
                lambda row, col, start=start: (col < 48)
                & (row == 32 * (col // 16) + start + col % 16)
            ),
        )
        face = spread(packed, square(lambda row, col, tag=tag: row == 4 * (col - 96) + tag))
        out[0:Z_SMALL] = half[0:32] + turn(half[32:64], 48, 1) + face
        face2 = spread(
            packed2, square(lambda row, col, tag=tag: (col < 16) & (row == 4 * col + tag))
        )
        out[Z_SMALL:Z_ROWS] = face2[0:8] + turn(face2[8:16], 16, 1) + five


def second(k_ref, f_ref, x, rows, k_rim, f_rim, lane, period, h):
    inside, pitch = pl.ds(8, rows), rows + 8
    k, e = k_ref[rows_of(x + 1, 0, pitch, rows)], f_ref[x + 1, inside]
    k_up, k_down = z_sides(k, k_rim, x, lane, period)
    e_up, e_down = z_sides(e, f_rim, x, lane, period)
    around = [
        (k_ref[rows_of(x, 0, pitch, rows)], f_ref[x, inside]),
        (k_ref[rows_of(x + 2, 0, pitch, rows)], f_ref[x + 2, inside]),
        (k_ref[rows_of(x + 1, -1, pitch, rows)], f_ref[x + 1, pl.ds(7, rows)]),
        (k_ref[rows_of(x + 1, 1, pitch, rows)], f_ref[x + 1, pl.ds(9, rows)]),
        (k_up, e_up),
        (k_down, e_down),
    ]
    total = k * sum(en for _, en in around) + sum(kn * en for kn, en in around)
    return 1.2 * e + 0.5 * h * total


def window_kernel(
    zlo, zhi, zp, whole, sides, sides2, kp2, ck2, scale2, first2,
    own, xp, xm, ye, cf, base2, edge2, blocks, small, fp2,
):
    lane = lanes_of((64, LANES))
    a_half, c_half = zlo[0:Z_SMALL], zhi[0:Z_SMALL]
    a = jnp.concatenate([a_half, turn(a_half, -48, 1)], 0)
    b = whole[...]
    c = jnp.concatenate([c_half, turn(c_half, -48, 1)], 0)

    def window(part):
        low = turn(a, BASE - 16 - 16 * part, 1)
        mid = turn(b, BASE - 32 * part, 1)
        high = turn(c, BASE + 32 - 16 * part, 1)
        value = jnp.where((lane < BASE) | (lane >= 112 + BASE), low, mid)
        value = jnp.where((lane >= BASE + 32) & (lane < BASE + 48), high, value)
        return jnp.where((lane >= BASE + 48) & (lane < 112 + BASE), 0.0, value)

    r, k, s = window(0), window(1), window(2)
    own[0], own[1], own[2] = r, k, s

    even, odd = pl.ds(0, 4, stride=2), pl.ds(1, 4, stride=2)

    def shrink(field, part, weight):
        halves = field.reshape(4, 2, 8, LANES)
        small[0:4] = halves[:, 0] + halves[:, 1]
        summed = small[0:4, even, :] + small[0:4, odd, :]
        for i in range(4):
            small[4 + i // 2, 4 * (i % 2) : 4 * (i % 2) + 4] = summed[i]

        def rule(row, col):
            cell = (row + 16 - BASE) % LANES
            return (cell < 64) & (cell // 2 == col - 32 * part)

        return spread(flat(small[4:6]), square(rule)) * weight

    four = shrink(r, 0, 0.5) + shrink(k, 1, 0.125) + shrink(s, 2, 0.5)
    lane8 = lanes_of((8, LANES))
    triple = jnp.zeros((8, LANES), F32)
    for n, ref in enumerate((zlo, zp, zhi)):
        for f in range(3):
            start = 24 * f + 8 * n
            moved = turn(ref[Z_SMALL:Z_ROWS], start - 64 - 8 * f, 1)
            triple = jnp.where((lane8 >= start) & (lane8 < start + 8), moved, triple)
    for q in range(16):
        blocks[q, 0:16] = four
        blocks[q, 16:24] = triple
    main = jnp.where(lane < 42, r, jnp.where(lane < 86, turn(k, 43, 1), turn(s, 86, 1)))
    low = jnp.where(lane == 127, r, jnp.where(lane == 126, k, turn(s, -2, 1)))
    high = jnp.where(lane == 42, r, jnp.where(lane == 43, k, turn(s, 2, 1)))
    ends = jnp.where(lane >= 64, low, turn(high, 86, 1))
    small[...] = ends.reshape(8, 8, LANES)
    ye[0] = small[:, 7, :]
    ye[1] = small[:, 0, :]
    for side, out, i in ((0, xp, 7), (1, xm, 0)):
        out[0:X_FACE] = main
        out[X_FACE:X_SEC] = sides[side]
        out[X_SEC:X_ENDS] = jnp.where(lane8 < 64, sides2[side, 0:8], sides2[side, 8:16])
        out[X_ENDS:X_ROWS] = ends[8 * i : 8 * i + 8]

    def rim(low, high, ready):
        below = spread(low, square(lambda row, col: ready(row) & (col == 4 * (row % 32) + 1)))
        above = spread(high, square(lambda row, col: ready(row) & (col == 4 * (row % 32) + 2)))
        return below + above

    cf[...] = rim(a_half, c_half, lambda row: row >= 96)

    def unfold(half):
        return jnp.concatenate([half, turn(half, -16, 1)], 0)

    rim_f2 = rim(unfold(zlo[Z_SMALL:Z_ROWS]), unfold(zhi[Z_SMALL:Z_ROWS]), lambda row: row < 16)
    rim_k2 = ck2[...]
    lane2 = lanes_of((16, LANES))
    inner2 = pl.ds(8, 16)
    fp2[1:17, inner2] = first2[...]
    for x in (0, 17):
        fp2[x, inner2] = jnp.zeros((16, LANES), F32)
    fp2[:, 0:8] = jnp.zeros((18, 8, LANES), F32)
    fp2[:, 24:32] = jnp.zeros((18, 8, LANES), F32)
    for x in range(16):
        base2[x] = second(kp2, fp2, x, 16, rim_k2, rim_f2, lane2, 64, scale2[x])
    for n, (x, step) in enumerate(((0, -1), (15, 1))):
        k = kp2[rows_of(x + 1, 0, 24, 16)] + kp2[rows_of(x + 1 + step, 0, 24, 16)]
        edge2[n] = 0.5 * scale2[x] * k
    for n, (y, step) in enumerate(((0, -1), (15, 1))):
        k = kp2[pl.ds(32 + y, 16, stride=24), :] + kp2[pl.ds(32 + y + step, 16, stride=24), :]
        edge2[2 + n] = 0.5 * scale2[:, y, :] * k


def columns_kernel(xlo, xhi, xp, sides, sides2, ye, after, yp, ym):
    lane8 = lanes_of((8, LANES))
    for side, out in ((0, yp), (1, ym)):
        out[0:64] = xlo[0:64]
        out[64:128] = xp[0:64]
        out[128:192] = xhi[0:64]
        out[Y_FACE:Y_SEC] = sides[2 + side]
        face = sides2.at[2 + side]
        out[Y_SEC:Y_ENDS] = jnp.where(lane8 < 64, face[0:8], face[8:16])
        out[Y_ENDS:Y_ROWS] = ye[side]


def wrapped(value):
    last = value.shape[0] - 1
    return [
        jnp.concatenate([value[1:], value[:1]], 0),
        jnp.concatenate([value[last:], value[:last]], 0),
        turn(value, -1, 1),
        turn(value, 1, 1),
        turn(value, -1, 2),
        turn(value, 1, 2),
    ]


def periodic_setup(r, k, s, coefs):
    near = wrapped(k)
    diagonal = s + 3.0 * k + 0.5 * sum(near)
    h = WEIGHT / diagonal
    half = 0.5 * h
    for n in range(6):
        coefs[n] = half * (k + near[n])
    start = h * r
    coefs[6] = start
    return start


def periodic_sweep(e, coefs):
    total = 0.2 * e + coefs[6]
    for n, other in enumerate(wrapped(e)):
        total = total + coefs[n] * other
    return total


def ring_kernel(blocks, ring):
    for q in range(16):
        for i in range(2):
            row = 8 * (2 * (q // 4) + i) + 2 * (q % 4)
            ring[row : row + 2] = blocks[q, 16 + 2 * i : 18 + 2 * i]


def four_kernel(place, blocks, four_out, l4, c4, w4):
    gx, gy = place[0], place[1]
    for q in range(16):
        for i in range(4):
            l4[4 * (q // 4) + i, 4 * (q % 4) : 4 * (q % 4) + 4] = blocks[q, 4 * i : 4 * i + 4]
    r4 = l4[...]
    e4 = periodic_setup(r4, turn(r4, 96, 2), turn(r4, 64, 2), c4)
    e4 = lax.fori_loop(0, COARSE_SWEEPS - 1, lambda _, e: periodic_sweep(e, c4), e4)
    l4[...] = e4
    for i in range(4):
        w4[4 * i : 4 * i + 4] = l4[4 * gx + i, pl.ds(4 * gy, 4)]
    lane16 = lanes_of((16, LANES))
    four = jnp.where((lane16 >= 8) & (lane16 < 24), w4[...], 0.0)
    four_out[...] = spread(four, square(lambda row, col: row == 8 + col // 8))


def five_kernel(place, ring, low, high, five_out, l5, l6, c5, c6, c7, w4):
    gx, gy = place[0], place[1]
    lane = lanes_of((64, LANES))

    def field(f):
        mid = turn(ring[...], -8 - 24 * f, 1)
        up = turn(high[...], 16 - 24 * f, 1)
        down = turn(low[...], 32 - 24 * f, 1)
        value = jnp.where(lane < 16, mid, jnp.where(lane < 40, up, down))
        value = jnp.where((lane >= 56) & (lane < 64), turn(mid, 64, 1), value)
        value = jnp.where(lane < 64, value, turn(value, 64, 1))
        return value.reshape(8, 8, LANES)

    to_six = square(lambda row, col: (row < 64) & (row // 2 == col % 32))
    mean = square(lambda row, col: row < 32)

    def level_six(values, weight):
        pairs = values.reshape(4, 2, 8, LANES)
        l6[...] = pairs[:, 0] + pairs[:, 1]
        summed = l6[:, pl.ds(0, 4, stride=2), :] + l6[:, pl.ds(1, 4, stride=2), :]
        l6[:, 0:4] = summed
        l6[:, 4:8] = summed
        return (spread(flat(l6[...]), to_six) * weight).reshape(4, 8, LANES)

    def level_seven(values):
        return (spread(flat(values), mean) * (1.0 / 32.0)).reshape(4, 8, LANES)

    fields5 = [field(f) for f in range(3)]
    fields6 = [level_six(v, w) for v, w in zip(fields5, (0.5, 0.125, 0.5))]
    e5 = periodic_setup(*fields5, c5)
    e6 = periodic_setup(*fields6, c6)
    e7 = periodic_setup(*[level_seven(v) for v in fields6], c7)

    def sweep(_, carry):
        b, c, d = carry
        return periodic_sweep(b, c5), periodic_sweep(c, c6), periodic_sweep(d, c7)

    e5, e6, e7 = lax.fori_loop(0, COARSE_SWEEPS - 1, sweep, (e5, e6, e7))
    l6[...] = e6 + e7
    six = l6[gx, pl.ds(gy, 1)] + jnp.zeros((8, LANES), F32)
    six = spread(six, square(lambda row, col: row == col // 32))
    l5[...] = e5
    w4[...] = jnp.zeros((16, LANES), F32)
    w4[0:2] = l5[2 * gx, pl.ds(2 * gy, 2)]
    w4[2:4] = l5[2 * gx + 1, pl.ds(2 * gy, 2)]
    five = six + spread(w4[0:8], square(lambda row, col: row == col // 16))
    for i in range(4):
        for j in range(2):
            row = 2 * (i // 2) + j
            five_out[4 * i + 2 * j : 4 * i + 2 * j + 2] = jnp.broadcast_to(
                five[row : row + 1], (2, LANES)
            )


def fine_kernel(
    kp, ck, scale, first, cf, base, edge, fp
):
    inner = pl.ds(8, 32)
    lane32 = lanes_of((32, LANES))
    for x in (0, 33):
        fp[x, inner] = jnp.zeros((32, LANES), F32)
    blank = jnp.zeros((8, LANES), F32)

    def fill(x, carry):
        fp[x + 1, inner] = first[x]
        fp[x + 1, 0:8] = blank
        fp[x + 1, 40:48] = blank
        return carry

    lax.fori_loop(0, 32, fill, 0, unroll=4)
    rim_k, rim_f = ck[...], cf[...]

    def slab(x, carry):
        base[x] = second(kp, fp, x, 32, rim_k, rim_f, lane32, LANES, scale[x])
        return carry

    lax.fori_loop(0, 32, slab, 0, unroll=4)
    for n, (x, step) in enumerate(((0, -1), (31, 1))):
        k = kp[rows_of(x + 1, 0, 40, 32)] + kp[rows_of(x + 1 + step, 0, 40, 32)]
        edge[n] = 0.5 * scale[x] * k
    for n, (y, step) in enumerate(((0, -1), (31, 1))):
        k = kp[pl.ds(48 + y, 32, stride=40), :] + kp[pl.ds(48 + y + step, 32, stride=40), :]
        edge[2 + n] = 0.5 * scale[:, y, :] * k


def three_kernel(own, xlo, xhi, ylo, yhi, three_out, r3, s3, k3, c3, ea, eb):
    lane8 = lanes_of((8, LANES))
    for ix in range(3):
        for iy, y_ref in enumerate((ylo, None, yhi)):
            for i in range(8):
                if ix == 1 and iy == 1:
                    r, k, s = [own[f, 8 * i : 8 * i + 8] for f in range(3)]
                else:
                    if iy == 1:
                        r = (xlo if ix == 0 else xhi)[8 * i : 8 * i + 8]
                    else:
                        r = y_ref[64 * ix + 8 * i : 64 * ix + 8 * i + 8]
                    k = turn(r, -43, 1)
                    s = turn(r, -86, 1)
                    if iy == 1 and ((ix == 0 and i == 7) or (ix == 2 and i == 0)):
                        low = (xlo if ix == 0 else xhi)[X_ENDS:X_ROWS]
                        high = turn(low, 42, 1)
                        r = jnp.where(lane8 == 127, low, jnp.where(lane8 == 42, high, r))
                        k = jnp.where(lane8 == 126, low, jnp.where(lane8 == 43, high, k))
                        low, high = turn(low, 2, 1), turn(high, -2, 1)
                        s = jnp.where(lane8 == 127, low, jnp.where(lane8 == 42, high, s))
                x, y = 8 * ix + i, 8 * iy
                r3[x, y : y + 8] = r
                k3[x, y + 8 : y + 16] = k
                s3[x, y : y + 8] = s
    lane1 = lanes_of((1, LANES))
    for y, y_ref in ((7, ylo), (16, yhi)):
        low = y_ref[Y_ENDS:Y_ROWS]
        high = turn(low, 42, 1)
        low_s, high_s = turn(low, 2, 1), turn(high, -2, 1)
        for i in range(8):
            row = slice(i, i + 1)

            def patch(ref, at, below, above, low_lane, high_lane):
                kept = jnp.where(lane1 == high_lane, above[row], ref[8 + i, at : at + 1])
                ref[8 + i, at : at + 1] = jnp.where(lane1 == low_lane, below[row], kept)

            patch(r3, y, low, high, 127, 42)
            patch(k3, y + 8, low, high, 126, 43)
            patch(s3, y, low_s, high_s, 127, 42)
    rim = jnp.zeros((24, 8, LANES), F32)
    for ref in (k3, ea, eb):
        ref[:, 0:8] = rim
        ref[:, 32:40] = rim
    mid = pl.ds(8, 24)

    def setup3(x, carry):
        k = k3[x, mid]
        near = [
            k3[x + 1, mid], k3[x - 1, mid], k3[x, pl.ds(9, 24)], k3[x, pl.ds(7, 24)],
            turn(k, -1, 1), turn(k, 1, 1),
        ]
        h = WEIGHT / (s3[x] + 3.0 * k + 0.5 * sum(near))
        half = 0.5 * h
        for n in range(6):
            c3[n, x] = half * (k + near[n])
        g = h * r3[x]
        c3[6, x] = g
        ea[x, mid] = g
        return carry

    lax.fori_loop(1, 23, setup3, 0, unroll=True)
    source, target = ea, eb
    for step in range(2, COARSE_SWEEPS + 1):

        def sweep3(x, carry, source=source, target=target):
            e = source[x, mid]
            near = [
                source[x + 1, mid], source[x - 1, mid],
                source[x, pl.ds(9, 24)], source[x, pl.ds(7, 24)],
                turn(e, -1, 1), turn(e, 1, 1),
            ]
            total = 0.2 * e + c3[6, x]
            for n in range(6):
                total = total + c3[n, x] * near[n]
            target[x, mid] = total
            return carry

        lax.fori_loop(step, 24 - step, sweep3, 0, unroll=True)
        source, target = target, source

    mine = source[8:16, 16:24]
    lane3 = lanes_of((8, 8, LANES))
    three = flat(jnp.where((lane3 >= BASE) & (lane3 < BASE + 32), mine, 0.0))
    three_out[...] = spread(three, square(lambda row, col: row == BASE + col // 4))


def finish_kernel(
    initial_far, three_in, four_in, five_in, xlo, xhi, ylo, yhi, base, base2, edge, edge2,
    out_far,
    w3, w2, w32, up, out, initial, sems,
):
    inputs = fetch(((initial_far, initial),), sems)
    lane8 = lanes_of((8, LANES))
    four = four_in[...] + five_in[...]
    for i in range(8):
        block = four[4 * (i // 2) : 4 * (i // 2) + 4]
        w3[i, pl.ds(0, 4, stride=2), :] = block
        w3[i, pl.ds(1, 4, stride=2), :] = block
    three = three_in[...] + flat(w3[...])

    def beyond(ref, start):
        half = ref[start : start + 8]
        other = turn(half, 64, 1)
        return jnp.concatenate(
            [jnp.where(lane8 < 64, half, other), jnp.where(lane8 < 64, other, half)], 0
        )

    w2[...] = base2[...]
    for n, (x, ref) in enumerate(((0, xlo), (15, xhi))):
        w2[x] = w2[x] + edge2[n] * beyond(ref, X_SEC)
    for n, (y, ref) in enumerate(((0, ylo), (15, yhi))):
        w2[:, y, :] = w2[:, y, :] + edge2[2 + n] * beyond(ref, Y_SEC)
    two = spread(flat(w2[...]), square(lambda row, col: row == col // 2))
    even8, odd8 = pl.ds(0, 8, stride=2), pl.ds(1, 8, stride=2)
    for i in range(16):
        block = three[8 * (i // 2) : 8 * (i // 2) + 8]
        w32[i, even8, :] = block
        w32[i, odd8, :] = block
    two = two.reshape(16, 16, LANES) + w32[...]
    up[:, pl.ds(0, 16, stride=2), :] = two
    up[:, pl.ds(1, 16, stride=2), :] = two

    depth = 32 // CHUNKS
    copies = []
    for c in range(CHUNKS):
        part = pl.ds(c * depth, depth)
        inputs[c].wait()
        for x in range(c * depth, (c + 1) * depth):
            total = initial[x] + (base[x] + up[x // 2])
            if x in (0, 31):
                face = (xhi if x else xlo)[X_FACE:X_SEC]
                total = total + edge[1 if x else 0] * face
            out[x] = total
        for n, (y, ref) in enumerate(((0, ylo), (31, yhi))):
            face = ref[pl.ds(Y_FACE + c * depth, depth)]
            out[part, y, :] = out[part, y, :] + edge[2 + n, part] * face
        copy = pltpu.make_async_copy(out.at[part], out_far.at[part], sems.at[1, c])
        copy.start()
        copies.append(copy)
    for copy in copies:
        copy.wait()


VM = pl.BlockSpec(memory_space=pltpu.VMEM)
SM = pl.BlockSpec(memory_space=pltpu.SMEM)
FAR = pl.BlockSpec(memory_space=pltpu.HBM)


def shape(*dims):
    return pltpu.VMEM(dims, F32)


def local(kernel, outs, ins, scratch, name, sems=None, out_spec=VM):
    scratch = [pltpu.VMEM(dims, F32) for dims in scratch]
    if sems is not None:
        scratch.append(pltpu.SemaphoreType.DMA(sems))
    return pl.pallas_call(
        kernel,
        out_shape=outs,
        in_specs=ins,
        out_specs=[out_spec] * len(outs),
        scratch_shapes=scratch,
        compiler_params=pltpu.CompilerParams(vmem_limit_bytes=24 * 1024 * 1024),
        name=name,
    )


def on_device(initial, rhs, kappa, sigma):
    place = jnp.stack([lax.axis_index(axis) for axis in ("gx", "gy", "gz")]).astype(jnp.int32)

    def passed(value, axis, step):
        count = lax.axis_size(axis)
        return lax.ppermute(value, axis, [(i, (i + step) % count) for i in range(count)])

    block = (32, 32, LANES)
    block2 = (16, 16, LANES)
    edge = shape(3, 32, LANES)
    far = [
        pltpu.with_memory_space_constraint(value, pltpu.HBM)
        for value in (kappa, initial, rhs, sigma)
    ]
    xp, xm, yp, ym, zs, kappa, initial = local(
        faces_kernel,
        [edge, edge, edge, edge, shape(2, 32, LANES)] + [shape(*block)] * 2,
        [FAR] * 2, [], "faces", sems=(2, CHUNKS),
    )(*far[:2])
    rhs, sigma = local(
        load_kernel, [shape(*block)] * 2, [FAR, FAR, VM], [], "load", sems=(2, CHUNKS)
    )(*far[2:], zs)
    zlo, zhi = passed(zs, "gz", 1), passed(zs, "gz", -1)
    xlo, xhi = passed(xp, "gx", 1), passed(xm, "gx", -1)
    ylo, yhi = passed(yp, "gy", 1), passed(ym, "gy", -1)
    kp, ck, scale, first, zp, zm, whole, sides, kp2, ck2, scale2, first2, sides2 = local(
        residual_kernel,
        [
            shape(1368, LANES), shape(32, LANES), shape(*block), shape(*block),
            shape(Z_ROWS, LANES), shape(Z_ROWS, LANES),
            shape(64, LANES), shape(4, 32, LANES), shape(440, LANES),
            shape(16, LANES), shape(*block2), shape(*block2), shape(4, 16, LANES),
        ],
        [VM] * 10,
        [
            (34, 48, LANES), (16, 32, LANES), (16, 32, LANES), (16, 32, LANES),
            (4, 32, LANES), (8, 16, LANES),
        ],
        "residual",
    )(kappa, initial, rhs, sigma, xlo, xhi, ylo, yhi, zlo, zhi)

    zlo, zhi = passed(zp, "gz", 1), passed(zm, "gz", -1)
    own, xp, xm, ye, cf, base2, edge2, blocks = local(
        window_kernel,
        [
            shape(3, 64, LANES), shape(X_ROWS, LANES), shape(X_ROWS, LANES),
            shape(2, 8, LANES), shape(32, LANES), shape(*block2), shape(4, 16, LANES),
            shape(16, 24, LANES),
        ],
        [VM] * 10, [(8, 8, LANES), (18, 32, LANES)], "window",
    )(zlo, zhi, zp, whole, sides, sides2, kp2, ck2, scale2, first2)
    xlo, xhi = passed(xp, "gx", 1), passed(xm, "gx", -1)
    planes = lax.all_to_all(blocks, ("gx", "gy"), 0, 0)
    base, edge = local(
        fine_kernel,
        [shape(*block), shape(4, 32, LANES)], [VM] * 5, [(34, 48, LANES)], "fine",
    )(kp, ck, scale, first, cf)
    yp, ym = local(
        columns_kernel, [shape(Y_ROWS, LANES)] * 2, [VM] * 7, [], "columns"
    )(xlo, xhi, xp, sides, sides2, ye, edge)
    ylo, yhi = passed(yp, "gy", 1), passed(ym, "gy", -1)
    (ring,) = local(ring_kernel, [shape(64, LANES)], [VM], [], "ring")(planes)
    ring_low, ring_high = passed(ring, "gz", 3), passed(ring, "gz", -3)
    small = shape(16, LANES)
    (four,) = local(
        four_kernel, [small], [SM, VM], [block2, (7,) + block2, (16, LANES)], "four"
    )(place, planes)
    padded3 = (24, 40, LANES)
    block3 = (24, 24, LANES)
    (three,) = local(
        three_kernel, [shape(64, LANES)], [VM] * 5,
        [block3, block3, padded3, (7,) + block3, padded3, padded3], "three",
    )(own, xlo, xhi, ylo, yhi)
    (five,) = local(
        five_kernel, [small], [SM] + [VM] * 3,
        [
            (8, 8, LANES), (4, 8, LANES), (7, 8, 8, LANES), (7, 4, 8, LANES), (7, 4, 8, LANES),
            (16, LANES),
        ],
        "five",
    )(place, ring, ring_low, ring_high)
    return local(
        finish_kernel, [pltpu.HBM(block, F32)], [FAR] + [VM] * 11,
        [(8, 8, LANES), block2, block2, (16, 32, LANES), block, block],
        "finish", sems=(2, CHUNKS), out_spec=FAR,
    )(far[1], three, four, five, xlo, xhi, ylo, yhi, base, base2, edge, edge2)[0]


def solution(mesh):
    spec = P("gx", "gy", "gz")
    return jax.shard_map(
        on_device, mesh=mesh, in_specs=(spec,) * 4, out_specs=spec, check_vma=False
    )
```

```python
import jax
import jax.numpy as jnp
from jax import lax
from jax.experimental import pallas as pl
from jax.experimental.pallas import tpu as pltpu
from jax.sharding import PartitionSpec as P

COARSE_SWEEPS = 8
WEIGHT = 0.8
LANES = 128
F32 = jnp.float32
BF16 = jnp.bfloat16

Z_SMALL, Z_ROWS = 32, 40
X_FACE, X_SEC, X_ENDS, X_ROWS = 64, 96, 104, 112
Y_FACE, Y_SEC, Y_ENDS, Y_ROWS = 192, 224, 232, 240
CHUNKS = 2
BASE = 5


def turn(value, shift, axis):
    size = value.shape[axis]
    if isinstance(shift, int):
        shift = shift % size
        if shift == 0:
            return value
    return pltpu.roll(value, shift, axis)


def lanes_of(shape):
    return lax.broadcasted_iota(jnp.int32, shape, len(shape) - 1)


def square(rule):
    row = lax.broadcasted_iota(jnp.int32, (LANES, LANES), 0)
    col = lax.broadcasted_iota(jnp.int32, (LANES, LANES), 1)
    return jnp.where(rule(row, col), 1.0, 0.0).astype(BF16)


def spread(value, chosen):
    total = None
    for part in range(3):
        piece = value.astype(BF16)
        term = jnp.dot(piece, chosen, preferred_element_type=F32)
        total = term if total is None else total + term
        if part < 2:
            value = value - piece.astype(F32)
    return total


def rows_of(x, shift, pitch, count):
    start = pitch * x + 8
    return pl.ds(start + shift if shift else pl.multiple_of(start, 8), count)


def flat(value):
    return value.reshape(-1, LANES)


def fetch(pairs, sems):
    depth = pairs[0][0].shape[0] // CHUNKS
    copies = []
    for c in range(CHUNKS):
        part = pl.ds(c * depth, depth)
        for n, (far, near) in enumerate(pairs):
            copy = pltpu.make_async_copy(far.at[part], near.at[part], sems.at[n, c])
            copy.start()
            copies.append(copy)
    return copies


def load_kernel(rhs_far, sigma_far, edge, rhs, sigma, sems):
    for copy in fetch(((rhs_far, rhs), (sigma_far, sigma)), sems):
        copy.wait()


def faces_kernel(kappa_far, initial_far, xp, xm, yp, ym, zs, kappa, initial, sems):
    depth = 32 // CHUNKS
    copies = fetch(((kappa_far, kappa), (initial_far, initial)), sems)
    lane = lanes_of((32, LANES))
    first = second = jnp.zeros((32, LANES), F32)

    def body(x, carry):
        first, second = carry
        mine = lane // 4 == x
        shift = 4 * x + 2
        first = jnp.where(mine, turn(kappa[x], shift, 1), first)
        second = jnp.where(mine, turn(initial[x], shift, 1), second)
        return first, second

    for c in range(CHUNKS):
        copies[2 * c].wait()
        copies[2 * c + 1].wait()
        first, second = lax.fori_loop(
            c * depth, (c + 1) * depth, body, (first, second), unroll=True
        )
    zs[0] = first
    zs[1] = second
    xp[0] = kappa[31]
    xp[1] = kappa[30]
    xp[2] = initial[31]
    xm[0] = kappa[0]
    xm[1] = kappa[1]
    xm[2] = initial[0]
    yp[0] = kappa[:, 31, :]
    yp[1] = kappa[:, 30, :]
    yp[2] = initial[:, 31, :]
    ym[0] = kappa[:, 0, :]
    ym[1] = kappa[:, 1, :]
    ym[2] = initial[:, 0, :]


def z_sides(value, rim, x, lane, period):
    near = turn(rim, 126 - 4 * x, 1)
    if period < LANES:
        other = turn(rim, lax.rem(190 - 4 * x, 128), 1)
        near = jnp.where((lane >= 32) & (lane < 96), other, near)
    inside = lane % period
    above = turn(jnp.where(inside == 0, near, value), LANES - 1, 1)
    below = turn(jnp.where(inside == period - 1, near, value), 1, 1)
    return above, below


def residual_kernel(
    kappa, initial, rhs, sigma, xlo, xhi, ylo, yhi, zlo, zhi,
    kp, ck, scale, first, zp, zm, fives, whole, sides_x, sides_y, kp2, ck2, scale2, first2,
    sides2_x, sides2_y, vp, pair_r, pair_k, pair_s, rims, small,
):
    lane = lanes_of((32, LANES))
    inner = pl.ds(8, 32)
    kp[rows_of(0, 0, 40, 32)] = xlo[0]
    kp[rows_of(33, 0, 40, 32)] = xhi[0]
    vp[0, inner] = xlo[2]
    vp[33, inner] = xhi[2]

    def fill(x, carry):
        one = pl.ds(x, 1)
        kp[rows_of(x + 1, 0, 40, 32)] = kappa[x]
        vp[x + 1, inner] = initial[x]
        kp[rows_of(x + 1, -1, 40, 1)] = ylo[0, one]
        kp[rows_of(x + 1, 32, 40, 1)] = yhi[0, one]
        vp[x + 1, 7:8] = ylo[2, one]
        vp[x + 1, 40:41] = yhi[2, one]
        return carry

    lax.fori_loop(0, 32, fill, 0, unroll=4)
    low_half = lane % 4 < 2
    rim_k = jnp.where(low_half, zlo[0], zhi[0])
    rim_v = jnp.where(low_half, zlo[1], zhi[1])
    ck[...] = rim_k

    def slab(x, packed):
        k = kappa[x]
        v = vp[x + 1, inner]
        around = [
            (kp[rows_of(x, 0, 40, 32)], vp[x, inner]),
            (kp[rows_of(x + 2, 0, 40, 32)], vp[x + 2, inner]),
            (kp[rows_of(x + 1, -1, 40, 32)], vp[x + 1, pl.ds(7, 32)]),
            (kp[rows_of(x + 1, 1, 40, 32)], vp[x + 1, pl.ds(9, 32)]),
        ]
        k_up, k_down = z_sides(k, rim_k, x, lane, LANES)
        v_up, v_down = z_sides(v, rim_v, x, lane, LANES)
        around += [(k_up, v_up), (k_down, v_down)]
        k_sum = sum(kn for kn, _ in around)
        v_sum = sum(vn for _, vn in around)
        both = sum(kn * vn for kn, vn in around)
        s = sigma[x]
        diagonal = s + 3.0 * k + 0.5 * k_sum
        r = rhs[x] - diagonal * v + 0.5 * (k * v_sum + both)
        h = WEIGHT / diagonal
        e = h * r
        scale[x] = h
        first[x] = e
        packed = jnp.where(lane // 4 == x, turn(e, 4 * x + 2, 1), packed)
        return r, k, s, packed

    def two(i, packed):
        r0, k0, s0, packed = slab(2 * i, packed)
        r1, k1, s1, packed = slab(2 * i + 1, packed)
        pair_r[i] = r0 + r1
        pair_k[i] = k0 + k1
        pair_s[i] = s0 + s1
        return packed

    packed = lax.fori_loop(0, 16, two, jnp.zeros((32, LANES), F32), unroll=3)
    sides_x[0] = first[31]
    sides_x[1] = first[0]
    sides_y[0] = first[:, 31, :]
    sides_y[1] = first[:, 0, :]

    even, odd = pl.ds(0, 16, stride=2), pl.ds(1, 16, stride=2)
    to_two = square(lambda row, col: row // 2 == col % 64)

    def level_two(ref, weight):
        summed = ref[:, even, :] + ref[:, odd, :]
        return (spread(flat(summed), to_two) * weight).reshape(16, 16, LANES)

    r2 = level_two(pair_r, 0.5)
    k2 = level_two(pair_k, 0.125)
    s2 = level_two(pair_s, 0.5)
    rims[0] = xlo[0] + xlo[1]
    rims[1] = xhi[0] + xhi[1]
    rims[2] = ylo[0] + ylo[1]
    rims[3] = yhi[0] + yhi[1]
    halo = rims[:, even, :] + rims[:, odd, :]
    halo = (spread(flat(halo), to_two) * 0.125).reshape(4, 16, LANES)
    kp2[rows_of(0, 0, 24, 16)] = halo[0]
    kp2[rows_of(17, 0, 24, 16)] = halo[1]
    for x in range(16):
        kp2[rows_of(x + 1, 0, 24, 16)] = k2[x]
        kp2[rows_of(x + 1, -1, 24, 1)] = halo[2, x : x + 1]
        kp2[rows_of(x + 1, 16, 24, 1)] = halo[3, x : x + 1]
    rims[0] = rim_k
    rim_pair = rims[0, even, :] + rims[0, odd, :]

    def rim_rule(row, col):
        low = (col % 4 == 1) & (row % 4 < 2)
        high = (col % 4 == 2) & (row % 4 >= 2)
        return (row // 8 == col // 4) & (low | high)

    rim_k2 = spread(rim_pair, square(rim_rule)) * 0.125
    ck2[...] = rim_k2
    lane2 = lanes_of((16, LANES))
    packed2 = jnp.zeros((16, LANES), F32)
    for x in range(16):
        k = k2[x]
        up, down = z_sides(k, rim_k2, x, lane2, 64)
        k_sum = (
            kp2[rows_of(x, 0, 24, 16)] + kp2[rows_of(x + 2, 0, 24, 16)]
            + kp2[rows_of(x + 1, -1, 24, 16)] + kp2[rows_of(x + 1, 1, 24, 16)] + up + down
        )
        h = WEIGHT / (s2[x] + 3.0 * k + 0.5 * k_sum)
        e = h * r2[x]
        scale2[x] = h
        first2[x] = e
        packed2 = jnp.where(lane2 // 4 == x, turn(e, 4 * x + 2, 1), packed2)
    sides2_x[0] = first2[15]
    sides2_x[1] = first2[0]
    sides2_y[0] = first2[:, 15, :]
    sides2_y[1] = first2[:, 0, :]

    even8, odd8 = pl.ds(0, 8, stride=2), pl.ds(1, 8, stride=2)

    def level_three(field, part, weight):
        halves = field.reshape(8, 2, 16, LANES)
        small[...] = halves[:, 0] + halves[:, 1]
        summed = small[:, even8, :] + small[:, odd8, :]
        rule = square(lambda row, col: (row < 64) & (row // 2 == col - 32 * part))
        return spread(flat(summed), rule) * weight

    three = level_three(r2, 0, 0.5) + level_three(k2, 1, 0.125) + level_three(s2, 2, 0.5)
    whole[...] = three
    cubes = three.reshape(2, 4, 8, LANES)
    small[0:2, 0:8] = cubes[:, 0] + cubes[:, 1] + cubes[:, 2] + cubes[:, 3]
    quads = [small[0:2, pl.ds(j, 2, stride=4), :] for j in range(4)]
    quad = quads[0] + quads[1] + quads[2] + quads[3]
    small[2, 0:8] = jnp.zeros((8, LANES), F32)
    small[2, 0:2] = quad[0]
    small[2, 2:4] = quad[1]
    five = spread(small[2, 0:8], square(lambda row, col: (row < 96) & (row // 4 == col - 64)))
    lane8 = lanes_of((8, LANES))
    five = five * jnp.where((lane8 >= 72) & (lane8 < 80), 1.0 / 64.0, 0.25)
    fives[...] = five
    for out, start, tag in ((zp, 16, 1), (zm, 0, 2)):
        half = spread(
            three,
            square(
                lambda row, col, start=start: (col < 48)
                & (row == 32 * (col // 16) + start + col % 16)
            ),
        )
        face = spread(packed, square(lambda row, col, tag=tag: row == 4 * (col - 96) + tag))
        out[0:Z_SMALL] = half[0:32] + turn(half[32:64], 48, 1) + face
        face2 = spread(
            packed2, square(lambda row, col, tag=tag: (col < 16) & (row == 4 * col + tag))
        )
        out[Z_SMALL:Z_ROWS] = face2[0:8] + turn(face2[8:16], 16, 1) + five


def second(k_ref, f_ref, x, rows, k_rim, f_rim, lane, period, h):
    inside, pitch = pl.ds(8, rows), rows + 8
    k, e = k_ref[rows_of(x + 1, 0, pitch, rows)], f_ref[x + 1, inside]
    k_up, k_down = z_sides(k, k_rim, x, lane, period)
    e_up, e_down = z_sides(e, f_rim, x, lane, period)
    around = [
        (k_ref[rows_of(x, 0, pitch, rows)], f_ref[x, inside]),
        (k_ref[rows_of(x + 2, 0, pitch, rows)], f_ref[x + 2, inside]),
        (k_ref[rows_of(x + 1, -1, pitch, rows)], f_ref[x + 1, pl.ds(7, rows)]),
        (k_ref[rows_of(x + 1, 1, pitch, rows)], f_ref[x + 1, pl.ds(9, rows)]),
        (k_up, e_up),
        (k_down, e_down),
    ]
    total = k * sum(en for _, en in around) + sum(kn * en for kn, en in around)
    return 1.2 * e + 0.5 * h * total


def window_kernel(
    zlo, zhi, fives, whole, sides, sides2,
    own, xp, xm, ye, cf, cf2, blocks, small,
):
    lane = lanes_of((64, LANES))
    a_half, c_half = zlo[0:Z_SMALL], zhi[0:Z_SMALL]
    a = jnp.concatenate([a_half, turn(a_half, -48, 1)], 0)
    b = whole[...]
    c = jnp.concatenate([c_half, turn(c_half, -48, 1)], 0)

    def window(part):
        low = turn(a, BASE - 16 - 16 * part, 1)
        mid = turn(b, BASE - 32 * part, 1)
        high = turn(c, BASE + 32 - 16 * part, 1)
        value = jnp.where((lane < BASE) | (lane >= 112 + BASE), low, mid)
        value = jnp.where((lane >= BASE + 32) & (lane < BASE + 48), high, value)
        return jnp.where((lane >= BASE + 48) & (lane < 112 + BASE), 0.0, value)

    r, k, s = window(0), window(1), window(2)
    own[0], own[1], own[2] = r, k, s

    even, odd = pl.ds(0, 4, stride=2), pl.ds(1, 4, stride=2)

    def shrink(field, part, weight):
        halves = field.reshape(4, 2, 8, LANES)
        small[0:4] = halves[:, 0] + halves[:, 1]
        summed = small[0:4, even, :] + small[0:4, odd, :]
        for i in range(4):
            small[4 + i // 2, 4 * (i % 2) : 4 * (i % 2) + 4] = summed[i]

        def rule(row, col):
            cell = (row + 16 - BASE) % LANES
            return (cell < 64) & (cell // 2 == col - 32 * part)

        return spread(flat(small[4:6]), square(rule)) * weight

    four = shrink(r, 0, 0.5) + shrink(k, 1, 0.125) + shrink(s, 2, 0.5)
    lane8 = lanes_of((8, LANES))
    for n, ref in enumerate((zlo[Z_SMALL:Z_ROWS], fives[...], zhi[Z_SMALL:Z_ROWS])):
        small[4 + n // 2, 4 * (n % 2) : 4 * (n % 2) + 4] = turn(ref, 32, 1)[0:4]
    small[5, 4:8] = jnp.zeros((4, LANES), F32)
    lane4 = lanes_of((16, LANES))
    four = jnp.where((lane4 < 96) | (lane4 >= 120), four, flat(small[4:6]))
    for q in range(16):
        blocks[q] = four
    main = jnp.where(lane < 42, r, jnp.where(lane < 86, turn(k, 43, 1), turn(s, 86, 1)))
    low = jnp.where(lane == 127, r, jnp.where(lane == 126, k, turn(s, -2, 1)))
    high = jnp.where(lane == 42, r, jnp.where(lane == 43, k, turn(s, 2, 1)))
    ends = jnp.where(lane >= 64, low, turn(high, 86, 1))
    small[...] = ends.reshape(8, 8, LANES)
    ye[0] = small[:, 7, :]
    ye[1] = small[:, 0, :]
    for side, out, i in ((0, xp, 7), (1, xm, 0)):
        out[0:X_FACE] = main
        out[X_FACE:X_SEC] = sides[side]
        out[X_SEC:X_ENDS] = jnp.where(lane8 < 64, sides2[side, 0:8], sides2[side, 8:16])
        out[X_ENDS:X_ROWS] = ends[8 * i : 8 * i + 8]

    def rim(low, high, ready):
        below = spread(low, square(lambda row, col: ready(row) & (col == 4 * (row % 32) + 1)))
        above = spread(high, square(lambda row, col: ready(row) & (col == 4 * (row % 32) + 2)))
        return below + above

    cf[...] = rim(a_half, c_half, lambda row: row >= 96)

    def unfold(half):
        return jnp.concatenate([half, turn(half, -16, 1)], 0)

    cf2[...] = rim(unfold(zlo[Z_SMALL:Z_ROWS]), unfold(zhi[Z_SMALL:Z_ROWS]), lambda row: row < 16)


def second_kernel(kp2, ck2, scale2, first2, cf2, base2, edge2, fp2):
    rim_f2 = cf2[...]
    rim_k2 = ck2[...]
    lane2 = lanes_of((16, LANES))
    inner2 = pl.ds(8, 16)
    fp2[1:17, inner2] = first2[...]
    for x in (0, 17):
        fp2[x, inner2] = jnp.zeros((16, LANES), F32)
    fp2[:, 0:8] = jnp.zeros((18, 8, LANES), F32)
    fp2[:, 24:32] = jnp.zeros((18, 8, LANES), F32)
    def slab(x, carry):
        base2[x] = second(kp2, fp2, x, 16, rim_k2, rim_f2, lane2, 64, scale2[x])
        return carry

    lax.fori_loop(0, 16, slab, 0, unroll=8)
    for n, (x, step) in enumerate(((0, -1), (15, 1))):
        k = kp2[rows_of(x + 1, 0, 24, 16)] + kp2[rows_of(x + 1 + step, 0, 24, 16)]
        edge2[n] = 0.5 * scale2[x] * k
    for n, (y, step) in enumerate(((0, -1), (15, 1))):
        k = kp2[pl.ds(32 + y, 16, stride=24), :] + kp2[pl.ds(32 + y + step, 16, stride=24), :]
        edge2[2 + n] = 0.5 * scale2[:, y, :] * k


def columns_kernel(xlo, xhi, xp, sides, sides2, ye, after, after2, yp, ym):
    lane8 = lanes_of((8, LANES))
    for side, out in ((0, yp), (1, ym)):
        out[0:64] = xlo[0:64]
        out[64:128] = xp[0:64]
        out[128:192] = xhi[0:64]
        out[Y_FACE:Y_SEC] = sides[side]
        face = sides2.at[side]
        out[Y_SEC:Y_ENDS] = jnp.where(lane8 < 64, face[0:8], face[8:16])
        out[Y_ENDS:Y_ROWS] = ye[side]


def wrapped(value):
    last = value.shape[0] - 1
    return [
        jnp.concatenate([value[1:], value[:1]], 0),
        jnp.concatenate([value[last:], value[:last]], 0),
        turn(value, -1, 1),
        turn(value, 1, 1),
        turn(value, -1, 2),
        turn(value, 1, 2),
    ]


def periodic_setup(r, k, s, coefs):
    near = wrapped(k)
    diagonal = s + 3.0 * k + 0.5 * sum(near)
    h = WEIGHT / diagonal
    half = 0.5 * h
    for n in range(6):
        coefs[n] = half * (k + near[n])
    start = h * r
    coefs[6] = start
    return start


def periodic_sweep(e, coefs):
    total = 0.2 * e + coefs[6]
    for n, other in enumerate(wrapped(e)):
        total = total + coefs[n] * other
    return total


def ring_kernel(blocks, ring):
    for q in range(16):
        for i in range(2):
            row = 8 * (2 * (q // 4) + i) + 2 * (q % 4)
            for n in range(3):
                source = blocks[q, 4 * n + 2 * i : 4 * n + 2 * i + 2]
                ring[n, row : row + 2] = source


def planes_kernel(
    place, blocks, ring, low, high, four_out, l4, l5, l6, c4, c5, c6, c7, w4
):
    gx, gy = place[0], place[1]
    for q in range(16):
        for i in range(4):
            l4[4 * (q // 4) + i, 4 * (q % 4) : 4 * (q % 4) + 4] = blocks[q, 4 * i : 4 * i + 4]
    lane = lanes_of((8, 8, LANES))

    def field(f):
        value = jnp.zeros((8, 8, LANES), F32)
        for ref, first in ((high, 2), (low, -4), (ring, -1)):
            for n in range(3):
                start = 8 * (first + n) % 64
                moved = turn(ref[n].reshape(8, 8, LANES), start - 96 - 8 * f, 2)
                value = jnp.where(lane // 8 == start // 8, moved, value)
        return jnp.where(lane < 64, value, turn(value, 64, 2))

    to_six = square(lambda row, col: (row < 64) & (row // 2 == col % 32))
    mean = square(lambda row, col: row < 32)

    def level_six(values, weight, n):
        pairs = values.reshape(4, 2, 8, LANES)
        l6[n] = pairs[:, 0] + pairs[:, 1]
        summed = l6[n, :, pl.ds(0, 4, stride=2), :] + l6[n, :, pl.ds(1, 4, stride=2), :]
        l6[n, :, 0:4] = summed
        l6[n, :, 4:8] = summed
        return (spread(flat(l6[n]), to_six) * weight).reshape(4, 8, LANES)

    def level_seven(values):
        return (spread(flat(values), mean) * (1.0 / 32.0)).reshape(4, 8, LANES)

    fields5 = [field(f) for f in range(3)]
    fields6 = [level_six(v, w, n) for n, (v, w) in enumerate(zip(fields5, (0.5, 0.125, 0.5)))]
    fields7 = [level_seven(v) for v in fields6]
    r4 = l4[...]
    e4 = periodic_setup(r4, turn(r4, 96, 2), turn(r4, 64, 2), c4)
    e5 = periodic_setup(*fields5, c5)
    e6 = periodic_setup(*fields6, c6)
    e7 = periodic_setup(*fields7, c7)

    def sweep(_, carry):
        a, b, c, d = carry
        return (
            periodic_sweep(a, c4), periodic_sweep(b, c5), periodic_sweep(c, c6),
            periodic_sweep(d, c7),
        )

    e4, e5, e6, e7 = lax.fori_loop(0, COARSE_SWEEPS - 1, sweep, (e4, e5, e6, e7))
    l6[0] = e6 + e7
    six = l6[0, gx, pl.ds(gy, 1)] + jnp.zeros((8, LANES), F32)
    six = spread(six, square(lambda row, col: row == col // 32))
    l5[...] = e5
    w4[...] = jnp.zeros((16, LANES), F32)
    w4[0:2] = l5[2 * gx, pl.ds(2 * gy, 2)]
    w4[2:4] = l5[2 * gx + 1, pl.ds(2 * gy, 2)]
    five = six + spread(w4[0:8], square(lambda row, col: row == col // 16))
    l4[...] = e4
    for i in range(4):
        w4[4 * i : 4 * i + 4] = l4[4 * gx + i, pl.ds(4 * gy, 4)]
    lane16 = lanes_of((16, LANES))
    four = jnp.where((lane16 >= 8) & (lane16 < 24), w4[...], 0.0)
    four = spread(four, square(lambda row, col: row == 8 + col // 8))
    for i in range(4):
        for j in range(2):
            row = 2 * (i // 2) + j
            w4[4 * i + 2 * j : 4 * i + 2 * j + 2] = jnp.broadcast_to(
                five[row : row + 1], (2, LANES)
            )
    four_out[...] = four + w4[...]


def fine_kernel(
    kp, ck, scale, first, cf, base, edge, fp
):
    inner = pl.ds(8, 32)
    lane32 = lanes_of((32, LANES))
    for x in (0, 33):
        fp[x, inner] = jnp.zeros((32, LANES), F32)
    blank = jnp.zeros((8, LANES), F32)

    def fill(x, carry):
        fp[x + 1, inner] = first[x]
        fp[x + 1, 0:8] = blank
        fp[x + 1, 40:48] = blank
        return carry

    lax.fori_loop(0, 32, fill, 0, unroll=4)
    rim_k, rim_f = ck[...], cf[...]

    def slab(x, carry):
        base[x] = second(kp, fp, x, 32, rim_k, rim_f, lane32, LANES, scale[x])
        return carry

    lax.fori_loop(0, 32, slab, 0, unroll=4)
    for n, (x, step) in enumerate(((0, -1), (31, 1))):
        k = kp[rows_of(x + 1, 0, 40, 32)] + kp[rows_of(x + 1 + step, 0, 40, 32)]
        edge[n] = 0.5 * scale[x] * k
    for n, (y, step) in enumerate(((0, -1), (31, 1))):
        k = kp[pl.ds(48 + y, 32, stride=40), :] + kp[pl.ds(48 + y + step, 32, stride=40), :]
        edge[2 + n] = 0.5 * scale[:, y, :] * k


def three_kernel(
    initial_far, own, xlo, xhi, ylo, yhi, base, base2, edge, edge2,
    three_out, two_out, fine_out,
    r3, s3, k3, c3, ea, eb, w2, sems,
):
    inputs = fetch(((initial_far, fine_out),), sems)
    lane8 = lanes_of((8, LANES))
    for ix in range(3):
        for iy, y_ref in enumerate((ylo, None, yhi)):
            for i in range(8):
                if ix == 1 and iy == 1:
                    r, k, s = [own[f, 8 * i : 8 * i + 8] for f in range(3)]
                else:
                    if iy == 1:
                        r = (xlo if ix == 0 else xhi)[8 * i : 8 * i + 8]
                    else:
                        r = y_ref[64 * ix + 8 * i : 64 * ix + 8 * i + 8]
                    k = turn(r, -43, 1)
                    s = turn(r, -86, 1)
                    if iy == 1 and ((ix == 0 and i == 7) or (ix == 2 and i == 0)):
                        low = (xlo if ix == 0 else xhi)[X_ENDS:X_ROWS]
                        high = turn(low, 42, 1)
                        r = jnp.where(lane8 == 127, low, jnp.where(lane8 == 42, high, r))
                        k = jnp.where(lane8 == 126, low, jnp.where(lane8 == 43, high, k))
                        low, high = turn(low, 2, 1), turn(high, -2, 1)
                        s = jnp.where(lane8 == 127, low, jnp.where(lane8 == 42, high, s))
                x, y = 8 * ix + i, 8 * iy
                r3[x, y : y + 8] = r
                k3[x, y + 8 : y + 16] = k
                s3[x, y : y + 8] = s
    lane1 = lanes_of((1, LANES))
    for y, y_ref in ((7, ylo), (16, yhi)):
        low = y_ref[Y_ENDS:Y_ROWS]
        high = turn(low, 42, 1)
        low_s, high_s = turn(low, 2, 1), turn(high, -2, 1)
        for i in range(8):
            row = slice(i, i + 1)

            def patch(ref, at, below, above, low_lane, high_lane):
                kept = jnp.where(lane1 == high_lane, above[row], ref[8 + i, at : at + 1])
                ref[8 + i, at : at + 1] = jnp.where(lane1 == low_lane, below[row], kept)

            patch(r3, y, low, high, 127, 42)
            patch(k3, y + 8, low, high, 126, 43)
            patch(s3, y, low_s, high_s, 127, 42)
    rim = jnp.zeros((24, 8, LANES), F32)
    for ref in (k3, ea, eb):
        ref[:, 0:8] = rim
        ref[:, 32:40] = rim
    mid = pl.ds(8, 24)

    def setup3(x, carry):
        k = k3[x, mid]
        near = [
            k3[x + 1, mid], k3[x - 1, mid], k3[x, pl.ds(9, 24)], k3[x, pl.ds(7, 24)],
            turn(k, -1, 1), turn(k, 1, 1),
        ]
        h = WEIGHT / (s3[x] + 3.0 * k + 0.5 * sum(near))
        half = 0.5 * h
        for n in range(6):
            c3[n, x] = half * (k + near[n])
        g = h * r3[x]
        c3[6, x] = g
        ea[x, mid] = g
        return carry

    lax.fori_loop(1, 23, setup3, 0, unroll=True)
    source, target = ea, eb
    for step in range(2, COARSE_SWEEPS + 1):

        def sweep3(x, carry, source=source, target=target):
            e = source[x, mid]
            near = [
                source[x + 1, mid], source[x - 1, mid],
                source[x, pl.ds(9, 24)], source[x, pl.ds(7, 24)],
                turn(e, -1, 1), turn(e, 1, 1),
            ]
            total = 0.2 * e + c3[6, x]
            for n in range(6):
                total = total + c3[n, x] * near[n]
            target[x, mid] = total
            return carry

        lax.fori_loop(step, 24 - step, sweep3, 0, unroll=True)
        source, target = target, source

    mine = source[8:16, 16:24]
    lane3 = lanes_of((8, 8, LANES))
    three = flat(jnp.where((lane3 >= BASE) & (lane3 < BASE + 32), mine, 0.0))
    three_out[...] = spread(three, square(lambda row, col: row == BASE + col // 4))

    def beyond(ref, start):
        half = ref[start : start + 8]
        other = turn(half, 64, 1)
        return jnp.concatenate(
            [jnp.where(lane8 < 64, half, other), jnp.where(lane8 < 64, other, half)], 0
        )

    w2[...] = base2[...]
    for n, (x, ref) in enumerate(((0, xlo), (15, xhi))):
        w2[x] = w2[x] + edge2[n] * beyond(ref, X_SEC)
    for n, (y, ref) in enumerate(((0, ylo), (15, yhi))):
        w2[:, y, :] = w2[:, y, :] + edge2[2 + n] * beyond(ref, Y_SEC)
    two_out[...] = spread(flat(w2[...]), square(lambda row, col: row == col // 2))

    for copy in inputs:
        copy.wait()

    def add(x, carry):
        fine_out[x] = fine_out[x] + base[x]
        return carry

    lax.fori_loop(0, 32, add, 0, unroll=8)
    for n, (x, ref) in enumerate(((0, xlo), (31, xhi))):
        fine_out[x] = fine_out[x] + edge[n] * ref[X_FACE:X_SEC]
    for n, (y, ref) in enumerate(((0, ylo), (31, yhi))):
        fine_out[:, y, :] = fine_out[:, y, :] + edge[2 + n] * ref[Y_FACE:Y_SEC]


def finish_kernel(
    three_in, two_in, four_in, fine_in, out_far, w3, w32, up, out, sems
):
    four = four_in[...]
    for i in range(8):
        block = four[4 * (i // 2) : 4 * (i // 2) + 4]
        w3[i, pl.ds(0, 4, stride=2), :] = block
        w3[i, pl.ds(1, 4, stride=2), :] = block
    three = three_in[...] + flat(w3[...])

    even8, odd8 = pl.ds(0, 8, stride=2), pl.ds(1, 8, stride=2)
    for i in range(16):
        block = three[8 * (i // 2) : 8 * (i // 2) + 8]
        w32[i, even8, :] = block
        w32[i, odd8, :] = block
    two = two_in[...].reshape(16, 16, LANES) + w32[...]
    up[:, pl.ds(0, 16, stride=2), :] = two
    up[:, pl.ds(1, 16, stride=2), :] = two

    depth = 32 // CHUNKS
    copies = []
    for c in range(CHUNKS):
        part = pl.ds(c * depth, depth)
        for x in range(c * depth, (c + 1) * depth):
            out[x] = fine_in[x] + up[x // 2]
        copy = pltpu.make_async_copy(out.at[part], out_far.at[part], sems.at[c])
        copy.start()
        copies.append(copy)
    for copy in copies:
        copy.wait()


VM = pl.BlockSpec(memory_space=pltpu.VMEM)
SM = pl.BlockSpec(memory_space=pltpu.SMEM)
FAR = pl.BlockSpec(memory_space=pltpu.HBM)


def shape(*dims):
    return pltpu.VMEM(dims, F32)


def local(kernel, outs, ins, scratch, name, sems=None, out_spec=VM):
    scratch = [pltpu.VMEM(dims, F32) for dims in scratch]
    if sems is not None:
        scratch.append(pltpu.SemaphoreType.DMA(sems))
    return pl.pallas_call(
        kernel,
        out_shape=outs,
        in_specs=ins,
        out_specs=[out_spec] * len(outs),
        scratch_shapes=scratch,
        compiler_params=pltpu.CompilerParams(vmem_limit_bytes=24 * 1024 * 1024),
        name=name,
    )


def on_device(initial, rhs, kappa, sigma):
    place = jnp.stack([lax.axis_index(axis) for axis in ("gx", "gy", "gz")]).astype(jnp.int32)

    def passed(value, axis, step):
        count = lax.axis_size(axis)
        return lax.ppermute(value, axis, [(i, (i + step) % count) for i in range(count)])

    block = (32, 32, LANES)
    block2 = (16, 16, LANES)
    edge = shape(3, 32, LANES)
    far = [
        pltpu.with_memory_space_constraint(value, pltpu.HBM)
        for value in (kappa, initial, rhs, sigma)
    ]
    xp, xm, yp, ym, zs, kappa, initial = local(
        faces_kernel,
        [edge, edge, edge, edge, shape(2, 32, LANES)] + [shape(*block)] * 2,
        [FAR] * 2, [], "faces", sems=(2, CHUNKS),
    )(*far[:2])
    rhs, sigma = local(
        load_kernel, [shape(*block)] * 2, [FAR, FAR, VM], [], "load", sems=(2, CHUNKS)
    )(*far[2:], zs)
    zlo, zhi = passed(zs, "gz", 1), passed(zs, "gz", -1)
    xlo, xhi = passed(xp, "gx", 1), passed(xm, "gx", -1)
    ylo, yhi = passed(yp, "gy", 1), passed(ym, "gy", -1)
    (
        kp, ck, scale, first, zp, zm, fives, whole, sides_x, sides_y, kp2, ck2, scale2, first2,
        sides2_x, sides2_y,
    ) = local(
        residual_kernel,
        [
            shape(1368, LANES), shape(32, LANES), shape(*block), shape(*block),
            shape(Z_ROWS, LANES), shape(Z_ROWS, LANES), shape(8, LANES),
            shape(64, LANES), shape(2, 32, LANES), shape(2, 32, LANES), shape(440, LANES),
            shape(16, LANES), shape(*block2), shape(*block2), shape(2, 16, LANES),
            shape(2, 16, LANES),
        ],
        [VM] * 10,
        [
            (34, 48, LANES), (16, 32, LANES), (16, 32, LANES), (16, 32, LANES),
            (4, 32, LANES), (8, 16, LANES),
        ],
        "residual",
    )(kappa, initial, rhs, sigma, xlo, xhi, ylo, yhi, zlo, zhi)

    zlo, zhi = passed(zp, "gz", 1), passed(zm, "gz", -1)
    own, xp, xm, ye, cf, cf2, blocks = local(
        window_kernel,
        [
            shape(3, 64, LANES), shape(X_ROWS, LANES), shape(X_ROWS, LANES),
            shape(2, 8, LANES), shape(32, LANES), shape(16, LANES),
            shape(16, 16, LANES),
        ],
        [VM] * 6, [(8, 8, LANES)], "window",
    )(zlo, zhi, fives, whole, sides_x, sides2_x)
    xlo, xhi = passed(xp, "gx", 1), passed(xm, "gx", -1)
    planes = lax.all_to_all(blocks, ("gx", "gy"), 0, 0)
    base, edge = local(
        fine_kernel,
        [shape(*block), shape(4, 32, LANES)], [VM] * 5, [(34, 48, LANES)], "fine",
    )(kp, ck, scale, first, cf)
    base2, edge2 = local(
        second_kernel, [shape(*block2), shape(4, 16, LANES)], [VM] * 5, [(18, 32, LANES)],
        "second",
    )(kp2, ck2, scale2, first2, cf2)
    yp, ym = local(
        columns_kernel, [shape(Y_ROWS, LANES)] * 2, [VM] * 8, [], "columns"
    )(xlo, xhi, xp, sides_y, sides2_y, ye, edge, edge2)
    ylo, yhi = passed(yp, "gy", 1), passed(ym, "gy", -1)
    (ring,) = local(ring_kernel, [shape(3, 64, LANES)], [VM], [], "ring")(planes)
    ring_low, ring_high = passed(ring, "gz", 3), passed(ring, "gz", -3)
    padded3 = (24, 40, LANES)
    block3 = (24, 24, LANES)
    three, two, fine = local(
        three_kernel, [shape(64, LANES), shape(256, LANES), shape(*block)], [FAR] + [VM] * 9,
        [block3, block3, padded3, (7,) + block3, padded3, padded3, block2], "three",
        sems=(1, CHUNKS),
    )(far[1], own, xlo, xhi, ylo, yhi, base, base2, edge, edge2)
    (four,) = local(
        planes_kernel, [shape(16, LANES)], [SM] + [VM] * 4,
        [
            block2, (8, 8, LANES), (3, 4, 8, LANES), (7,) + block2,
            (7, 8, 8, LANES), (7, 4, 8, LANES), (7, 4, 8, LANES), (16, LANES),
        ],
        "planes",
    )(place, planes, ring, ring_low, ring_high)
    return local(
        finish_kernel, [pltpu.HBM(block, F32)], [VM] * 4,
        [(8, 8, LANES), block2, (16, 32, LANES), block],
        "finish", sems=(CHUNKS,), out_spec=FAR,
    )(three, two, four, fine)[0]


def solution(mesh):
    spec = P("gx", "gy", "gz")
    return jax.shard_map(
        on_device, mesh=mesh, in_specs=(spec,) * 4, out_specs=spec, check_vma=False
    )
```

```python
import jax
import jax.numpy as jnp
from jax import lax
from jax.experimental import pallas as pl
from jax.experimental.pallas import tpu as pltpu
from jax.sharding import PartitionSpec as P

COARSE_SWEEPS = 8
WEIGHT = 0.8
LANES = 128
F32 = jnp.float32
BF16 = jnp.bfloat16

Z_SMALL, Z_ROWS = 32, 40
X_FACE, X_SEC, X_ENDS, X_ROWS = 64, 96, 104, 112
Y_FACE, Y_SEC, Y_ENDS, Y_ROWS = 192, 224, 232, 240
CHUNKS = 2
BASE = 5


def turn(value, shift, axis):
    size = value.shape[axis]
    if isinstance(shift, int):
        shift = shift % size
        if shift == 0:
            return value
    return pltpu.roll(value, shift, axis)


def lanes_of(shape):
    return lax.broadcasted_iota(jnp.int32, shape, len(shape) - 1)


def square(rule):
    row = lax.broadcasted_iota(jnp.int32, (LANES, LANES), 0)
    col = lax.broadcasted_iota(jnp.int32, (LANES, LANES), 1)
    return jnp.where(rule(row, col), 1.0, 0.0).astype(BF16)


def spread(value, chosen):
    total = None
    for part in range(3):
        piece = value.astype(BF16)
        term = jnp.dot(piece, chosen, preferred_element_type=F32)
        total = term if total is None else total + term
        if part < 2:
            value = value - piece.astype(F32)
    return total


def rows_of(x, shift, pitch, count):
    start = pitch * x + 8
    return pl.ds(start + shift if shift else pl.multiple_of(start, 8), count)


def flat(value):
    return value.reshape(-1, LANES)


def fetch(pairs, sems):
    depth = pairs[0][0].shape[0] // CHUNKS
    copies = []
    for c in range(CHUNKS):
        part = pl.ds(c * depth, depth)
        for n, (far, near) in enumerate(pairs):
            copy = pltpu.make_async_copy(far.at[part], near.at[part], sems.at[n, c])
            copy.start()
            copies.append(copy)
    return copies


def faces_kernel(kappa_far, initial_far, xp, xm, yp, ym, zs, kappa, initial, sems):
    depth = 32 // CHUNKS
    copies = fetch(((kappa_far, kappa), (initial_far, initial)), sems)
    lane = lanes_of((32, LANES))
    first = second = jnp.zeros((32, LANES), F32)

    def body(x, carry):
        first, second = carry
        mine = lane // 4 == x
        shift = 4 * x + 2
        first = jnp.where(mine, turn(kappa[x], shift, 1), first)
        second = jnp.where(mine, turn(initial[x], shift, 1), second)
        return first, second

    for c in range(CHUNKS):
        copies[2 * c].wait()
        copies[2 * c + 1].wait()
        first, second = lax.fori_loop(
            c * depth, (c + 1) * depth, body, (first, second), unroll=True
        )
    zs[0] = first
    zs[1] = second
    xp[0] = kappa[31]
    xp[1] = kappa[30]
    xp[2] = initial[31]
    xm[0] = kappa[0]
    xm[1] = kappa[1]
    xm[2] = initial[0]
    yp[0] = kappa[:, 31, :]
    yp[1] = kappa[:, 30, :]
    yp[2] = initial[:, 31, :]
    ym[0] = kappa[:, 0, :]
    ym[1] = kappa[:, 1, :]
    ym[2] = initial[:, 0, :]


def z_sides(value, rim, x, lane, period):
    near = turn(rim, 126 - 4 * x, 1)
    if period < LANES:
        other = turn(rim, lax.rem(190 - 4 * x, 128), 1)
        near = jnp.where((lane >= 32) & (lane < 96), other, near)
    inside = lane % period
    above = turn(jnp.where(inside == 0, near, value), LANES - 1, 1)
    below = turn(jnp.where(inside == period - 1, near, value), 1, 1)
    return above, below


def inside_kernel(
    kappa, initial, rhs, sigma, zlo, zhi, kp, ck, diagonal, rest, pair_k, pair_s, vp
):
    lane = lanes_of((32, LANES))
    inner = pl.ds(8, 32)
    blank, blank8 = jnp.zeros((32, LANES), F32), jnp.zeros((8, LANES), F32)
    for x in (0, 33):
        kp[rows_of(x, 0, 40, 32)] = blank
        vp[x, inner] = blank
    kp[40 * 33 : 40 * 33 + 8] = blank8

    def fill(x, carry):
        kp[rows_of(x + 1, -8, 40, 8)] = blank8
        kp[rows_of(x + 1, 0, 40, 32)] = kappa[x]
        vp[x + 1, inner] = initial[x]
        vp[x + 1, 0:8] = blank8
        vp[x + 1, 40:48] = blank8
        return carry

    lax.fori_loop(0, 32, fill, 0, unroll=4)
    low_half = lane % 4 < 2
    rim_k = jnp.where(low_half, zlo[0], zhi[0])
    rim_v = jnp.where(low_half, zlo[1], zhi[1])
    ck[...] = rim_k

    def slab(x):
        k = kappa[x]
        v = initial[x]
        around = [
            (kp[rows_of(x, 0, 40, 32)], vp[x, inner]),
            (kp[rows_of(x + 2, 0, 40, 32)], vp[x + 2, inner]),
            (kp[rows_of(x + 1, -1, 40, 32)], vp[x + 1, pl.ds(7, 32)]),
            (kp[rows_of(x + 1, 1, 40, 32)], vp[x + 1, pl.ds(9, 32)]),
        ]
        k_up, k_down = z_sides(k, rim_k, x, lane, LANES)
        v_up, v_down = z_sides(v, rim_v, x, lane, LANES)
        around += [(k_up, v_up), (k_down, v_down)]
        k_sum = sum(kn for kn, _ in around)
        v_sum = sum(vn for _, vn in around)
        both = sum(kn * vn for kn, vn in around)
        s = sigma[x]
        d = s + 3.0 * k + 0.5 * k_sum
        diagonal[x] = d
        rest[x] = rhs[x] - d * v + 0.5 * (k * v_sum + both)
        return k, s

    def two(i, carry):
        k0, s0 = slab(2 * i)
        k1, s1 = slab(2 * i + 1)
        pair_k[i] = k0 + k1
        pair_s[i] = s0 + s1
        return carry

    lax.fori_loop(0, 16, two, 0, unroll=3)


def residual_kernel(
    kappa, initial, kp_in, diagonal_in, rest_in, rim, pair_k, pair_s, xlo, xhi, ylo, yhi,
    kp, scale, first, zp, zm, fives, whole, sides_x, sides_y, kp2, ck2, scale2, first2,
    sides2_x, sides2_y, pair_r, rims, small,
):
    lane = lanes_of((32, LANES))
    rim_k = rim[...]
    kp[rows_of(0, 0, 40, 32)] = xlo[0]
    kp[rows_of(33, 0, 40, 32)] = xhi[0]
    kp[pl.ds(47, 32, stride=40), :] = ylo[0]
    kp[pl.ds(80, 32, stride=40), :] = yhi[0]

    def beyond(at, message):
        kn, vn = message[0], message[2]
        scale[at] = scale[at] + 0.5 * kn
        k, v = kappa[at], initial[at]
        first[at] = first[at] + 0.5 * ((k + kn) * vn - kn * v)

    every = slice(None)
    beyond(0, xlo)
    beyond(31, xhi)
    beyond((every, 0, every), ylo)
    beyond((every, 31, every), yhi)

    def slab(x, packed):
        r = first[x]
        h = WEIGHT / scale[x]
        e = h * r
        scale[x] = h
        first[x] = e
        packed = jnp.where(lane // 4 == x, turn(e, 4 * x + 2, 1), packed)
        return r, packed

    def two(i, packed):
        r0, packed = slab(2 * i, packed)
        r1, packed = slab(2 * i + 1, packed)
        pair_r[i] = r0 + r1
        return packed

    packed = lax.fori_loop(0, 16, two, jnp.zeros((32, LANES), F32), unroll=8)
    sides_x[0] = first[31]
    sides_x[1] = first[0]
    sides_y[0] = first[:, 31, :]
    sides_y[1] = first[:, 0, :]

    even, odd = pl.ds(0, 16, stride=2), pl.ds(1, 16, stride=2)
    to_two = square(lambda row, col: row // 2 == col % 64)

    def level_two(ref, weight):
        summed = ref[:, even, :] + ref[:, odd, :]
        return (spread(flat(summed), to_two) * weight).reshape(16, 16, LANES)

    r2 = level_two(pair_r, 0.5)
    k2 = level_two(pair_k, 0.125)
    s2 = level_two(pair_s, 0.5)
    rims[0] = xlo[0] + xlo[1]
    rims[1] = xhi[0] + xhi[1]
    rims[2] = ylo[0] + ylo[1]
    rims[3] = yhi[0] + yhi[1]
    halo = rims[:, even, :] + rims[:, odd, :]
    halo = (spread(flat(halo), to_two) * 0.125).reshape(4, 16, LANES)
    kp2[rows_of(0, 0, 24, 16)] = halo[0]
    kp2[rows_of(17, 0, 24, 16)] = halo[1]
    for x in range(16):
        kp2[rows_of(x + 1, 0, 24, 16)] = k2[x]
        kp2[rows_of(x + 1, -1, 24, 1)] = halo[2, x : x + 1]
        kp2[rows_of(x + 1, 16, 24, 1)] = halo[3, x : x + 1]
    rims[0] = rim_k
    rim_pair = rims[0, even, :] + rims[0, odd, :]

    def rim_rule(row, col):
        low = (col % 4 == 1) & (row % 4 < 2)
        high = (col % 4 == 2) & (row % 4 >= 2)
        return (row // 8 == col // 4) & (low | high)

    rim_k2 = spread(rim_pair, square(rim_rule)) * 0.125
    ck2[...] = rim_k2
    lane2 = lanes_of((16, LANES))
    packed2 = jnp.zeros((16, LANES), F32)
    for x in range(16):
        k = k2[x]
        up, down = z_sides(k, rim_k2, x, lane2, 64)
        k_sum = (
            kp2[rows_of(x, 0, 24, 16)] + kp2[rows_of(x + 2, 0, 24, 16)]
            + kp2[rows_of(x + 1, -1, 24, 16)] + kp2[rows_of(x + 1, 1, 24, 16)] + up + down
        )
        h = WEIGHT / (s2[x] + 3.0 * k + 0.5 * k_sum)
        e = h * r2[x]
        scale2[x] = h
        first2[x] = e
        packed2 = jnp.where(lane2 // 4 == x, turn(e, 4 * x + 2, 1), packed2)
    sides2_x[0] = first2[15]
    sides2_x[1] = first2[0]
    sides2_y[0] = first2[:, 15, :]
    sides2_y[1] = first2[:, 0, :]

    even8, odd8 = pl.ds(0, 8, stride=2), pl.ds(1, 8, stride=2)

    def level_three(field, part, weight):
        halves = field.reshape(8, 2, 16, LANES)
        small[...] = halves[:, 0] + halves[:, 1]
        summed = small[:, even8, :] + small[:, odd8, :]
        rule = square(lambda row, col: (row < 64) & (row // 2 == col - 32 * part))
        return spread(flat(summed), rule) * weight

    three = level_three(r2, 0, 0.5) + level_three(k2, 1, 0.125) + level_three(s2, 2, 0.5)
    whole[...] = three
    cubes = three.reshape(2, 4, 8, LANES)
    small[0:2, 0:8] = cubes[:, 0] + cubes[:, 1] + cubes[:, 2] + cubes[:, 3]
    quads = [small[0:2, pl.ds(j, 2, stride=4), :] for j in range(4)]
    quad = quads[0] + quads[1] + quads[2] + quads[3]
    small[2, 0:8] = jnp.zeros((8, LANES), F32)
    small[2, 0:2] = quad[0]
    small[2, 2:4] = quad[1]
    five = spread(small[2, 0:8], square(lambda row, col: (row < 96) & (row // 4 == col - 64)))
    lane8 = lanes_of((8, LANES))
    five = five * jnp.where((lane8 >= 72) & (lane8 < 80), 1.0 / 64.0, 0.25)
    fives[...] = five
    for out, start, tag in ((zp, 16, 1), (zm, 0, 2)):
        half = spread(
            three,
            square(
                lambda row, col, start=start: (col < 48)
                & (row == 32 * (col // 16) + start + col % 16)
            ),
        )
        face = spread(packed, square(lambda row, col, tag=tag: row == 4 * (col - 96) + tag))
        out[0:Z_SMALL] = half[0:32] + turn(half[32:64], 48, 1) + face
        face2 = spread(
            packed2, square(lambda row, col, tag=tag: (col < 16) & (row == 4 * col + tag))
        )
        out[Z_SMALL:Z_ROWS] = face2[0:8] + turn(face2[8:16], 16, 1) + five


def second(k_ref, f_ref, x, rows, k_rim, f_rim, lane, period, h):
    inside, pitch = pl.ds(8, rows), rows + 8
    k, e = k_ref[rows_of(x + 1, 0, pitch, rows)], f_ref[x + 1, inside]
    k_up, k_down = z_sides(k, k_rim, x, lane, period)
    e_up, e_down = z_sides(e, f_rim, x, lane, period)
    around = [
        (k_ref[rows_of(x, 0, pitch, rows)], f_ref[x, inside]),
        (k_ref[rows_of(x + 2, 0, pitch, rows)], f_ref[x + 2, inside]),
        (k_ref[rows_of(x + 1, -1, pitch, rows)], f_ref[x + 1, pl.ds(7, rows)]),
        (k_ref[rows_of(x + 1, 1, pitch, rows)], f_ref[x + 1, pl.ds(9, rows)]),
        (k_up, e_up),
        (k_down, e_down),
    ]
    total = k * sum(en for _, en in around) + sum(kn * en for kn, en in around)
    return 1.2 * e + 0.5 * h * total


def window_kernel(
    zlo, zhi, fives, whole, sides, sides2,
    own, xp, xm, ye, cf, cf2, blocks, small,
):
    lane = lanes_of((64, LANES))
    a_half, c_half = zlo[0:Z_SMALL], zhi[0:Z_SMALL]
    a = jnp.concatenate([a_half, turn(a_half, -48, 1)], 0)
    b = whole[...]
    c = jnp.concatenate([c_half, turn(c_half, -48, 1)], 0)

    def window(part):
        low = turn(a, BASE - 16 - 16 * part, 1)
        mid = turn(b, BASE - 32 * part, 1)
        high = turn(c, BASE + 32 - 16 * part, 1)
        value = jnp.where((lane < BASE) | (lane >= 112 + BASE), low, mid)
        value = jnp.where((lane >= BASE + 32) & (lane < BASE + 48), high, value)
        return jnp.where((lane >= BASE + 48) & (lane < 112 + BASE), 0.0, value)

    r, k, s = window(0), window(1), window(2)
    own[0], own[1], own[2] = r, k, s

    even, odd = pl.ds(0, 4, stride=2), pl.ds(1, 4, stride=2)

    def shrink(field, part, weight):
        halves = field.reshape(4, 2, 8, LANES)
        small[0:4] = halves[:, 0] + halves[:, 1]
        summed = small[0:4, even, :] + small[0:4, odd, :]
        for i in range(4):
            small[4 + i // 2, 4 * (i % 2) : 4 * (i % 2) + 4] = summed[i]

        def rule(row, col):
            cell = (row + 16 - BASE) % LANES
            return (cell < 64) & (cell // 2 == col - 32 * part)

        return spread(flat(small[4:6]), square(rule)) * weight

    four = shrink(r, 0, 0.5) + shrink(k, 1, 0.125) + shrink(s, 2, 0.5)
    lane8 = lanes_of((8, LANES))
    for n, ref in enumerate((zlo[Z_SMALL:Z_ROWS], fives[...], zhi[Z_SMALL:Z_ROWS])):
        small[4 + n // 2, 4 * (n % 2) : 4 * (n % 2) + 4] = turn(ref, 32, 1)[0:4]
    small[5, 4:8] = jnp.zeros((4, LANES), F32)
    lane4 = lanes_of((16, LANES))
    four = jnp.where((lane4 < 96) | (lane4 >= 120), four, flat(small[4:6]))
    for q in range(16):
        blocks[q] = four
    main = jnp.where(lane < 42, r, jnp.where(lane < 86, turn(k, 43, 1), turn(s, 86, 1)))
    low = jnp.where(lane == 127, r, jnp.where(lane == 126, k, turn(s, -2, 1)))
    high = jnp.where(lane == 42, r, jnp.where(lane == 43, k, turn(s, 2, 1)))
    ends = jnp.where(lane >= 64, low, turn(high, 86, 1))
    small[...] = ends.reshape(8, 8, LANES)
    ye[0] = small[:, 7, :]
    ye[1] = small[:, 0, :]
    for side, out, i in ((0, xp, 7), (1, xm, 0)):
        out[0:X_FACE] = main
        out[X_FACE:X_SEC] = sides[side]
        out[X_SEC:X_ENDS] = jnp.where(lane8 < 64, sides2[side, 0:8], sides2[side, 8:16])
        out[X_ENDS:X_ROWS] = ends[8 * i : 8 * i + 8]

    def rim(low, high, ready):
        below = spread(low, square(lambda row, col: ready(row) & (col == 4 * (row % 32) + 1)))
        above = spread(high, square(lambda row, col: ready(row) & (col == 4 * (row % 32) + 2)))
        return below + above

    cf[...] = rim(a_half, c_half, lambda row: row >= 96)

    def unfold(half):
        return jnp.concatenate([half, turn(half, -16, 1)], 0)

    cf2[...] = rim(unfold(zlo[Z_SMALL:Z_ROWS]), unfold(zhi[Z_SMALL:Z_ROWS]), lambda row: row < 16)


def second_kernel(kp2, ck2, scale2, first2, cf2, base2, edge2, fp2):
    rim_f2 = cf2[...]
    rim_k2 = ck2[...]
    lane2 = lanes_of((16, LANES))
    inner2 = pl.ds(8, 16)
    fp2[1:17, inner2] = first2[...]
    for x in (0, 17):
        fp2[x, inner2] = jnp.zeros((16, LANES), F32)
    fp2[:, 0:8] = jnp.zeros((18, 8, LANES), F32)
    fp2[:, 24:32] = jnp.zeros((18, 8, LANES), F32)
    def slab(x, carry):
        base2[x] = second(kp2, fp2, x, 16, rim_k2, rim_f2, lane2, 64, scale2[x])
        return carry

    lax.fori_loop(0, 16, slab, 0, unroll=8)
    for n, (x, step) in enumerate(((0, -1), (15, 1))):
        k = kp2[rows_of(x + 1, 0, 24, 16)] + kp2[rows_of(x + 1 + step, 0, 24, 16)]
        edge2[n] = 0.5 * scale2[x] * k
    for n, (y, step) in enumerate(((0, -1), (15, 1))):
        k = kp2[pl.ds(32 + y, 16, stride=24), :] + kp2[pl.ds(32 + y + step, 16, stride=24), :]
        edge2[2 + n] = 0.5 * scale2[:, y, :] * k


def columns_kernel(xlo, xhi, xp, sides, sides2, ye, after, after2, yp, ym):
    lane8 = lanes_of((8, LANES))
    for side, out in ((0, yp), (1, ym)):
        out[0:64] = xlo[0:64]
        out[64:128] = xp[0:64]
        out[128:192] = xhi[0:64]
        out[Y_FACE:Y_SEC] = sides[side]
        face = sides2.at[side]
        out[Y_SEC:Y_ENDS] = jnp.where(lane8 < 64, face[0:8], face[8:16])
        out[Y_ENDS:Y_ROWS] = ye[side]


def wrapped(value):
    last = value.shape[0] - 1
    return [
        jnp.concatenate([value[1:], value[:1]], 0),
        jnp.concatenate([value[last:], value[:last]], 0),
        turn(value, -1, 1),
        turn(value, 1, 1),
        turn(value, -1, 2),
        turn(value, 1, 2),
    ]


def periodic_setup(r, k, s, coefs):
    near = wrapped(k)
    diagonal = s + 3.0 * k + 0.5 * sum(near)
    h = WEIGHT / diagonal
    half = 0.5 * h
    for n in range(6):
        coefs[n] = half * (k + near[n])
    start = h * r
    coefs[6] = start
    return start


def periodic_sweep(e, coefs):
    total = 0.2 * e + coefs[6]
    for n, other in enumerate(wrapped(e)):
        total = total + coefs[n] * other
    return total


def ring_kernel(blocks, ring):
    for q in range(16):
        for i in range(2):
            row = 8 * (2 * (q // 4) + i) + 2 * (q % 4)
            for n in range(3):
                source = blocks[q, 4 * n + 2 * i : 4 * n + 2 * i + 2]
                ring[n, row : row + 2] = source


def planes_kernel(
    place, blocks, ring, low, high, four_out, l4, l5, l6, c4, c5, c6, c7, w4
):
    gx, gy = place[0], place[1]
    for q in range(16):
        for i in range(4):
            l4[4 * (q // 4) + i, 4 * (q % 4) : 4 * (q % 4) + 4] = blocks[q, 4 * i : 4 * i + 4]
    lane = lanes_of((8, 8, LANES))

    def field(f):
        value = jnp.zeros((8, 8, LANES), F32)
        for ref, first in ((high, 2), (low, -4), (ring, -1)):
            for n in range(3):
                start = 8 * (first + n) % 64
                moved = turn(ref[n].reshape(8, 8, LANES), start - 96 - 8 * f, 2)
                value = jnp.where(lane // 8 == start // 8, moved, value)
        return jnp.where(lane < 64, value, turn(value, 64, 2))

    to_six = square(lambda row, col: (row < 64) & (row // 2 == col % 32))
    mean = square(lambda row, col: row < 32)

    def level_six(values, weight, n):
        pairs = values.reshape(4, 2, 8, LANES)
        l6[n] = pairs[:, 0] + pairs[:, 1]
        summed = l6[n, :, pl.ds(0, 4, stride=2), :] + l6[n, :, pl.ds(1, 4, stride=2), :]
        l6[n, :, 0:4] = summed
        l6[n, :, 4:8] = summed
        return (spread(flat(l6[n]), to_six) * weight).reshape(4, 8, LANES)

    def level_seven(values):
        return (spread(flat(values), mean) * (1.0 / 32.0)).reshape(4, 8, LANES)

    fields5 = [field(f) for f in range(3)]
    fields6 = [level_six(v, w, n) for n, (v, w) in enumerate(zip(fields5, (0.5, 0.125, 0.5)))]
    fields7 = [level_seven(v) for v in fields6]
    r4 = l4[...]
    e4 = periodic_setup(r4, turn(r4, 96, 2), turn(r4, 64, 2), c4)
    e5 = periodic_setup(*fields5, c5)
    e6 = periodic_setup(*fields6, c6)
    e7 = periodic_setup(*fields7, c7)

    def sweep(_, carry):
        a, b, c, d = carry
        return (
            periodic_sweep(a, c4), periodic_sweep(b, c5), periodic_sweep(c, c6),
            periodic_sweep(d, c7),
        )

    e4, e5, e6, e7 = lax.fori_loop(0, COARSE_SWEEPS - 1, sweep, (e4, e5, e6, e7))
    l6[0] = e6 + e7
    six = l6[0, gx, pl.ds(gy, 1)] + jnp.zeros((8, LANES), F32)
    six = spread(six, square(lambda row, col: row == col // 32))
    l5[...] = e5
    w4[...] = jnp.zeros((16, LANES), F32)
    w4[0:2] = l5[2 * gx, pl.ds(2 * gy, 2)]
    w4[2:4] = l5[2 * gx + 1, pl.ds(2 * gy, 2)]
    five = six + spread(w4[0:8], square(lambda row, col: row == col // 16))
    l4[...] = e4
    for i in range(4):
        w4[4 * i : 4 * i + 4] = l4[4 * gx + i, pl.ds(4 * gy, 4)]
    lane16 = lanes_of((16, LANES))
    four = jnp.where((lane16 >= 8) & (lane16 < 24), w4[...], 0.0)
    four = spread(four, square(lambda row, col: row == 8 + col // 8))
    for i in range(4):
        for j in range(2):
            row = 2 * (i // 2) + j
            w4[4 * i + 2 * j : 4 * i + 2 * j + 2] = jnp.broadcast_to(
                five[row : row + 1], (2, LANES)
            )
    four_out[...] = four + w4[...]


def fine_kernel(
    kp, ck, scale, first, cf, base, edge, fp
):
    inner = pl.ds(8, 32)
    lane32 = lanes_of((32, LANES))
    for x in (0, 33):
        fp[x, inner] = jnp.zeros((32, LANES), F32)
    blank = jnp.zeros((8, LANES), F32)

    def fill(x, carry):
        fp[x + 1, inner] = first[x]
        fp[x + 1, 0:8] = blank
        fp[x + 1, 40:48] = blank
        return carry

    lax.fori_loop(0, 32, fill, 0, unroll=4)
    rim_k, rim_f = ck[...], cf[...]

    def slab(x, carry):
        base[x] = second(kp, fp, x, 32, rim_k, rim_f, lane32, LANES, scale[x])
        return carry

    lax.fori_loop(0, 32, slab, 0, unroll=4)
    for n, (x, step) in enumerate(((0, -1), (31, 1))):
        k = kp[rows_of(x + 1, 0, 40, 32)] + kp[rows_of(x + 1 + step, 0, 40, 32)]
        edge[n] = 0.5 * scale[x] * k
    for n, (y, step) in enumerate(((0, -1), (31, 1))):
        k = kp[pl.ds(48 + y, 32, stride=40), :] + kp[pl.ds(48 + y + step, 32, stride=40), :]
        edge[2 + n] = 0.5 * scale[:, y, :] * k


def three_kernel(
    initial_far, own, xlo, xhi, ylo, yhi, base, base2, edge, edge2,
    three_out, two_out, fine_out,
    r3, s3, k3, c3, ea, eb, w2, sems,
):
    inputs = fetch(((initial_far, fine_out),), sems)
    lane8 = lanes_of((8, LANES))
    for ix in range(3):
        for iy, y_ref in enumerate((ylo, None, yhi)):
            for i in range(8):
                if ix == 1 and iy == 1:
                    r, k, s = [own[f, 8 * i : 8 * i + 8] for f in range(3)]
                else:
                    if iy == 1:
                        r = (xlo if ix == 0 else xhi)[8 * i : 8 * i + 8]
                    else:
                        r = y_ref[64 * ix + 8 * i : 64 * ix + 8 * i + 8]
                    k = turn(r, -43, 1)
                    s = turn(r, -86, 1)
                    if iy == 1 and ((ix == 0 and i == 7) or (ix == 2 and i == 0)):
                        low = (xlo if ix == 0 else xhi)[X_ENDS:X_ROWS]
                        high = turn(low, 42, 1)
                        r = jnp.where(lane8 == 127, low, jnp.where(lane8 == 42, high, r))
                        k = jnp.where(lane8 == 126, low, jnp.where(lane8 == 43, high, k))
                        low, high = turn(low, 2, 1), turn(high, -2, 1)
                        s = jnp.where(lane8 == 127, low, jnp.where(lane8 == 42, high, s))
                x, y = 8 * ix + i, 8 * iy
                r3[x, y : y + 8] = r
                k3[x, y + 8 : y + 16] = k
                s3[x, y : y + 8] = s
    lane1 = lanes_of((1, LANES))
    for y, y_ref in ((7, ylo), (16, yhi)):
        low = y_ref[Y_ENDS:Y_ROWS]
        high = turn(low, 42, 1)
        low_s, high_s = turn(low, 2, 1), turn(high, -2, 1)
        for i in range(8):
            row = slice(i, i + 1)

            def patch(ref, at, below, above, low_lane, high_lane):
                kept = jnp.where(lane1 == high_lane, above[row], ref[8 + i, at : at + 1])
                ref[8 + i, at : at + 1] = jnp.where(lane1 == low_lane, below[row], kept)

            patch(r3, y, low, high, 127, 42)
            patch(k3, y + 8, low, high, 126, 43)
            patch(s3, y, low_s, high_s, 127, 42)
    rim = jnp.zeros((24, 8, LANES), F32)
    for ref in (k3, ea, eb):
        ref[:, 0:8] = rim
        ref[:, 32:40] = rim
    mid = pl.ds(8, 24)

    def setup3(x, carry):
        k = k3[x, mid]
        near = [
            k3[x + 1, mid], k3[x - 1, mid], k3[x, pl.ds(9, 24)], k3[x, pl.ds(7, 24)],
            turn(k, -1, 1), turn(k, 1, 1),
        ]
        h = WEIGHT / (s3[x] + 3.0 * k + 0.5 * sum(near))
        half = 0.5 * h
        for n in range(6):
            c3[n, x] = half * (k + near[n])
        g = h * r3[x]
        c3[6, x] = g
        ea[x, mid] = g
        return carry

    lax.fori_loop(1, 23, setup3, 0, unroll=True)
    source, target = ea, eb
    for step in range(2, COARSE_SWEEPS + 1):

        def sweep3(x, carry, source=source, target=target):
            e = source[x, mid]
            near = [
                source[x + 1, mid], source[x - 1, mid],
                source[x, pl.ds(9, 24)], source[x, pl.ds(7, 24)],
                turn(e, -1, 1), turn(e, 1, 1),
            ]
            total = 0.2 * e + c3[6, x]
            for n in range(6):
                total = total + c3[n, x] * near[n]
            target[x, mid] = total
            return carry

        lax.fori_loop(step, 24 - step, sweep3, 0, unroll=True)
        source, target = target, source

    mine = source[8:16, 16:24]
    lane3 = lanes_of((8, 8, LANES))
    three = flat(jnp.where((lane3 >= BASE) & (lane3 < BASE + 32), mine, 0.0))
    three_out[...] = spread(three, square(lambda row, col: row == BASE + col // 4))

    def beyond(ref, start):
        half = ref[start : start + 8]
        other = turn(half, 64, 1)
        return jnp.concatenate(
            [jnp.where(lane8 < 64, half, other), jnp.where(lane8 < 64, other, half)], 0
        )

    w2[...] = base2[...]
    for n, (x, ref) in enumerate(((0, xlo), (15, xhi))):
        w2[x] = w2[x] + edge2[n] * beyond(ref, X_SEC)
    for n, (y, ref) in enumerate(((0, ylo), (15, yhi))):
        w2[:, y, :] = w2[:, y, :] + edge2[2 + n] * beyond(ref, Y_SEC)
    two_out[...] = spread(flat(w2[...]), square(lambda row, col: row == col // 2))

    for copy in inputs:
        copy.wait()

    def add(x, carry):
        fine_out[x] = fine_out[x] + base[x]
        return carry

    lax.fori_loop(0, 32, add, 0, unroll=8)
    for n, (x, ref) in enumerate(((0, xlo), (31, xhi))):
        fine_out[x] = fine_out[x] + edge[n] * ref[X_FACE:X_SEC]
    for n, (y, ref) in enumerate(((0, ylo), (31, yhi))):
        fine_out[:, y, :] = fine_out[:, y, :] + edge[2 + n] * ref[Y_FACE:Y_SEC]


def finish_kernel(
    three_in, two_in, four_in, fine_in, out_far, w3, w32, up, out, sems
):
    four = four_in[...]
    for i in range(8):
        block = four[4 * (i // 2) : 4 * (i // 2) + 4]
        w3[i, pl.ds(0, 4, stride=2), :] = block
        w3[i, pl.ds(1, 4, stride=2), :] = block
    three = three_in[...] + flat(w3[...])

    even8, odd8 = pl.ds(0, 8, stride=2), pl.ds(1, 8, stride=2)
    for i in range(16):
        block = three[8 * (i // 2) : 8 * (i // 2) + 8]
        w32[i, even8, :] = block
        w32[i, odd8, :] = block
    two = two_in[...].reshape(16, 16, LANES) + w32[...]
    up[:, pl.ds(0, 16, stride=2), :] = two
    up[:, pl.ds(1, 16, stride=2), :] = two

    depth = 32 // CHUNKS
    copies = []
    for c in range(CHUNKS):
        part = pl.ds(c * depth, depth)
        for x in range(c * depth, (c + 1) * depth):
            out[x] = fine_in[x] + up[x // 2]
        copy = pltpu.make_async_copy(out.at[part], out_far.at[part], sems.at[c])
        copy.start()
        copies.append(copy)
    for copy in copies:
        copy.wait()


VM = pl.BlockSpec(memory_space=pltpu.VMEM)
SM = pl.BlockSpec(memory_space=pltpu.SMEM)
FAR = pl.BlockSpec(memory_space=pltpu.HBM)


def shape(*dims):
    return pltpu.VMEM(dims, F32)


def local(kernel, outs, ins, scratch, name, sems=None, out_spec=VM, aliases=None):
    scratch = [pltpu.VMEM(dims, F32) for dims in scratch]
    if sems is not None:
        scratch.append(pltpu.SemaphoreType.DMA(sems))
    return pl.pallas_call(
        kernel,
        out_shape=outs,
        in_specs=ins,
        out_specs=[out_spec] * len(outs),
        scratch_shapes=scratch,
        input_output_aliases=aliases or {},
        compiler_params=pltpu.CompilerParams(vmem_limit_bytes=24 * 1024 * 1024),
        name=name,
    )


def on_device(initial, rhs, kappa, sigma):
    place = jnp.stack([lax.axis_index(axis) for axis in ("gx", "gy", "gz")]).astype(jnp.int32)

    def passed(value, axis, step):
        count = lax.axis_size(axis)
        return lax.ppermute(value, axis, [(i, (i + step) % count) for i in range(count)])

    block = (32, 32, LANES)
    block2 = (16, 16, LANES)
    edge = shape(3, 32, LANES)
    far = [
        pltpu.with_memory_space_constraint(value, pltpu.HBM)
        for value in (kappa, initial)
    ]
    xp, xm, yp, ym, zs, kappa, initial = local(
        faces_kernel,
        [edge, edge, edge, edge, shape(2, 32, LANES)] + [shape(*block)] * 2,
        [FAR] * 2, [], "faces", sems=(2, CHUNKS),
    )(*far)
    zlo, zhi = passed(zs, "gz", 1), passed(zs, "gz", -1)
    xlo, xhi = passed(xp, "gx", 1), passed(xm, "gx", -1)
    ylo, yhi = passed(yp, "gy", 1), passed(ym, "gy", -1)
    kp, ck, diagonal, rest, pair_k, pair_s = local(
        inside_kernel,
        [
            shape(1368, LANES), shape(32, LANES), shape(*block), shape(*block),
            shape(16, 32, LANES), shape(16, 32, LANES),
        ],
        [VM] * 6, [(34, 48, LANES)], "inside",
    )(kappa, initial, rhs, sigma, zlo, zhi)
    (
        kp, scale, first, zp, zm, fives, whole, sides_x, sides_y, kp2, ck2, scale2, first2,
        sides2_x, sides2_y,
    ) = local(
        residual_kernel,
        [
            shape(1368, LANES), shape(*block), shape(*block),
            shape(Z_ROWS, LANES), shape(Z_ROWS, LANES), shape(8, LANES),
            shape(64, LANES), shape(2, 32, LANES), shape(2, 32, LANES), shape(440, LANES),
            shape(16, LANES), shape(*block2), shape(*block2), shape(2, 16, LANES),
            shape(2, 16, LANES),
        ],
        [VM] * 12, [(16, 32, LANES), (4, 32, LANES), (8, 16, LANES)],
        "residual", aliases={2: 0, 3: 1, 4: 2},
    )(
        kappa, initial, kp, diagonal, rest, ck, pair_k, pair_s, xlo, xhi, ylo, yhi
    )

    zlo, zhi = passed(zp, "gz", 1), passed(zm, "gz", -1)
    own, xp, xm, ye, cf, cf2, blocks = local(
        window_kernel,
        [
            shape(3, 64, LANES), shape(X_ROWS, LANES), shape(X_ROWS, LANES),
            shape(2, 8, LANES), shape(32, LANES), shape(16, LANES),
            shape(16, 16, LANES),
        ],
        [VM] * 6, [(8, 8, LANES)], "window",
    )(zlo, zhi, fives, whole, sides_x, sides2_x)
    xlo, xhi = passed(xp, "gx", 1), passed(xm, "gx", -1)
    planes = lax.all_to_all(blocks, ("gx", "gy"), 0, 0)
    base, edge = local(
        fine_kernel,
        [shape(*block), shape(4, 32, LANES)], [VM] * 5, [(34, 48, LANES)], "fine",
    )(kp, ck, scale, first, cf)
    base2, edge2 = local(
        second_kernel, [shape(*block2), shape(4, 16, LANES)], [VM] * 5, [(18, 32, LANES)],
        "second",
    )(kp2, ck2, scale2, first2, cf2)
    yp, ym = local(
        columns_kernel, [shape(Y_ROWS, LANES)] * 2, [VM] * 8, [], "columns"
    )(xlo, xhi, xp, sides_y, sides2_y, ye, edge, edge2)
    ylo, yhi = passed(yp, "gy", 1), passed(ym, "gy", -1)
    (ring,) = local(ring_kernel, [shape(3, 64, LANES)], [VM], [], "ring")(planes)
    ring_low, ring_high = passed(ring, "gz", 3), passed(ring, "gz", -3)
    padded3 = (24, 40, LANES)
    block3 = (24, 24, LANES)
    three, two, fine = local(
        three_kernel, [shape(64, LANES), shape(256, LANES), shape(*block)], [FAR] + [VM] * 9,
        [block3, block3, padded3, (7,) + block3, padded3, padded3, block2], "three",
        sems=(1, CHUNKS),
    )(far[1], own, xlo, xhi, ylo, yhi, base, base2, edge, edge2)
    (four,) = local(
        planes_kernel, [shape(16, LANES)], [SM] + [VM] * 4,
        [
            block2, (8, 8, LANES), (3, 4, 8, LANES), (7,) + block2,
            (7, 8, 8, LANES), (7, 4, 8, LANES), (7, 4, 8, LANES), (16, LANES),
        ],
        "planes",
    )(place, planes, ring, ring_low, ring_high)
    return local(
        finish_kernel, [pltpu.HBM(block, F32)], [VM] * 4,
        [(8, 8, LANES), block2, (16, 32, LANES), block],
        "finish", sems=(CHUNKS,), out_spec=FAR,
    )(three, two, four, fine)[0]


def solution(mesh):
    spec = P("gx", "gy", "gz")
    return jax.shard_map(
        on_device, mesh=mesh, in_specs=(spec,) * 4, out_specs=spec, check_vma=False
    )
```

```python
import jax
import jax.numpy as jnp
from jax import lax
from jax.experimental import pallas as pl
from jax.experimental.pallas import tpu as pltpu
from jax.sharding import PartitionSpec as P

COARSE_SWEEPS = 8
WEIGHT = 0.8
LANES = 128
F32 = jnp.float32
BF16 = jnp.bfloat16

Z_SMALL, Z_ROWS = 32, 40
X_FACE, X_SEC, X_ENDS, X_ROWS = 64, 96, 104, 112
Y_FACE, Y_SEC, Y_ENDS, Y_ROWS = 192, 224, 232, 240
CHUNKS = 2
BASE = 5


def turn(value, shift, axis):
    size = value.shape[axis]
    if isinstance(shift, int):
        shift = shift % size
        if shift == 0:
            return value
    return pltpu.roll(value, shift, axis)


def lanes_of(shape):
    return lax.broadcasted_iota(jnp.int32, shape, len(shape) - 1)


def square(rule):
    row = lax.broadcasted_iota(jnp.int32, (LANES, LANES), 0)
    col = lax.broadcasted_iota(jnp.int32, (LANES, LANES), 1)
    return jnp.where(rule(row, col), 1.0, 0.0).astype(BF16)


def spread(value, chosen):
    total = None
    for part in range(3):
        piece = value.astype(BF16)
        term = jnp.dot(piece, chosen, preferred_element_type=F32)
        total = term if total is None else total + term
        if part < 2:
            value = value - piece.astype(F32)
    return total


def rows_of(x, shift, pitch, count):
    start = pitch * x + 8
    return pl.ds(start + shift if shift else pl.multiple_of(start, 8), count)


def flat(value):
    return value.reshape(-1, LANES)


def fetch(pairs, sems):
    depth = pairs[0][0].shape[0] // CHUNKS
    copies = []
    for c in range(CHUNKS):
        part = pl.ds(c * depth, depth)
        for n, (far, near) in enumerate(pairs):
            copy = pltpu.make_async_copy(far.at[part], near.at[part], sems.at[n, c])
            copy.start()
            copies.append(copy)
    return copies


def faces_kernel(kappa_far, initial_far, xp, xm, yp, ym, zs, kappa, initial, sems):
    depth = 32 // CHUNKS
    copies = fetch(((kappa_far, kappa), (initial_far, initial)), sems)
    lane = lanes_of((32, LANES))
    first = second = jnp.zeros((32, LANES), F32)

    def body(x, carry):
        first, second = carry
        mine = lane // 4 == x
        shift = 4 * x + 2
        first = jnp.where(mine, turn(kappa[x], shift, 1), first)
        second = jnp.where(mine, turn(initial[x], shift, 1), second)
        return first, second

    for c in range(CHUNKS):
        copies[2 * c].wait()
        copies[2 * c + 1].wait()
        first, second = lax.fori_loop(
            c * depth, (c + 1) * depth, body, (first, second), unroll=True
        )
    zs[0] = first
    zs[1] = second
    xp[0] = kappa[31]
    xp[1] = kappa[30]
    xp[2] = initial[31]
    xm[0] = kappa[0]
    xm[1] = kappa[1]
    xm[2] = initial[0]
    yp[0] = kappa[:, 31, :]
    yp[1] = kappa[:, 30, :]
    yp[2] = initial[:, 31, :]
    ym[0] = kappa[:, 0, :]
    ym[1] = kappa[:, 1, :]
    ym[2] = initial[:, 0, :]


def z_sides(value, rim, x, lane, period):
    near = turn(rim, 126 - 4 * x, 1)
    if period < LANES:
        other = turn(rim, lax.rem(190 - 4 * x, 128), 1)
        near = jnp.where((lane >= 32) & (lane < 96), other, near)
    inside = lane % period
    above = turn(jnp.where(inside == 0, near, value), LANES - 1, 1)
    below = turn(jnp.where(inside == period - 1, near, value), 1, 1)
    return above, below


def inside_kernel(
    kappa, initial, rhs, sigma, zlo, zhi, kp, ck, diagonal, rest, pair_k, pair_s, vp
):
    lane = lanes_of((32, LANES))
    inner = pl.ds(8, 32)
    blank, blank8 = jnp.zeros((32, LANES), F32), jnp.zeros((8, LANES), F32)
    for x in (0, 33):
        kp[rows_of(x, 0, 40, 32)] = blank
        vp[x, inner] = blank
    kp[0:8] = blank8
    kp[40 * 33 : 40 * 33 + 8] = blank8
    kp[40 * 34 : 40 * 34 + 8] = blank8

    def fill(x, carry):
        kp[rows_of(x + 1, -8, 40, 8)] = blank8
        kp[rows_of(x + 1, 0, 40, 32)] = kappa[x]
        vp[x + 1, inner] = initial[x]
        vp[x + 1, 0:8] = blank8
        vp[x + 1, 40:48] = blank8
        return carry

    lax.fori_loop(0, 32, fill, 0, unroll=4)
    low_half = lane % 4 < 2
    rim_k = jnp.where(low_half, zlo[0], zhi[0])
    rim_v = jnp.where(low_half, zlo[1], zhi[1])
    ck[...] = rim_k

    def slab(x):
        k = kappa[x]
        v = initial[x]
        around = [
            (kp[rows_of(x, 0, 40, 32)], vp[x, inner]),
            (kp[rows_of(x + 2, 0, 40, 32)], vp[x + 2, inner]),
            (kp[rows_of(x + 1, -1, 40, 32)], vp[x + 1, pl.ds(7, 32)]),
            (kp[rows_of(x + 1, 1, 40, 32)], vp[x + 1, pl.ds(9, 32)]),
        ]
        k_up, k_down = z_sides(k, rim_k, x, lane, LANES)
        v_up, v_down = z_sides(v, rim_v, x, lane, LANES)
        around += [(k_up, v_up), (k_down, v_down)]
        k_sum = sum(kn for kn, _ in around)
        v_sum = sum(vn for _, vn in around)
        both = sum(kn * vn for kn, vn in around)
        s = sigma[x]
        d = s + 3.0 * k + 0.5 * k_sum
        diagonal[x] = d
        rest[x] = rhs[x] - d * v + 0.5 * (k * v_sum + both)
        return k, s

    def two(i, carry):
        k0, s0 = slab(2 * i)
        k1, s1 = slab(2 * i + 1)
        pair_k[i] = k0 + k1
        pair_s[i] = s0 + s1
        return carry

    lax.fori_loop(0, 16, two, 0, unroll=3)


def residual_kernel(
    kappa, initial, diagonal, rest, rim, pair_k, pair_s, xlo, xhi, ylo, yhi,
    scale, first, beside, zp, zm, fives, whole, sides_x, sides_y, kp2, ck2, scale2, first2,
    sides2_x, sides2_y, pair_r, rims, small, fix,
):
    lane = lanes_of((32, LANES))
    row = lax.broadcasted_iota(jnp.int32, (32, LANES), 0)
    rim_k = rim[...]
    for n, message in enumerate((xlo, xhi, ylo, yhi)):
        beside[n] = message[0]

    def beyond(k, v, message):
        kn, vn = message[0], message[2]
        return 0.5 * kn, 0.5 * ((k + kn) * vn - kn * v)

    fix[0], fix[1] = beyond(kappa[:, 0, :], initial[:, 0, :], ylo)
    fix[2], fix[3] = beyond(kappa[:, 31, :], initial[:, 31, :], yhi)

    def slab(x, packed, message=None):
        one = pl.ds(x, 1)
        d, r = diagonal[x], rest[x]
        if message is not None:
            more_d, more_r = beyond(kappa[x], initial[x], message)
            d, r = d + more_d, r + more_r
        d = jnp.where(row == 0, d + fix[0, one], jnp.where(row == 31, d + fix[2, one], d))
        r = jnp.where(row == 0, r + fix[1, one], jnp.where(row == 31, r + fix[3, one], r))
        h = WEIGHT / d
        e = h * r
        scale[x] = h
        first[x] = e
        packed = jnp.where(lane // 4 == x, turn(e, 4 * x + 2, 1), packed)
        return r, packed

    def two(i, packed, low=None, high=None):
        r0, packed = slab(2 * i, packed, low)
        r1, packed = slab(2 * i + 1, packed, high)
        pair_r[i] = r0 + r1
        return packed

    packed = two(0, jnp.zeros((32, LANES), F32), low=xlo)
    packed = lax.fori_loop(1, 15, two, packed, unroll=14)
    packed = two(15, packed, high=xhi)
    sides_x[0] = first[31]
    sides_x[1] = first[0]
    sides_y[0] = first[:, 31, :]
    sides_y[1] = first[:, 0, :]

    even, odd = pl.ds(0, 16, stride=2), pl.ds(1, 16, stride=2)
    to_two = square(lambda row, col: row // 2 == col % 64)

    def level_two(ref, weight):
        summed = ref[:, even, :] + ref[:, odd, :]
        return (spread(flat(summed), to_two) * weight).reshape(16, 16, LANES)

    r2 = level_two(pair_r, 0.5)
    k2 = level_two(pair_k, 0.125)
    s2 = level_two(pair_s, 0.5)
    rims[0] = xlo[0] + xlo[1]
    rims[1] = xhi[0] + xhi[1]
    rims[2] = ylo[0] + ylo[1]
    rims[3] = yhi[0] + yhi[1]
    halo = rims[:, even, :] + rims[:, odd, :]
    halo = (spread(flat(halo), to_two) * 0.125).reshape(4, 16, LANES)
    kp2[rows_of(0, 0, 24, 16)] = halo[0]
    kp2[rows_of(17, 0, 24, 16)] = halo[1]
    for x in range(16):
        kp2[rows_of(x + 1, 0, 24, 16)] = k2[x]
        kp2[rows_of(x + 1, -1, 24, 1)] = halo[2, x : x + 1]
        kp2[rows_of(x + 1, 16, 24, 1)] = halo[3, x : x + 1]
    rims[0] = rim_k
    rim_pair = rims[0, even, :] + rims[0, odd, :]

    def rim_rule(row, col):
        low = (col % 4 == 1) & (row % 4 < 2)
        high = (col % 4 == 2) & (row % 4 >= 2)
        return (row // 8 == col // 4) & (low | high)

    rim_k2 = spread(rim_pair, square(rim_rule)) * 0.125
    ck2[...] = rim_k2
    lane2 = lanes_of((16, LANES))
    packed2 = jnp.zeros((16, LANES), F32)
    for x in range(16):
        k = k2[x]
        up, down = z_sides(k, rim_k2, x, lane2, 64)
        k_sum = (
            kp2[rows_of(x, 0, 24, 16)] + kp2[rows_of(x + 2, 0, 24, 16)]
            + kp2[rows_of(x + 1, -1, 24, 16)] + kp2[rows_of(x + 1, 1, 24, 16)] + up + down
        )
        h = WEIGHT / (s2[x] + 3.0 * k + 0.5 * k_sum)
        e = h * r2[x]
        scale2[x] = h
        first2[x] = e
        packed2 = jnp.where(lane2 // 4 == x, turn(e, 4 * x + 2, 1), packed2)
    sides2_x[0] = first2[15]
    sides2_x[1] = first2[0]
    sides2_y[0] = first2[:, 15, :]
    sides2_y[1] = first2[:, 0, :]

    even8, odd8 = pl.ds(0, 8, stride=2), pl.ds(1, 8, stride=2)

    def level_three(field, part, weight):
        halves = field.reshape(8, 2, 16, LANES)
        small[...] = halves[:, 0] + halves[:, 1]
        summed = small[:, even8, :] + small[:, odd8, :]
        rule = square(lambda row, col: (row < 64) & (row // 2 == col - 32 * part))
        return spread(flat(summed), rule) * weight

    three = level_three(r2, 0, 0.5) + level_three(k2, 1, 0.125) + level_three(s2, 2, 0.5)
    whole[...] = three
    cubes = three.reshape(2, 4, 8, LANES)
    small[0:2, 0:8] = cubes[:, 0] + cubes[:, 1] + cubes[:, 2] + cubes[:, 3]
    quads = [small[0:2, pl.ds(j, 2, stride=4), :] for j in range(4)]
    quad = quads[0] + quads[1] + quads[2] + quads[3]
    small[2, 0:8] = jnp.zeros((8, LANES), F32)
    small[2, 0:2] = quad[0]
    small[2, 2:4] = quad[1]
    five = spread(small[2, 0:8], square(lambda row, col: (row < 96) & (row // 4 == col - 64)))
    lane8 = lanes_of((8, LANES))
    five = five * jnp.where((lane8 >= 72) & (lane8 < 80), 1.0 / 64.0, 0.25)
    fives[...] = five
    for out, start, tag in ((zp, 16, 1), (zm, 0, 2)):
        half = spread(
            three,
            square(
                lambda row, col, start=start: (col < 48)
                & (row == 32 * (col // 16) + start + col % 16)
            ),
        )
        face = spread(packed, square(lambda row, col, tag=tag: row == 4 * (col - 96) + tag))
        out[0:Z_SMALL] = half[0:32] + turn(half[32:64], 48, 1) + face
        face2 = spread(
            packed2, square(lambda row, col, tag=tag: (col < 16) & (row == 4 * col + tag))
        )
        out[Z_SMALL:Z_ROWS] = face2[0:8] + turn(face2[8:16], 16, 1) + five


def second(k_ref, f_ref, x, rows, k_rim, f_rim, lane, period, h):
    inside, pitch = pl.ds(8, rows), rows + 8
    k, e = k_ref[rows_of(x + 1, 0, pitch, rows)], f_ref[x + 1, inside]
    k_up, k_down = z_sides(k, k_rim, x, lane, period)
    e_up, e_down = z_sides(e, f_rim, x, lane, period)
    around = [
        (k_ref[rows_of(x, 0, pitch, rows)], f_ref[x, inside]),
        (k_ref[rows_of(x + 2, 0, pitch, rows)], f_ref[x + 2, inside]),
        (k_ref[rows_of(x + 1, -1, pitch, rows)], f_ref[x + 1, pl.ds(7, rows)]),
        (k_ref[rows_of(x + 1, 1, pitch, rows)], f_ref[x + 1, pl.ds(9, rows)]),
        (k_up, e_up),
        (k_down, e_down),
    ]
    total = k * sum(en for _, en in around) + sum(kn * en for kn, en in around)
    return 1.2 * e + 0.5 * h * total


def window_kernel(
    zlo, zhi, fives, whole, sides, sides2,
    own, xp, xm, ye, cf, cf2, blocks, small,
):
    lane = lanes_of((64, LANES))
    a_half, c_half = zlo[0:Z_SMALL], zhi[0:Z_SMALL]
    a = jnp.concatenate([a_half, turn(a_half, -48, 1)], 0)
    b = whole[...]
    c = jnp.concatenate([c_half, turn(c_half, -48, 1)], 0)

    def window(part):
        low = turn(a, BASE - 16 - 16 * part, 1)
        mid = turn(b, BASE - 32 * part, 1)
        high = turn(c, BASE + 32 - 16 * part, 1)
        value = jnp.where((lane < BASE) | (lane >= 112 + BASE), low, mid)
        value = jnp.where((lane >= BASE + 32) & (lane < BASE + 48), high, value)
        return jnp.where((lane >= BASE + 48) & (lane < 112 + BASE), 0.0, value)

    r, k, s = window(0), window(1), window(2)
    own[0], own[1], own[2] = r, k, s

    even, odd = pl.ds(0, 4, stride=2), pl.ds(1, 4, stride=2)

    def shrink(field, part, weight):
        halves = field.reshape(4, 2, 8, LANES)
        small[0:4] = halves[:, 0] + halves[:, 1]
        summed = small[0:4, even, :] + small[0:4, odd, :]
        for i in range(4):
            small[4 + i // 2, 4 * (i % 2) : 4 * (i % 2) + 4] = summed[i]

        def rule(row, col):
            cell = (row + 16 - BASE) % LANES
            return (cell < 64) & (cell // 2 == col - 32 * part)

        return spread(flat(small[4:6]), square(rule)) * weight

    four = shrink(r, 0, 0.5) + shrink(k, 1, 0.125) + shrink(s, 2, 0.5)
    lane8 = lanes_of((8, LANES))
    for n, ref in enumerate((zlo[Z_SMALL:Z_ROWS], fives[...], zhi[Z_SMALL:Z_ROWS])):
        small[4 + n // 2, 4 * (n % 2) : 4 * (n % 2) + 4] = turn(ref, 32, 1)[0:4]
    small[5, 4:8] = jnp.zeros((4, LANES), F32)
    lane4 = lanes_of((16, LANES))
    four = jnp.where((lane4 < 96) | (lane4 >= 120), four, flat(small[4:6]))
    for q in range(16):
        blocks[q] = four
    main = jnp.where(lane < 42, r, jnp.where(lane < 86, turn(k, 43, 1), turn(s, 86, 1)))
    low = jnp.where(lane == 127, r, jnp.where(lane == 126, k, turn(s, -2, 1)))
    high = jnp.where(lane == 42, r, jnp.where(lane == 43, k, turn(s, 2, 1)))
    ends = jnp.where(lane >= 64, low, turn(high, 86, 1))
    small[...] = ends.reshape(8, 8, LANES)
    ye[0] = small[:, 7, :]
    ye[1] = small[:, 0, :]
    for side, out, i in ((0, xp, 7), (1, xm, 0)):
        out[0:X_FACE] = main
        out[X_FACE:X_SEC] = sides[side]
        out[X_SEC:X_ENDS] = jnp.where(lane8 < 64, sides2[side, 0:8], sides2[side, 8:16])
        out[X_ENDS:X_ROWS] = ends[8 * i : 8 * i + 8]

    def rim(low, high, ready):
        below = spread(low, square(lambda row, col: ready(row) & (col == 4 * (row % 32) + 1)))
        above = spread(high, square(lambda row, col: ready(row) & (col == 4 * (row % 32) + 2)))
        return below + above

    cf[...] = rim(a_half, c_half, lambda row: row >= 96)

    def unfold(half):
        return jnp.concatenate([half, turn(half, -16, 1)], 0)

    cf2[...] = rim(unfold(zlo[Z_SMALL:Z_ROWS]), unfold(zhi[Z_SMALL:Z_ROWS]), lambda row: row < 16)


def second_kernel(kp2, ck2, scale2, first2, cf2, base2, edge2, fp2):
    rim_f2 = cf2[...]
    rim_k2 = ck2[...]
    lane2 = lanes_of((16, LANES))
    inner2 = pl.ds(8, 16)
    fp2[1:17, inner2] = first2[...]
    for x in (0, 17):
        fp2[x, inner2] = jnp.zeros((16, LANES), F32)
    fp2[:, 0:8] = jnp.zeros((18, 8, LANES), F32)
    fp2[:, 24:32] = jnp.zeros((18, 8, LANES), F32)
    def slab(x, carry):
        base2[x] = second(kp2, fp2, x, 16, rim_k2, rim_f2, lane2, 64, scale2[x])
        return carry

    lax.fori_loop(0, 16, slab, 0, unroll=8)
    for n, (x, step) in enumerate(((0, -1), (15, 1))):
        k = kp2[rows_of(x + 1, 0, 24, 16)] + kp2[rows_of(x + 1 + step, 0, 24, 16)]
        edge2[n] = 0.5 * scale2[x] * k
    for n, (y, step) in enumerate(((0, -1), (15, 1))):
        k = kp2[pl.ds(32 + y, 16, stride=24), :] + kp2[pl.ds(32 + y + step, 16, stride=24), :]
        edge2[2 + n] = 0.5 * scale2[:, y, :] * k


def columns_kernel(xlo, xhi, xp, sides, sides2, ye, after, after2, yp, ym):
    lane8 = lanes_of((8, LANES))
    for side, out in ((0, yp), (1, ym)):
        out[0:64] = xlo[0:64]
        out[64:128] = xp[0:64]
        out[128:192] = xhi[0:64]
        out[Y_FACE:Y_SEC] = sides[side]
        face = sides2.at[side]
        out[Y_SEC:Y_ENDS] = jnp.where(lane8 < 64, face[0:8], face[8:16])
        out[Y_ENDS:Y_ROWS] = ye[side]


def wrapped(value):
    last = value.shape[0] - 1
    return [
        jnp.concatenate([value[1:], value[:1]], 0),
        jnp.concatenate([value[last:], value[:last]], 0),
        turn(value, -1, 1),
        turn(value, 1, 1),
        turn(value, -1, 2),
        turn(value, 1, 2),
    ]


def periodic_setup(r, k, s, coefs):
    near = wrapped(k)
    diagonal = s + 3.0 * k + 0.5 * sum(near)
    h = WEIGHT / diagonal
    half = 0.5 * h
    for n in range(6):
        coefs[n] = half * (k + near[n])
    start = h * r
    coefs[6] = start
    return start


def periodic_sweep(e, coefs):
    total = 0.2 * e + coefs[6]
    for n, other in enumerate(wrapped(e)):
        total = total + coefs[n] * other
    return total


def ring_kernel(blocks, ring):
    for q in range(16):
        for i in range(2):
            row = 8 * (2 * (q // 4) + i) + 2 * (q % 4)
            for n in range(3):
                source = blocks[q, 4 * n + 2 * i : 4 * n + 2 * i + 2]
                ring[n, row : row + 2] = source


def planes_kernel(
    place, blocks, ring, low, high, four_out, l4, l5, l6, c4, c5, c6, c7, w4
):
    gx, gy = place[0], place[1]
    for q in range(16):
        for i in range(4):
            l4[4 * (q // 4) + i, 4 * (q % 4) : 4 * (q % 4) + 4] = blocks[q, 4 * i : 4 * i + 4]
    lane = lanes_of((8, 8, LANES))

    def field(f):
        value = jnp.zeros((8, 8, LANES), F32)
        for ref, first in ((high, 2), (low, -4), (ring, -1)):
            for n in range(3):
                start = 8 * (first + n) % 64
                moved = turn(ref[n].reshape(8, 8, LANES), start - 96 - 8 * f, 2)
                value = jnp.where(lane // 8 == start // 8, moved, value)
        return jnp.where(lane < 64, value, turn(value, 64, 2))

    to_six = square(lambda row, col: (row < 64) & (row // 2 == col % 32))
    mean = square(lambda row, col: row < 32)

    def level_six(values, weight, n):
        pairs = values.reshape(4, 2, 8, LANES)
        l6[n] = pairs[:, 0] + pairs[:, 1]
        summed = l6[n, :, pl.ds(0, 4, stride=2), :] + l6[n, :, pl.ds(1, 4, stride=2), :]
        l6[n, :, 0:4] = summed
        l6[n, :, 4:8] = summed
        return (spread(flat(l6[n]), to_six) * weight).reshape(4, 8, LANES)

    def level_seven(values):
        return (spread(flat(values), mean) * (1.0 / 32.0)).reshape(4, 8, LANES)

    fields5 = [field(f) for f in range(3)]
    fields6 = [level_six(v, w, n) for n, (v, w) in enumerate(zip(fields5, (0.5, 0.125, 0.5)))]
    fields7 = [level_seven(v) for v in fields6]
    r4 = l4[...]
    e4 = periodic_setup(r4, turn(r4, 96, 2), turn(r4, 64, 2), c4)
    e5 = periodic_setup(*fields5, c5)
    e6 = periodic_setup(*fields6, c6)
    e7 = periodic_setup(*fields7, c7)

    def sweep(_, carry):
        a, b, c, d = carry
        return (
            periodic_sweep(a, c4), periodic_sweep(b, c5), periodic_sweep(c, c6),
            periodic_sweep(d, c7),
        )

    e4, e5, e6, e7 = lax.fori_loop(0, COARSE_SWEEPS - 1, sweep, (e4, e5, e6, e7))
    l6[0] = e6 + e7
    six = l6[0, gx, pl.ds(gy, 1)] + jnp.zeros((8, LANES), F32)
    six = spread(six, square(lambda row, col: row == col // 32))
    l5[...] = e5
    w4[...] = jnp.zeros((16, LANES), F32)
    w4[0:2] = l5[2 * gx, pl.ds(2 * gy, 2)]
    w4[2:4] = l5[2 * gx + 1, pl.ds(2 * gy, 2)]
    five = six + spread(w4[0:8], square(lambda row, col: row == col // 16))
    l4[...] = e4
    for i in range(4):
        w4[4 * i : 4 * i + 4] = l4[4 * gx + i, pl.ds(4 * gy, 4)]
    lane16 = lanes_of((16, LANES))
    four = jnp.where((lane16 >= 8) & (lane16 < 24), w4[...], 0.0)
    four = spread(four, square(lambda row, col: row == 8 + col // 8))
    for i in range(4):
        for j in range(2):
            row = 2 * (i // 2) + j
            w4[4 * i + 2 * j : 4 * i + 2 * j + 2] = jnp.broadcast_to(
                five[row : row + 1], (2, LANES)
            )
    four_out[...] = four + w4[...]


def fine_kernel(
    kp, ck, scale, first, cf, beside, base, edge, fp
):
    inner = pl.ds(8, 32)
    lane32 = lanes_of((32, LANES))
    for x in (0, 33):
        fp[x, inner] = jnp.zeros((32, LANES), F32)
    blank = jnp.zeros((8, LANES), F32)

    def fill(x, carry):
        fp[x + 1, inner] = first[x]
        fp[x + 1, 0:8] = blank
        fp[x + 1, 40:48] = blank
        return carry

    lax.fori_loop(0, 32, fill, 0, unroll=4)
    rim_k, rim_f = ck[...], cf[...]

    def slab(x, carry):
        base[x] = second(kp, fp, x, 32, rim_k, rim_f, lane32, LANES, scale[x])
        return carry

    lax.fori_loop(0, 32, slab, 0, unroll=4)
    for n, x in enumerate((0, 31)):
        edge[n] = 0.5 * scale[x] * (kp[rows_of(x + 1, 0, 40, 32)] + beside[n])
    for n, y in enumerate((0, 31)):
        k = kp[pl.ds(48 + y, 32, stride=40), :] + beside[2 + n]
        edge[2 + n] = 0.5 * scale[:, y, :] * k


def three_kernel(
    initial_far, own, xlo, xhi, ylo, yhi, base, base2, edge, edge2,
    three_out, two_out, fine_out,
    r3, s3, k3, c3, ea, eb, w2, sems,
):
    inputs = fetch(((initial_far, fine_out),), sems)
    lane8 = lanes_of((8, LANES))
    for ix in range(3):
        for iy, y_ref in enumerate((ylo, None, yhi)):
            for i in range(8):
                if ix == 1 and iy == 1:
                    r, k, s = [own[f, 8 * i : 8 * i + 8] for f in range(3)]
                else:
                    if iy == 1:
                        r = (xlo if ix == 0 else xhi)[8 * i : 8 * i + 8]
                    else:
                        r = y_ref[64 * ix + 8 * i : 64 * ix + 8 * i + 8]
                    k = turn(r, -43, 1)
                    s = turn(r, -86, 1)
                    if iy == 1 and ((ix == 0 and i == 7) or (ix == 2 and i == 0)):
                        low = (xlo if ix == 0 else xhi)[X_ENDS:X_ROWS]
                        high = turn(low, 42, 1)
                        r = jnp.where(lane8 == 127, low, jnp.where(lane8 == 42, high, r))
                        k = jnp.where(lane8 == 126, low, jnp.where(lane8 == 43, high, k))
                        low, high = turn(low, 2, 1), turn(high, -2, 1)
                        s = jnp.where(lane8 == 127, low, jnp.where(lane8 == 42, high, s))
                x, y = 8 * ix + i, 8 * iy
                r3[x, y : y + 8] = r
                k3[x, y + 8 : y + 16] = k
                s3[x, y : y + 8] = s
    lane1 = lanes_of((1, LANES))
    for y, y_ref in ((7, ylo), (16, yhi)):
        low = y_ref[Y_ENDS:Y_ROWS]
        high = turn(low, 42, 1)
        low_s, high_s = turn(low, 2, 1), turn(high, -2, 1)
        for i in range(8):
            row = slice(i, i + 1)

            def patch(ref, at, below, above, low_lane, high_lane):
                kept = jnp.where(lane1 == high_lane, above[row], ref[8 + i, at : at + 1])
                ref[8 + i, at : at + 1] = jnp.where(lane1 == low_lane, below[row], kept)

            patch(r3, y, low, high, 127, 42)
            patch(k3, y + 8, low, high, 126, 43)
            patch(s3, y, low_s, high_s, 127, 42)
    rim = jnp.zeros((24, 8, LANES), F32)
    for ref in (k3, ea, eb):
        ref[:, 0:8] = rim
        ref[:, 32:40] = rim
    mid = pl.ds(8, 24)

    def setup3(x, carry):
        k = k3[x, mid]
        near = [
            k3[x + 1, mid], k3[x - 1, mid], k3[x, pl.ds(9, 24)], k3[x, pl.ds(7, 24)],
            turn(k, -1, 1), turn(k, 1, 1),
        ]
        h = WEIGHT / (s3[x] + 3.0 * k + 0.5 * sum(near))
        half = 0.5 * h
        for n in range(6):
            c3[n, x] = half * (k + near[n])
        g = h * r3[x]
        c3[6, x] = g
        ea[x, mid] = g
        return carry

    lax.fori_loop(1, 23, setup3, 0, unroll=True)
    source, target = ea, eb
    for step in range(2, COARSE_SWEEPS + 1):

        def sweep3(x, carry, source=source, target=target):
            e = source[x, mid]
            near = [
                source[x + 1, mid], source[x - 1, mid],
                source[x, pl.ds(9, 24)], source[x, pl.ds(7, 24)],
                turn(e, -1, 1), turn(e, 1, 1),
            ]
            total = 0.2 * e + c3[6, x]
            for n in range(6):
                total = total + c3[n, x] * near[n]
            target[x, mid] = total
            return carry

        lax.fori_loop(step, 24 - step, sweep3, 0, unroll=True)
        source, target = target, source

    mine = source[8:16, 16:24]
    lane3 = lanes_of((8, 8, LANES))
    three = flat(jnp.where((lane3 >= BASE) & (lane3 < BASE + 32), mine, 0.0))
    three_out[...] = spread(three, square(lambda row, col: row == BASE + col // 4))

    def beyond(ref, start):
        half = ref[start : start + 8]
        other = turn(half, 64, 1)
        return jnp.concatenate(
            [jnp.where(lane8 < 64, half, other), jnp.where(lane8 < 64, other, half)], 0
        )

    w2[...] = base2[...]
    for n, (x, ref) in enumerate(((0, xlo), (15, xhi))):
        w2[x] = w2[x] + edge2[n] * beyond(ref, X_SEC)
    for n, (y, ref) in enumerate(((0, ylo), (15, yhi))):
        w2[:, y, :] = w2[:, y, :] + edge2[2 + n] * beyond(ref, Y_SEC)
    two_out[...] = spread(flat(w2[...]), square(lambda row, col: row == col // 2))

    for copy in inputs:
        copy.wait()

    def add(x, carry):
        fine_out[x] = fine_out[x] + base[x]
        return carry

    lax.fori_loop(0, 32, add, 0, unroll=8)
    for n, (x, ref) in enumerate(((0, xlo), (31, xhi))):
        fine_out[x] = fine_out[x] + edge[n] * ref[X_FACE:X_SEC]
    for n, (y, ref) in enumerate(((0, ylo), (31, yhi))):
        fine_out[:, y, :] = fine_out[:, y, :] + edge[2 + n] * ref[Y_FACE:Y_SEC]


def finish_kernel(
    three_in, two_in, four_in, fine_in, out_far, w3, w32, up, out, sems
):
    four = four_in[...]
    for i in range(8):
        block = four[4 * (i // 2) : 4 * (i // 2) + 4]
        w3[i, pl.ds(0, 4, stride=2), :] = block
        w3[i, pl.ds(1, 4, stride=2), :] = block
    three = three_in[...] + flat(w3[...])

    even8, odd8 = pl.ds(0, 8, stride=2), pl.ds(1, 8, stride=2)
    for i in range(16):
        block = three[8 * (i // 2) : 8 * (i // 2) + 8]
        w32[i, even8, :] = block
        w32[i, odd8, :] = block
    two = two_in[...].reshape(16, 16, LANES) + w32[...]
    up[:, pl.ds(0, 16, stride=2), :] = two
    up[:, pl.ds(1, 16, stride=2), :] = two

    depth = 32 // CHUNKS
    copies = []
    for c in range(CHUNKS):
        part = pl.ds(c * depth, depth)
        for x in range(c * depth, (c + 1) * depth):
            out[x] = fine_in[x] + up[x // 2]
        copy = pltpu.make_async_copy(out.at[part], out_far.at[part], sems.at[c])
        copy.start()
        copies.append(copy)
    for copy in copies:
        copy.wait()


VM = pl.BlockSpec(memory_space=pltpu.VMEM)
SM = pl.BlockSpec(memory_space=pltpu.SMEM)
FAR = pl.BlockSpec(memory_space=pltpu.HBM)


def shape(*dims):
    return pltpu.VMEM(dims, F32)


def local(kernel, outs, ins, scratch, name, sems=None, out_spec=VM):
    scratch = [pltpu.VMEM(dims, F32) for dims in scratch]
    if sems is not None:
        scratch.append(pltpu.SemaphoreType.DMA(sems))
    return pl.pallas_call(
        kernel,
        out_shape=outs,
        in_specs=ins,
        out_specs=[out_spec] * len(outs),
        scratch_shapes=scratch,
        compiler_params=pltpu.CompilerParams(vmem_limit_bytes=24 * 1024 * 1024),
        name=name,
    )


def on_device(initial, rhs, kappa, sigma):
    place = jnp.stack([lax.axis_index(axis) for axis in ("gx", "gy", "gz")]).astype(jnp.int32)

    def passed(value, axis, step):
        count = lax.axis_size(axis)
        return lax.ppermute(value, axis, [(i, (i + step) % count) for i in range(count)])

    block = (32, 32, LANES)
    block2 = (16, 16, LANES)
    edge = shape(3, 32, LANES)
    far = [
        pltpu.with_memory_space_constraint(value, pltpu.HBM)
        for value in (kappa, initial)
    ]
    xp, xm, yp, ym, zs, kappa, initial = local(
        faces_kernel,
        [edge, edge, edge, edge, shape(2, 32, LANES)] + [shape(*block)] * 2,
        [FAR] * 2, [], "faces", sems=(2, CHUNKS),
    )(*far)
    zlo, zhi = passed(zs, "gz", 1), passed(zs, "gz", -1)
    xlo, xhi = passed(xp, "gx", 1), passed(xm, "gx", -1)
    ylo, yhi = passed(yp, "gy", 1), passed(ym, "gy", -1)
    kp, ck, diagonal, rest, pair_k, pair_s = local(
        inside_kernel,
        [
            shape(1368, LANES), shape(32, LANES), shape(*block), shape(*block),
            shape(16, 32, LANES), shape(16, 32, LANES),
        ],
        [VM] * 6, [(34, 48, LANES)], "inside",
    )(kappa, initial, rhs, sigma, zlo, zhi)
    (
        scale, first, beside, zp, zm, fives, whole, sides_x, sides_y, kp2, ck2, scale2, first2,
        sides2_x, sides2_y,
    ) = local(
        residual_kernel,
        [
            shape(*block), shape(*block), shape(4, 32, LANES),
            shape(Z_ROWS, LANES), shape(Z_ROWS, LANES), shape(8, LANES),
            shape(64, LANES), shape(2, 32, LANES), shape(2, 32, LANES), shape(440, LANES),
            shape(16, LANES), shape(*block2), shape(*block2), shape(2, 16, LANES),
            shape(2, 16, LANES),
        ],
        [VM] * 11, [(16, 32, LANES), (4, 32, LANES), (8, 16, LANES), (4, 32, LANES)],
        "residual",
    )(kappa, initial, diagonal, rest, ck, pair_k, pair_s, xlo, xhi, ylo, yhi)

    zlo, zhi = passed(zp, "gz", 1), passed(zm, "gz", -1)
    own, xp, xm, ye, cf, cf2, blocks = local(
        window_kernel,
        [
            shape(3, 64, LANES), shape(X_ROWS, LANES), shape(X_ROWS, LANES),
            shape(2, 8, LANES), shape(32, LANES), shape(16, LANES),
            shape(16, 16, LANES),
        ],
        [VM] * 6, [(8, 8, LANES)], "window",
    )(zlo, zhi, fives, whole, sides_x, sides2_x)
    xlo, xhi = passed(xp, "gx", 1), passed(xm, "gx", -1)
    planes = lax.all_to_all(blocks, ("gx", "gy"), 0, 0)
    base, edge = local(
        fine_kernel,
        [shape(*block), shape(4, 32, LANES)], [VM] * 6, [(34, 48, LANES)], "fine",
    )(kp, ck, scale, first, cf, beside)
    base2, edge2 = local(
        second_kernel, [shape(*block2), shape(4, 16, LANES)], [VM] * 5, [(18, 32, LANES)],
        "second",
    )(kp2, ck2, scale2, first2, cf2)
    yp, ym = local(
        columns_kernel, [shape(Y_ROWS, LANES)] * 2, [VM] * 8, [], "columns"
    )(xlo, xhi, xp, sides_y, sides2_y, ye, edge, edge2)
    ylo, yhi = passed(yp, "gy", 1), passed(ym, "gy", -1)
    (ring,) = local(ring_kernel, [shape(3, 64, LANES)], [VM], [], "ring")(planes)
    ring_low, ring_high = passed(ring, "gz", 3), passed(ring, "gz", -3)
    padded3 = (24, 40, LANES)
    block3 = (24, 24, LANES)
    three, two, fine = local(
        three_kernel, [shape(64, LANES), shape(256, LANES), shape(*block)], [FAR] + [VM] * 9,
        [block3, block3, padded3, (7,) + block3, padded3, padded3, block2], "three",
        sems=(1, CHUNKS),
    )(far[1], own, xlo, xhi, ylo, yhi, base, base2, edge, edge2)
    (four,) = local(
        planes_kernel, [shape(16, LANES)], [SM] + [VM] * 4,
        [
            block2, (8, 8, LANES), (3, 4, 8, LANES), (7,) + block2,
            (7, 8, 8, LANES), (7, 4, 8, LANES), (7, 4, 8, LANES), (16, LANES),
        ],
        "planes",
    )(place, planes, ring, ring_low, ring_high)
    return local(
        finish_kernel, [pltpu.HBM(block, F32)], [VM] * 4,
        [(8, 8, LANES), block2, (16, 32, LANES), block],
        "finish", sems=(CHUNKS,), out_spec=FAR,
    )(three, two, four, fine)[0]


def solution(mesh):
    spec = P("gx", "gy", "gz")
    return jax.shard_map(
        on_device, mesh=mesh, in_specs=(spec,) * 4, out_specs=spec, check_vma=False
    )
```

```python
import jax
import jax.numpy as jnp
from jax import lax
from jax.experimental import pallas as pl
from jax.experimental.pallas import tpu as pltpu
from jax.sharding import PartitionSpec as P

COARSE_SWEEPS = 8
WEIGHT = 0.8
LANES = 128
F32 = jnp.float32
BF16 = jnp.bfloat16

Z_SMALL, Z_ROWS = 32, 40
X_FACE, X_SEC, X_ENDS, X_ROWS = 64, 96, 104, 112
Y_FACE, Y_SEC, Y_ENDS, Y_ROWS = 192, 224, 232, 240
CHUNKS = 2
BASE = 5


def turn(value, shift, axis):
    size = value.shape[axis]
    if isinstance(shift, int):
        shift = shift % size
        if shift == 0:
            return value
    return pltpu.roll(value, shift, axis)


def lanes_of(shape):
    return lax.broadcasted_iota(jnp.int32, shape, len(shape) - 1)


def square(rule):
    row = lax.broadcasted_iota(jnp.int32, (LANES, LANES), 0)
    col = lax.broadcasted_iota(jnp.int32, (LANES, LANES), 1)
    return jnp.where(rule(row, col), 1.0, 0.0).astype(BF16)


def spread(value, chosen):
    total = None
    for part in range(3):
        piece = value.astype(BF16)
        term = jnp.dot(piece, chosen, preferred_element_type=F32)
        total = term if total is None else total + term
        if part < 2:
            value = value - piece.astype(F32)
    return total


def rows_of(x, shift, pitch, count):
    start = pitch * x + 8
    return pl.ds(start + shift if shift else pl.multiple_of(start, 8), count)


def flat(value):
    return value.reshape(-1, LANES)


def fetch(pairs, sems):
    depth = pairs[0][0].shape[0] // CHUNKS
    copies = []
    for c in range(CHUNKS):
        part = pl.ds(c * depth, depth)
        for n, (far, near) in enumerate(pairs):
            copy = pltpu.make_async_copy(far.at[part], near.at[part], sems.at[n, c])
            copy.start()
            copies.append(copy)
    return copies


def faces_kernel(kappa_far, initial_far, xp, xm, yp, ym, zs, kappa, initial, sems):
    depth = 32 // CHUNKS
    copies = fetch(((kappa_far, kappa), (initial_far, initial)), sems)
    lane = lanes_of((32, LANES))
    first = second = jnp.zeros((32, LANES), F32)

    def body(x, carry):
        first, second = carry
        mine = lane // 4 == x
        shift = 4 * x + 2
        first = jnp.where(mine, turn(kappa[x], shift, 1), first)
        second = jnp.where(mine, turn(initial[x], shift, 1), second)
        return first, second

    for c in range(CHUNKS):
        copies[2 * c].wait()
        copies[2 * c + 1].wait()
        first, second = lax.fori_loop(
            c * depth, (c + 1) * depth, body, (first, second), unroll=True
        )
    zs[0] = first
    zs[1] = second
    xp[0] = kappa[31]
    xp[1] = kappa[30]
    xp[2] = initial[31]
    xm[0] = kappa[0]
    xm[1] = kappa[1]
    xm[2] = initial[0]
    yp[0] = kappa[:, 31, :]
    yp[1] = kappa[:, 30, :]
    yp[2] = initial[:, 31, :]
    ym[0] = kappa[:, 0, :]
    ym[1] = kappa[:, 1, :]
    ym[2] = initial[:, 0, :]


def z_sides(value, rim, x, lane, period):
    near = turn(rim, 126 - 4 * x, 1)
    if period < LANES:
        other = turn(rim, lax.rem(190 - 4 * x, 128), 1)
        near = jnp.where((lane >= 32) & (lane < 96), other, near)
    inside = lane % period
    above = turn(jnp.where(inside == 0, near, value), LANES - 1, 1)
    below = turn(jnp.where(inside == period - 1, near, value), 1, 1)
    return above, below


def inside_kernel(
    kappa, initial, rhs, sigma, zlo, zhi, kp, ck, diagonal, rest, pair_k, pair_s, vp
):
    lane = lanes_of((32, LANES))
    inner = pl.ds(8, 32)
    blank, blank8 = jnp.zeros((32, LANES), F32), jnp.zeros((8, LANES), F32)
    for x in (0, 33):
        kp[rows_of(x, 0, 40, 32)] = blank
        vp[x, inner] = blank
    kp[0:8] = blank8
    kp[40 * 33 : 40 * 33 + 8] = blank8
    kp[40 * 34 : 40 * 34 + 8] = blank8

    def fill(x, carry):
        kp[rows_of(x + 1, -8, 40, 8)] = blank8
        kp[rows_of(x + 1, 0, 40, 32)] = kappa[x]
        vp[x + 1, inner] = initial[x]
        vp[x + 1, 0:8] = blank8
        vp[x + 1, 40:48] = blank8
        return carry

    lax.fori_loop(0, 32, fill, 0, unroll=4)
    low_half = lane % 4 < 2
    rim_k = jnp.where(low_half, zlo[0], zhi[0])
    rim_v = jnp.where(low_half, zlo[1], zhi[1])
    ck[...] = rim_k

    def slab(x):
        k = kappa[x]
        v = initial[x]
        around = [
            (kp[rows_of(x, 0, 40, 32)], vp[x, inner]),
            (kp[rows_of(x + 2, 0, 40, 32)], vp[x + 2, inner]),
            (kp[rows_of(x + 1, -1, 40, 32)], vp[x + 1, pl.ds(7, 32)]),
            (kp[rows_of(x + 1, 1, 40, 32)], vp[x + 1, pl.ds(9, 32)]),
        ]
        k_up, k_down = z_sides(k, rim_k, x, lane, LANES)
        v_up, v_down = z_sides(v, rim_v, x, lane, LANES)
        around += [(k_up, v_up), (k_down, v_down)]
        k_sum = sum(kn for kn, _ in around)
        v_sum = sum(vn for _, vn in around)
        both = sum(kn * vn for kn, vn in around)
        s = sigma[x]
        d = s + 3.0 * k + 0.5 * k_sum
        diagonal[x] = d
        rest[x] = rhs[x] - d * v + 0.5 * (k * v_sum + both)
        return k, s

    def two(i, carry):
        k0, s0 = slab(2 * i)
        k1, s1 = slab(2 * i + 1)
        pair_k[i] = k0 + k1
        pair_s[i] = s0 + s1
        return carry

    lax.fori_loop(0, 16, two, 0, unroll=3)


def residual_kernel(
    kappa, initial, diagonal, rest, rim, pair_k, pair_s, xlo, xhi, ylo, yhi,
    scale, first, beside, zp, zm, fives, whole, sides_x, sides_y, kp2, ck2, scale2, first2,
    sides2_x, sides2_y, pair_r, rims, small, fix,
):
    lane = lanes_of((32, LANES))
    row = lax.broadcasted_iota(jnp.int32, (32, LANES), 0)
    rim_k = rim[...]
    for n, message in enumerate((xlo, xhi, ylo, yhi)):
        beside[n] = message[0]

    def beyond(k, v, message):
        kn, vn = message[0], message[2]
        return 0.5 * kn, 0.5 * ((k + kn) * vn - kn * v)

    fix[0], fix[1] = beyond(kappa[:, 0, :], initial[:, 0, :], ylo)
    fix[2], fix[3] = beyond(kappa[:, 31, :], initial[:, 31, :], yhi)

    def slab(x, packed, message=None):
        one = pl.ds(x, 1)
        d, r = diagonal[x], rest[x]
        if message is not None:
            more_d, more_r = beyond(kappa[x], initial[x], message)
            d, r = d + more_d, r + more_r
        d = jnp.where(row == 0, d + fix[0, one], jnp.where(row == 31, d + fix[2, one], d))
        r = jnp.where(row == 0, r + fix[1, one], jnp.where(row == 31, r + fix[3, one], r))
        h = WEIGHT / d
        e = h * r
        scale[x] = h
        first[x] = e
        packed = jnp.where(lane // 4 == x, turn(e, 4 * x + 2, 1), packed)
        return r, packed

    def two(i, packed, low=None, high=None):
        r0, packed = slab(2 * i, packed, low)
        r1, packed = slab(2 * i + 1, packed, high)
        pair_r[i] = r0 + r1
        return packed

    packed = two(0, jnp.zeros((32, LANES), F32), low=xlo)
    packed = lax.fori_loop(1, 15, two, packed, unroll=14)
    packed = two(15, packed, high=xhi)
    sides_x[0] = first[31]
    sides_x[1] = first[0]
    sides_y[0] = first[:, 31, :]
    sides_y[1] = first[:, 0, :]

    even, odd = pl.ds(0, 16, stride=2), pl.ds(1, 16, stride=2)
    to_two = square(lambda row, col: row // 2 == col % 64)

    def level_two(ref, weight):
        summed = ref[:, even, :] + ref[:, odd, :]
        return (spread(flat(summed), to_two) * weight).reshape(16, 16, LANES)

    r2 = level_two(pair_r, 0.5)
    k2 = level_two(pair_k, 0.125)
    s2 = level_two(pair_s, 0.5)
    rims[0] = xlo[0] + xlo[1]
    rims[1] = xhi[0] + xhi[1]
    rims[2] = ylo[0] + ylo[1]
    rims[3] = yhi[0] + yhi[1]
    halo = rims[:, even, :] + rims[:, odd, :]
    halo = (spread(flat(halo), to_two) * 0.125).reshape(4, 16, LANES)
    kp2[rows_of(0, 0, 24, 16)] = halo[0]
    kp2[rows_of(17, 0, 24, 16)] = halo[1]
    for x in range(16):
        kp2[rows_of(x + 1, 0, 24, 16)] = k2[x]
        kp2[rows_of(x + 1, -1, 24, 1)] = halo[2, x : x + 1]
        kp2[rows_of(x + 1, 16, 24, 1)] = halo[3, x : x + 1]
    rims[0] = rim_k
    rim_pair = rims[0, even, :] + rims[0, odd, :]

    def rim_rule(row, col):
        low = (col % 4 == 1) & (row % 4 < 2)
        high = (col % 4 == 2) & (row % 4 >= 2)
        return (row // 8 == col // 4) & (low | high)

    rim_k2 = spread(rim_pair, square(rim_rule)) * 0.125
    ck2[...] = rim_k2
    lane2 = lanes_of((16, LANES))
    packed2 = jnp.zeros((16, LANES), F32)
    for x in range(16):
        k = k2[x]
        up, down = z_sides(k, rim_k2, x, lane2, 64)
        k_sum = (
            kp2[rows_of(x, 0, 24, 16)] + kp2[rows_of(x + 2, 0, 24, 16)]
            + kp2[rows_of(x + 1, -1, 24, 16)] + kp2[rows_of(x + 1, 1, 24, 16)] + up + down
        )
        h = WEIGHT / (s2[x] + 3.0 * k + 0.5 * k_sum)
        e = h * r2[x]
        scale2[x] = h
        first2[x] = e
        packed2 = jnp.where(lane2 // 4 == x, turn(e, 4 * x + 2, 1), packed2)
    sides2_x[0] = first2[15]
    sides2_x[1] = first2[0]
    sides2_y[0] = first2[:, 15, :]
    sides2_y[1] = first2[:, 0, :]

    even8, odd8 = pl.ds(0, 8, stride=2), pl.ds(1, 8, stride=2)

    def level_three(field, part, weight):
        halves = field.reshape(8, 2, 16, LANES)
        small[...] = halves[:, 0] + halves[:, 1]
        summed = small[:, even8, :] + small[:, odd8, :]
        rule = square(lambda row, col: (row < 64) & (row // 2 == col - 32 * part))
        return spread(flat(summed), rule) * weight

    three = level_three(r2, 0, 0.5) + level_three(k2, 1, 0.125) + level_three(s2, 2, 0.5)
    whole[...] = three
    cubes = three.reshape(2, 4, 8, LANES)
    small[0:2, 0:8] = cubes[:, 0] + cubes[:, 1] + cubes[:, 2] + cubes[:, 3]
    quads = [small[0:2, pl.ds(j, 2, stride=4), :] for j in range(4)]
    quad = quads[0] + quads[1] + quads[2] + quads[3]
    small[2, 0:8] = jnp.zeros((8, LANES), F32)
    small[2, 0:2] = quad[0]
    small[2, 2:4] = quad[1]
    five = spread(small[2, 0:8], square(lambda row, col: (row < 96) & (row // 4 == col - 64)))
    lane8 = lanes_of((8, LANES))
    five = five * jnp.where((lane8 >= 72) & (lane8 < 80), 1.0 / 64.0, 0.25)
    fives[...] = five
    for out, start, tag in ((zp, 16, 1), (zm, 0, 2)):
        half = spread(
            three,
            square(
                lambda row, col, start=start: (col < 48)
                & (row == 32 * (col // 16) + start + col % 16)
            ),
        )
        face = spread(packed, square(lambda row, col, tag=tag: row == 4 * (col - 96) + tag))
        out[0:Z_SMALL] = half[0:32] + turn(half[32:64], 48, 1) + face
        face2 = spread(
            packed2, square(lambda row, col, tag=tag: (col < 16) & (row == 4 * col + tag))
        )
        out[Z_SMALL:Z_ROWS] = face2[0:8] + turn(face2[8:16], 16, 1) + five


def second(k_ref, f_ref, x, rows, k_rim, f_rim, lane, period, h):
    inside, pitch = pl.ds(8, rows), rows + 8
    k, e = k_ref[rows_of(x + 1, 0, pitch, rows)], f_ref[x + 1, inside]
    k_up, k_down = z_sides(k, k_rim, x, lane, period)
    e_up, e_down = z_sides(e, f_rim, x, lane, period)
    around = [
        (k_ref[rows_of(x, 0, pitch, rows)], f_ref[x, inside]),
        (k_ref[rows_of(x + 2, 0, pitch, rows)], f_ref[x + 2, inside]),
        (k_ref[rows_of(x + 1, -1, pitch, rows)], f_ref[x + 1, pl.ds(7, rows)]),
        (k_ref[rows_of(x + 1, 1, pitch, rows)], f_ref[x + 1, pl.ds(9, rows)]),
        (k_up, e_up),
        (k_down, e_down),
    ]
    total = k * sum(en for _, en in around) + sum(kn * en for kn, en in around)
    return 1.2 * e + 0.5 * h * total


def window_kernel(
    zlo, zhi, fives, whole, sides, sides2,
    own, xp, xm, ye, cf, cf2, blocks, small,
):
    lane = lanes_of((64, LANES))
    a_half, c_half = zlo[0:Z_SMALL], zhi[0:Z_SMALL]
    a = jnp.concatenate([a_half, turn(a_half, -48, 1)], 0)
    b = whole[...]
    c = jnp.concatenate([c_half, turn(c_half, -48, 1)], 0)

    def window(part):
        low = turn(a, BASE - 16 - 16 * part, 1)
        mid = turn(b, BASE - 32 * part, 1)
        high = turn(c, BASE + 32 - 16 * part, 1)
        value = jnp.where((lane < BASE) | (lane >= 112 + BASE), low, mid)
        value = jnp.where((lane >= BASE + 32) & (lane < BASE + 48), high, value)
        return jnp.where((lane >= BASE + 48) & (lane < 112 + BASE), 0.0, value)

    r, k, s = window(0), window(1), window(2)
    own[0], own[1], own[2] = r, k, s

    even, odd = pl.ds(0, 4, stride=2), pl.ds(1, 4, stride=2)

    def shrink(field, part, weight):
        halves = field.reshape(4, 2, 8, LANES)
        small[0:4] = halves[:, 0] + halves[:, 1]
        summed = small[0:4, even, :] + small[0:4, odd, :]
        for i in range(4):
            small[4 + i // 2, 4 * (i % 2) : 4 * (i % 2) + 4] = summed[i]

        def rule(row, col):
            cell = (row + 16 - BASE) % LANES
            return (cell < 64) & (cell // 2 == col - 32 * part)

        return spread(flat(small[4:6]), square(rule)) * weight

    four = shrink(r, 0, 0.5) + shrink(k, 1, 0.125) + shrink(s, 2, 0.5)
    lane8 = lanes_of((8, LANES))
    for n, ref in enumerate((zlo[Z_SMALL:Z_ROWS], fives[...], zhi[Z_SMALL:Z_ROWS])):
        small[4 + n // 2, 4 * (n % 2) : 4 * (n % 2) + 4] = turn(ref, 32, 1)[0:4]
    small[5, 4:8] = jnp.zeros((4, LANES), F32)
    lane4 = lanes_of((16, LANES))
    four = jnp.where((lane4 < 96) | (lane4 >= 120), four, flat(small[4:6]))
    for q in range(16):
        blocks[q] = four
    main = jnp.where(lane < 42, r, jnp.where(lane < 86, turn(k, 43, 1), turn(s, 86, 1)))
    low = jnp.where(lane == 127, r, jnp.where(lane == 126, k, turn(s, -2, 1)))
    high = jnp.where(lane == 42, r, jnp.where(lane == 43, k, turn(s, 2, 1)))
    ends = jnp.where(lane >= 64, low, turn(high, 86, 1))
    small[...] = ends.reshape(8, 8, LANES)
    ye[0] = small[:, 7, :]
    ye[1] = small[:, 0, :]
    for side, out, i in ((0, xp, 7), (1, xm, 0)):
        out[0:X_FACE] = main
        out[X_FACE:X_SEC] = sides[side]
        out[X_SEC:X_ENDS] = jnp.where(lane8 < 64, sides2[side, 0:8], sides2[side, 8:16])
        out[X_ENDS:X_ROWS] = ends[8 * i : 8 * i + 8]

    def rim(low, high, ready):
        below = spread(low, square(lambda row, col: ready(row) & (col == 4 * (row % 32) + 1)))
        above = spread(high, square(lambda row, col: ready(row) & (col == 4 * (row % 32) + 2)))
        return below + above

    cf[...] = rim(a_half, c_half, lambda row: row >= 96)

    def unfold(half):
        return jnp.concatenate([half, turn(half, -16, 1)], 0)

    cf2[...] = rim(unfold(zlo[Z_SMALL:Z_ROWS]), unfold(zhi[Z_SMALL:Z_ROWS]), lambda row: row < 16)


def second_kernel(kp2, ck2, scale2, first2, cf2, base2, edge2, fp2):
    rim_f2 = cf2[...]
    rim_k2 = ck2[...]
    lane2 = lanes_of((16, LANES))
    inner2 = pl.ds(8, 16)
    fp2[1:17, inner2] = first2[...]
    for x in (0, 17):
        fp2[x, inner2] = jnp.zeros((16, LANES), F32)
    fp2[:, 0:8] = jnp.zeros((18, 8, LANES), F32)
    fp2[:, 24:32] = jnp.zeros((18, 8, LANES), F32)
    def slab(x, carry):
        base2[x] = second(kp2, fp2, x, 16, rim_k2, rim_f2, lane2, 64, scale2[x])
        return carry

    lax.fori_loop(0, 16, slab, 0, unroll=8)
    for n, (x, step) in enumerate(((0, -1), (15, 1))):
        k = kp2[rows_of(x + 1, 0, 24, 16)] + kp2[rows_of(x + 1 + step, 0, 24, 16)]
        edge2[n] = 0.5 * scale2[x] * k
    for n, (y, step) in enumerate(((0, -1), (15, 1))):
        k = kp2[pl.ds(32 + y, 16, stride=24), :] + kp2[pl.ds(32 + y + step, 16, stride=24), :]
        edge2[2 + n] = 0.5 * scale2[:, y, :] * k


def columns_kernel(xlo, xhi, xp, sides, sides2, ye, after, after2, yp, ym):
    lane8 = lanes_of((8, LANES))
    for side, out in ((0, yp), (1, ym)):
        out[0:64] = xlo[0:64]
        out[64:128] = xp[0:64]
        out[128:192] = xhi[0:64]
        out[Y_FACE:Y_SEC] = sides[side]
        face = sides2.at[side]
        out[Y_SEC:Y_ENDS] = jnp.where(lane8 < 64, face[0:8], face[8:16])
        out[Y_ENDS:Y_ROWS] = ye[side]


def wrapped(value):
    last = value.shape[0] - 1
    return [
        jnp.concatenate([value[1:], value[:1]], 0),
        jnp.concatenate([value[last:], value[:last]], 0),
        turn(value, -1, 1),
        turn(value, 1, 1),
        turn(value, -1, 2),
        turn(value, 1, 2),
    ]


def periodic_setup(r, k, s, coefs):
    near = wrapped(k)
    diagonal = s + 3.0 * k + 0.5 * sum(near)
    h = WEIGHT / diagonal
    half = 0.5 * h
    for n in range(6):
        coefs[n] = half * (k + near[n])
    start = h * r
    coefs[6] = start
    return start


def periodic_sweep(e, coefs):
    total = 0.2 * e + coefs[6]
    for n, other in enumerate(wrapped(e)):
        total = total + coefs[n] * other
    return total


def ring_kernel(blocks, ring):
    for q in range(16):
        for i in range(2):
            row = 8 * (2 * (q // 4) + i) + 2 * (q % 4)
            for n in range(3):
                source = blocks[q, 4 * n + 2 * i : 4 * n + 2 * i + 2]
                ring[n, row : row + 2] = source


def planes_kernel(
    place, blocks, ring, low, high, four_out, l4, l5, l6, c4, c5, c6, c7, w4
):
    gx, gy = place[0], place[1]
    for q in range(16):
        for i in range(4):
            l4[4 * (q // 4) + i, 4 * (q % 4) : 4 * (q % 4) + 4] = blocks[q, 4 * i : 4 * i + 4]
    lane = lanes_of((8, 8, LANES))

    def field(f):
        value = jnp.zeros((8, 8, LANES), F32)
        for ref, first in ((high, 2), (low, -4), (ring, -1)):
            for n in range(3):
                start = 8 * (first + n) % 64
                moved = turn(ref[n].reshape(8, 8, LANES), start - 96 - 8 * f, 2)
                value = jnp.where(lane // 8 == start // 8, moved, value)
        return jnp.where(lane < 64, value, turn(value, 64, 2))

    to_six = square(lambda row, col: (row < 64) & (row // 2 == col % 32))
    mean = square(lambda row, col: row < 32)

    def level_six(values, weight, n):
        pairs = values.reshape(4, 2, 8, LANES)
        l6[n] = pairs[:, 0] + pairs[:, 1]
        summed = l6[n, :, pl.ds(0, 4, stride=2), :] + l6[n, :, pl.ds(1, 4, stride=2), :]
        l6[n, :, 0:4] = summed
        l6[n, :, 4:8] = summed
        return (spread(flat(l6[n]), to_six) * weight).reshape(4, 8, LANES)

    def level_seven(values):
        return (spread(flat(values), mean) * (1.0 / 32.0)).reshape(4, 8, LANES)

    fields5 = [field(f) for f in range(3)]
    fields6 = [level_six(v, w, n) for n, (v, w) in enumerate(zip(fields5, (0.5, 0.125, 0.5)))]
    fields7 = [level_seven(v) for v in fields6]
    r4 = l4[...]
    e4 = periodic_setup(r4, turn(r4, 96, 2), turn(r4, 64, 2), c4)
    e5 = periodic_setup(*fields5, c5)
    e6 = periodic_setup(*fields6, c6)
    e7 = periodic_setup(*fields7, c7)

    def sweep(_, carry):
        a, b, c, d = carry
        return (
            periodic_sweep(a, c4), periodic_sweep(b, c5), periodic_sweep(c, c6),
            periodic_sweep(d, c7),
        )

    e4, e5, e6, e7 = lax.fori_loop(0, COARSE_SWEEPS - 1, sweep, (e4, e5, e6, e7))
    l6[0] = e6 + e7
    six = l6[0, gx, pl.ds(gy, 1)] + jnp.zeros((8, LANES), F32)
    six = spread(six, square(lambda row, col: row == col // 32))
    l5[...] = e5
    w4[...] = jnp.zeros((16, LANES), F32)
    w4[0:2] = l5[2 * gx, pl.ds(2 * gy, 2)]
    w4[2:4] = l5[2 * gx + 1, pl.ds(2 * gy, 2)]
    five = six + spread(w4[0:8], square(lambda row, col: row == col // 16))
    l4[...] = e4
    for i in range(4):
        w4[4 * i : 4 * i + 4] = l4[4 * gx + i, pl.ds(4 * gy, 4)]
    lane16 = lanes_of((16, LANES))
    four = jnp.where((lane16 >= 8) & (lane16 < 24), w4[...], 0.0)
    four = spread(four, square(lambda row, col: row == 8 + col // 8))
    for i in range(4):
        for j in range(2):
            row = 2 * (i // 2) + j
            w4[4 * i + 2 * j : 4 * i + 2 * j + 2] = jnp.broadcast_to(
                five[row : row + 1], (2, LANES)
            )
    four_out[...] = four + w4[...]


def fine_kernel(
    kp, ck, scale, first, cf, beside, base, edge, fp
):
    inner = pl.ds(8, 32)
    lane32 = lanes_of((32, LANES))
    for x in (0, 33):
        fp[x, inner] = jnp.zeros((32, LANES), F32)
    blank = jnp.zeros((8, LANES), F32)

    def fill(x, carry):
        fp[x + 1, inner] = first[x]
        fp[x + 1, 0:8] = blank
        fp[x + 1, 40:48] = blank
        return carry

    lax.fori_loop(0, 32, fill, 0, unroll=4)
    rim_k, rim_f = ck[...], cf[...]

    def slab(x, carry):
        base[x] = second(kp, fp, x, 32, rim_k, rim_f, lane32, LANES, scale[x])
        return carry

    lax.fori_loop(0, 32, slab, 0, unroll=4)
    for n, x in enumerate((0, 31)):
        edge[n] = 0.5 * scale[x] * (kp[rows_of(x + 1, 0, 40, 32)] + beside[n])
    for n, y in enumerate((0, 31)):
        k = kp[pl.ds(48 + y, 32, stride=40), :] + beside[2 + n]
        edge[2 + n] = 0.5 * scale[:, y, :] * k


def three_kernel(
    initial, own, xlo, xhi, ylo, yhi, base, base2, edge, edge2,
    three_out, two_out, fine_out,
    r3, s3, k3, c3, ea, eb, w2,
):
    lane8 = lanes_of((8, LANES))
    for ix in range(3):
        for iy, y_ref in enumerate((ylo, None, yhi)):
            for i in range(8):
                if ix == 1 and iy == 1:
                    r, k, s = [own[f, 8 * i : 8 * i + 8] for f in range(3)]
                else:
                    if iy == 1:
                        r = (xlo if ix == 0 else xhi)[8 * i : 8 * i + 8]
                    else:
                        r = y_ref[64 * ix + 8 * i : 64 * ix + 8 * i + 8]
                    k = turn(r, -43, 1)
                    s = turn(r, -86, 1)
                    if iy == 1 and ((ix == 0 and i == 7) or (ix == 2 and i == 0)):
                        low = (xlo if ix == 0 else xhi)[X_ENDS:X_ROWS]
                        high = turn(low, 42, 1)
                        r = jnp.where(lane8 == 127, low, jnp.where(lane8 == 42, high, r))
                        k = jnp.where(lane8 == 126, low, jnp.where(lane8 == 43, high, k))
                        low, high = turn(low, 2, 1), turn(high, -2, 1)
                        s = jnp.where(lane8 == 127, low, jnp.where(lane8 == 42, high, s))
                x, y = 8 * ix + i, 8 * iy
                r3[x, y : y + 8] = r
                k3[x, y + 8 : y + 16] = k
                s3[x, y : y + 8] = s
    lane1 = lanes_of((1, LANES))
    for y, y_ref in ((7, ylo), (16, yhi)):
        low = y_ref[Y_ENDS:Y_ROWS]
        high = turn(low, 42, 1)
        low_s, high_s = turn(low, 2, 1), turn(high, -2, 1)
        for i in range(8):
            row = slice(i, i + 1)

            def patch(ref, at, below, above, low_lane, high_lane):
                kept = jnp.where(lane1 == high_lane, above[row], ref[8 + i, at : at + 1])
                ref[8 + i, at : at + 1] = jnp.where(lane1 == low_lane, below[row], kept)

            patch(r3, y, low, high, 127, 42)
            patch(k3, y + 8, low, high, 126, 43)
            patch(s3, y, low_s, high_s, 127, 42)
    rim = jnp.zeros((24, 8, LANES), F32)
    for ref in (k3, ea, eb):
        ref[:, 0:8] = rim
        ref[:, 32:40] = rim
    mid = pl.ds(8, 24)

    def setup3(x, carry):
        k = k3[x, mid]
        near = [
            k3[x + 1, mid], k3[x - 1, mid], k3[x, pl.ds(9, 24)], k3[x, pl.ds(7, 24)],
            turn(k, -1, 1), turn(k, 1, 1),
        ]
        h = WEIGHT / (s3[x] + 3.0 * k + 0.5 * sum(near))
        half = 0.5 * h
        for n in range(6):
            c3[n, x] = half * (k + near[n])
        g = h * r3[x]
        c3[6, x] = g
        ea[x, mid] = g
        return carry

    lax.fori_loop(1, 23, setup3, 0, unroll=True)
    source, target = ea, eb
    for step in range(2, COARSE_SWEEPS + 1):

        def sweep3(x, carry, source=source, target=target):
            e = source[x, mid]
            near = [
                source[x + 1, mid], source[x - 1, mid],
                source[x, pl.ds(9, 24)], source[x, pl.ds(7, 24)],
                turn(e, -1, 1), turn(e, 1, 1),
            ]
            total = 0.2 * e + c3[6, x]
            for n in range(6):
                total = total + c3[n, x] * near[n]
            target[x, mid] = total
            return carry

        lax.fori_loop(step, 24 - step, sweep3, 0, unroll=True)
        source, target = target, source

    mine = source[8:16, 16:24]
    lane3 = lanes_of((8, 8, LANES))
    three = flat(jnp.where((lane3 >= BASE) & (lane3 < BASE + 32), mine, 0.0))
    three_out[...] = spread(three, square(lambda row, col: row == BASE + col // 4))

    def beyond(ref, start):
        half = ref[start : start + 8]
        other = turn(half, 64, 1)
        return jnp.concatenate(
            [jnp.where(lane8 < 64, half, other), jnp.where(lane8 < 64, other, half)], 0
        )

    w2[...] = base2[...]
    for n, (x, ref) in enumerate(((0, xlo), (15, xhi))):
        w2[x] = w2[x] + edge2[n] * beyond(ref, X_SEC)
    for n, (y, ref) in enumerate(((0, ylo), (15, yhi))):
        w2[:, y, :] = w2[:, y, :] + edge2[2 + n] * beyond(ref, Y_SEC)
    two_out[...] = spread(flat(w2[...]), square(lambda row, col: row == col // 2))

    def add(x, carry):
        fine_out[x] = initial[x] + base[x]
        return carry

    lax.fori_loop(0, 32, add, 0, unroll=8)
    for n, (x, ref) in enumerate(((0, xlo), (31, xhi))):
        fine_out[x] = fine_out[x] + edge[n] * ref[X_FACE:X_SEC]
    for n, (y, ref) in enumerate(((0, ylo), (31, yhi))):
        fine_out[:, y, :] = fine_out[:, y, :] + edge[2 + n] * ref[Y_FACE:Y_SEC]


def finish_kernel(
    three_in, two_in, four_in, fine_in, out_far, w3, w32, up, out, sems
):
    four = four_in[...]
    for i in range(8):
        block = four[4 * (i // 2) : 4 * (i // 2) + 4]
        w3[i, pl.ds(0, 4, stride=2), :] = block
        w3[i, pl.ds(1, 4, stride=2), :] = block
    three = three_in[...] + flat(w3[...])

    even8, odd8 = pl.ds(0, 8, stride=2), pl.ds(1, 8, stride=2)
    for i in range(16):
        block = three[8 * (i // 2) : 8 * (i // 2) + 8]
        w32[i, even8, :] = block
        w32[i, odd8, :] = block
    two = two_in[...].reshape(16, 16, LANES) + w32[...]
    up[:, pl.ds(0, 16, stride=2), :] = two
    up[:, pl.ds(1, 16, stride=2), :] = two

    depth = 32 // CHUNKS
    copies = []
    for c in range(CHUNKS):
        part = pl.ds(c * depth, depth)
        for x in range(c * depth, (c + 1) * depth):
            out[x] = fine_in[x] + up[x // 2]
        copy = pltpu.make_async_copy(out.at[part], out_far.at[part], sems.at[c])
        copy.start()
        copies.append(copy)
    for copy in copies:
        copy.wait()


VM = pl.BlockSpec(memory_space=pltpu.VMEM)
SM = pl.BlockSpec(memory_space=pltpu.SMEM)
FAR = pl.BlockSpec(memory_space=pltpu.HBM)


def shape(*dims):
    return pltpu.VMEM(dims, F32)


def local(kernel, outs, ins, scratch, name, sems=None, out_spec=VM):
    scratch = [pltpu.VMEM(dims, F32) for dims in scratch]
    if sems is not None:
        scratch.append(pltpu.SemaphoreType.DMA(sems))
    return pl.pallas_call(
        kernel,
        out_shape=outs,
        in_specs=ins,
        out_specs=[out_spec] * len(outs),
        scratch_shapes=scratch,
        compiler_params=pltpu.CompilerParams(vmem_limit_bytes=24 * 1024 * 1024),
        name=name,
    )


def on_device(initial, rhs, kappa, sigma):
    start = initial
    place = jnp.stack([lax.axis_index(axis) for axis in ("gx", "gy", "gz")]).astype(jnp.int32)

    def passed(value, axis, step):
        count = lax.axis_size(axis)
        return lax.ppermute(value, axis, [(i, (i + step) % count) for i in range(count)])

    block = (32, 32, LANES)
    block2 = (16, 16, LANES)
    edge = shape(3, 32, LANES)
    far = [
        pltpu.with_memory_space_constraint(value, pltpu.HBM)
        for value in (kappa, initial)
    ]
    xp, xm, yp, ym, zs, kappa, initial = local(
        faces_kernel,
        [edge, edge, edge, edge, shape(2, 32, LANES)] + [shape(*block)] * 2,
        [FAR] * 2, [], "faces", sems=(2, CHUNKS),
    )(*far)
    zlo, zhi = passed(zs, "gz", 1), passed(zs, "gz", -1)
    xlo, xhi = passed(xp, "gx", 1), passed(xm, "gx", -1)
    ylo, yhi = passed(yp, "gy", 1), passed(ym, "gy", -1)
    kp, ck, diagonal, rest, pair_k, pair_s = local(
        inside_kernel,
        [
            shape(1368, LANES), shape(32, LANES), shape(*block), shape(*block),
            shape(16, 32, LANES), shape(16, 32, LANES),
        ],
        [VM] * 6, [(34, 48, LANES)], "inside",
    )(kappa, initial, rhs, sigma, zlo, zhi)
    (
        scale, first, beside, zp, zm, fives, whole, sides_x, sides_y, kp2, ck2, scale2, first2,
        sides2_x, sides2_y,
    ) = local(
        residual_kernel,
        [
            shape(*block), shape(*block), shape(4, 32, LANES),
            shape(Z_ROWS, LANES), shape(Z_ROWS, LANES), shape(8, LANES),
            shape(64, LANES), shape(2, 32, LANES), shape(2, 32, LANES), shape(440, LANES),
            shape(16, LANES), shape(*block2), shape(*block2), shape(2, 16, LANES),
            shape(2, 16, LANES),
        ],
        [VM] * 11, [(16, 32, LANES), (4, 32, LANES), (8, 16, LANES), (4, 32, LANES)],
        "residual",
    )(kappa, initial, diagonal, rest, ck, pair_k, pair_s, xlo, xhi, ylo, yhi)

    zlo, zhi = passed(zp, "gz", 1), passed(zm, "gz", -1)
    own, xp, xm, ye, cf, cf2, blocks = local(
        window_kernel,
        [
            shape(3, 64, LANES), shape(X_ROWS, LANES), shape(X_ROWS, LANES),
            shape(2, 8, LANES), shape(32, LANES), shape(16, LANES),
            shape(16, 16, LANES),
        ],
        [VM] * 6, [(8, 8, LANES)], "window",
    )(zlo, zhi, fives, whole, sides_x, sides2_x)
    xlo, xhi = passed(xp, "gx", 1), passed(xm, "gx", -1)
    planes = lax.all_to_all(blocks, ("gx", "gy"), 0, 0)
    base, edge = local(
        fine_kernel,
        [shape(*block), shape(4, 32, LANES)], [VM] * 6, [(34, 48, LANES)], "fine",
    )(kp, ck, scale, first, cf, beside)
    base2, edge2 = local(
        second_kernel, [shape(*block2), shape(4, 16, LANES)], [VM] * 5, [(18, 32, LANES)],
        "second",
    )(kp2, ck2, scale2, first2, cf2)
    yp, ym = local(
        columns_kernel, [shape(Y_ROWS, LANES)] * 2, [VM] * 8, [], "columns"
    )(xlo, xhi, xp, sides_y, sides2_y, ye, edge, edge2)
    ylo, yhi = passed(yp, "gy", 1), passed(ym, "gy", -1)
    (ring,) = local(ring_kernel, [shape(3, 64, LANES)], [VM], [], "ring")(planes)
    ring_low, ring_high = passed(ring, "gz", 3), passed(ring, "gz", -3)
    padded3 = (24, 40, LANES)
    block3 = (24, 24, LANES)
    three, two, fine = local(
        three_kernel, [shape(64, LANES), shape(256, LANES), shape(*block)], [VM] * 10,
        [block3, block3, padded3, (7,) + block3, padded3, padded3, block2], "three",
    )(start, own, xlo, xhi, ylo, yhi, base, base2, edge, edge2)
    (four,) = local(
        planes_kernel, [shape(16, LANES)], [SM] + [VM] * 4,
        [
            block2, (8, 8, LANES), (3, 4, 8, LANES), (7,) + block2,
            (7, 8, 8, LANES), (7, 4, 8, LANES), (7, 4, 8, LANES), (16, LANES),
        ],
        "planes",
    )(place, planes, ring, ring_low, ring_high)
    return local(
        finish_kernel, [pltpu.HBM(block, F32)], [VM] * 4,
        [(8, 8, LANES), block2, (16, 32, LANES), block],
        "finish", sems=(CHUNKS,), out_spec=FAR,
    )(three, two, four, fine)[0]


def solution(mesh):
    spec = P("gx", "gy", "gz")
    return jax.shard_map(
        on_device, mesh=mesh, in_specs=(spec,) * 4, out_specs=spec, check_vma=False
    )
```

```python
import jax
import jax.numpy as jnp
from jax import lax
from jax.experimental import pallas as pl
from jax.experimental.pallas import tpu as pltpu
from jax.sharding import PartitionSpec as P

COARSE_SWEEPS = 8
WEIGHT = 0.8
LANES = 128
F32 = jnp.float32
BF16 = jnp.bfloat16

Z_SMALL, Z_ROWS = 32, 40
X_FACE, X_SEC, X_ENDS, X_ROWS = 64, 96, 104, 112
Y_FACE, Y_SEC, Y_ENDS, Y_ROWS = 192, 224, 232, 240
CHUNKS = 2
BASE = 5


def turn(value, shift, axis):
    size = value.shape[axis]
    if isinstance(shift, int):
        shift = shift % size
        if shift == 0:
            return value
    return pltpu.roll(value, shift, axis)


def lanes_of(shape):
    return lax.broadcasted_iota(jnp.int32, shape, len(shape) - 1)


def square(rule):
    row = lax.broadcasted_iota(jnp.int32, (LANES, LANES), 0)
    col = lax.broadcasted_iota(jnp.int32, (LANES, LANES), 1)
    return jnp.where(rule(row, col), 1.0, 0.0).astype(BF16)


def spread(value, chosen):
    total = None
    for part in range(3):
        piece = value.astype(BF16)
        term = jnp.dot(piece, chosen, preferred_element_type=F32)
        total = term if total is None else total + term
        if part < 2:
            value = value - piece.astype(F32)
    return total


def rows_of(x, shift, pitch, count):
    start = pitch * x + 8
    return pl.ds(start + shift if shift else pl.multiple_of(start, 8), count)


def flat(value):
    return value.reshape(-1, LANES)


def fetch(pairs, sems):
    depth = pairs[0][0].shape[0] // CHUNKS
    copies = []
    for c in range(CHUNKS):
        part = pl.ds(c * depth, depth)
        for n, (far, near) in enumerate(pairs):
            copy = pltpu.make_async_copy(far.at[part], near.at[part], sems.at[n, c])
            copy.start()
            copies.append(copy)
    return copies


def faces_kernel(kappa_far, initial_far, xp, xm, yp, ym, zs, kappa, initial, sems):
    depth = 32 // CHUNKS
    copies = fetch(((kappa_far, kappa), (initial_far, initial)), sems)
    lane = lanes_of((32, LANES))
    first = second = jnp.zeros((32, LANES), F32)

    def body(x, carry):
        first, second = carry
        mine = lane // 4 == x
        shift = 4 * x + 2
        first = jnp.where(mine, turn(kappa[x], shift, 1), first)
        second = jnp.where(mine, turn(initial[x], shift, 1), second)
        return first, second

    for c in range(CHUNKS):
        copies[2 * c].wait()
        copies[2 * c + 1].wait()
        first, second = lax.fori_loop(
            c * depth, (c + 1) * depth, body, (first, second), unroll=True
        )
    zs[0] = first
    zs[1] = second
    xp[0] = kappa[31]
    xp[1] = kappa[30]
    xp[2] = initial[31]
    xm[0] = kappa[0]
    xm[1] = kappa[1]
    xm[2] = initial[0]
    yp[0] = kappa[:, 31, :]
    yp[1] = kappa[:, 30, :]
    yp[2] = initial[:, 31, :]
    ym[0] = kappa[:, 0, :]
    ym[1] = kappa[:, 1, :]
    ym[2] = initial[:, 0, :]


def z_sides(value, rim, x, lane, period):
    near = turn(rim, 126 - 4 * x, 1)
    if period < LANES:
        other = turn(rim, lax.rem(190 - 4 * x, 128), 1)
        near = jnp.where((lane >= 32) & (lane < 96), other, near)
    inside = lane % period
    above = turn(jnp.where(inside == 0, near, value), LANES - 1, 1)
    below = turn(jnp.where(inside == period - 1, near, value), 1, 1)
    return above, below


def inside_kernel(
    kappa, initial, rhs, sigma, zlo, zhi, kp, ck, diagonal, rest, pair_k, pair_s, vp
):
    lane = lanes_of((32, LANES))
    inner = pl.ds(8, 32)
    blank, blank8 = jnp.zeros((32, LANES), F32), jnp.zeros((8, LANES), F32)
    for x in (0, 33):
        kp[rows_of(x, 0, 40, 32)] = blank
        vp[x, inner] = blank
    kp[0:8] = blank8
    kp[40 * 33 : 40 * 33 + 8] = blank8
    kp[40 * 34 : 40 * 34 + 8] = blank8

    def fill(x, carry):
        kp[rows_of(x + 1, -8, 40, 8)] = blank8
        kp[rows_of(x + 1, 0, 40, 32)] = kappa[x]
        vp[x + 1, inner] = initial[x]
        vp[x + 1, 0:8] = blank8
        vp[x + 1, 40:48] = blank8
        return carry

    lax.fori_loop(0, 32, fill, 0, unroll=4)
    low_half = lane % 4 < 2
    rim_k = jnp.where(low_half, zlo[0], zhi[0])
    rim_v = jnp.where(low_half, zlo[1], zhi[1])
    ck[...] = rim_k

    def slab(x):
        k = kappa[x]
        v = initial[x]
        around = [
            (kp[rows_of(x, 0, 40, 32)], vp[x, inner]),
            (kp[rows_of(x + 2, 0, 40, 32)], vp[x + 2, inner]),
            (kp[rows_of(x + 1, -1, 40, 32)], vp[x + 1, pl.ds(7, 32)]),
            (kp[rows_of(x + 1, 1, 40, 32)], vp[x + 1, pl.ds(9, 32)]),
        ]
        k_up, k_down = z_sides(k, rim_k, x, lane, LANES)
        v_up, v_down = z_sides(v, rim_v, x, lane, LANES)
        around += [(k_up, v_up), (k_down, v_down)]
        k_sum = sum(kn for kn, _ in around)
        v_sum = sum(vn for _, vn in around)
        both = sum(kn * vn for kn, vn in around)
        s = sigma[x]
        d = s + 3.0 * k + 0.5 * k_sum
        diagonal[x] = d
        rest[x] = rhs[x] - d * v + 0.5 * (k * v_sum + both)
        return k, s

    def two(i, carry):
        k0, s0 = slab(2 * i)
        k1, s1 = slab(2 * i + 1)
        pair_k[i] = k0 + k1
        pair_s[i] = s0 + s1
        return carry

    lax.fori_loop(0, 16, two, 0, unroll=3)


def residual_kernel(
    kappa, initial, diagonal, rest, rim, pair_k, pair_s, xlo, xhi, ylo, yhi,
    scale, first, beside, zp, zm, fives, whole, sides_x, sides_y, kp2, ck2, scale2, first2,
    sides2_x, sides2_y, pair_r, rims, small, fix,
):
    lane = lanes_of((32, LANES))
    row = lax.broadcasted_iota(jnp.int32, (32, LANES), 0)
    rim_k = rim[...]
    for n, message in enumerate((xlo, xhi, ylo, yhi)):
        beside[n] = message[0]

    def beyond(k, v, message):
        kn, vn = message[0], message[2]
        return 0.5 * kn, 0.5 * ((k + kn) * vn - kn * v)

    fix[0], fix[1] = beyond(kappa[:, 0, :], initial[:, 0, :], ylo)
    fix[2], fix[3] = beyond(kappa[:, 31, :], initial[:, 31, :], yhi)

    def slab(x, packed, message=None):
        one = pl.ds(x, 1)
        d, r = diagonal[x], rest[x]
        if message is not None:
            more_d, more_r = beyond(kappa[x], initial[x], message)
            d, r = d + more_d, r + more_r
        d = jnp.where(row == 0, d + fix[0, one], jnp.where(row == 31, d + fix[2, one], d))
        r = jnp.where(row == 0, r + fix[1, one], jnp.where(row == 31, r + fix[3, one], r))
        h = WEIGHT / d
        e = h * r
        scale[x] = h
        first[x] = e
        packed = jnp.where(lane // 4 == x, turn(e, 4 * x + 2, 1), packed)
        return r, packed

    def two(i, packed, low=None, high=None):
        r0, packed = slab(2 * i, packed, low)
        r1, packed = slab(2 * i + 1, packed, high)
        pair_r[i] = r0 + r1
        return packed

    packed = two(0, jnp.zeros((32, LANES), F32), low=xlo)
    packed = lax.fori_loop(1, 15, two, packed, unroll=14)
    packed = two(15, packed, high=xhi)
    sides_x[0] = first[31]
    sides_x[1] = first[0]
    sides_y[0] = first[:, 31, :]
    sides_y[1] = first[:, 0, :]

    even, odd = pl.ds(0, 16, stride=2), pl.ds(1, 16, stride=2)
    to_two = square(lambda row, col: row // 2 == col % 64)

    def level_two(ref, weight):
        summed = ref[:, even, :] + ref[:, odd, :]
        return (spread(flat(summed), to_two) * weight).reshape(16, 16, LANES)

    r2 = level_two(pair_r, 0.5)
    k2 = level_two(pair_k, 0.125)
    s2 = level_two(pair_s, 0.5)
    rims[0] = xlo[0] + xlo[1]
    rims[1] = xhi[0] + xhi[1]
    rims[2] = ylo[0] + ylo[1]
    rims[3] = yhi[0] + yhi[1]
    halo = rims[:, even, :] + rims[:, odd, :]
    halo = (spread(flat(halo), to_two) * 0.125).reshape(4, 16, LANES)
    kp2[rows_of(0, 0, 24, 16)] = halo[0]
    kp2[rows_of(17, 0, 24, 16)] = halo[1]
    for x in range(16):
        kp2[rows_of(x + 1, 0, 24, 16)] = k2[x]
        kp2[rows_of(x + 1, -1, 24, 1)] = halo[2, x : x + 1]
        kp2[rows_of(x + 1, 16, 24, 1)] = halo[3, x : x + 1]
    rims[0] = rim_k
    rim_pair = rims[0, even, :] + rims[0, odd, :]

    def rim_rule(row, col):
        low = (col % 4 == 1) & (row % 4 < 2)
        high = (col % 4 == 2) & (row % 4 >= 2)
        return (row // 8 == col // 4) & (low | high)

    rim_k2 = spread(rim_pair, square(rim_rule)) * 0.125
    ck2[...] = rim_k2
    lane2 = lanes_of((16, LANES))
    packed2 = jnp.zeros((16, LANES), F32)
    for x in range(16):
        k = k2[x]
        up, down = z_sides(k, rim_k2, x, lane2, 64)
        k_sum = (
            kp2[rows_of(x, 0, 24, 16)] + kp2[rows_of(x + 2, 0, 24, 16)]
            + kp2[rows_of(x + 1, -1, 24, 16)] + kp2[rows_of(x + 1, 1, 24, 16)] + up + down
        )
        h = WEIGHT / (s2[x] + 3.0 * k + 0.5 * k_sum)
        e = h * r2[x]
        scale2[x] = h
        first2[x] = e
        packed2 = jnp.where(lane2 // 4 == x, turn(e, 4 * x + 2, 1), packed2)
    sides2_x[0] = first2[15]
    sides2_x[1] = first2[0]
    sides2_y[0] = first2[:, 15, :]
    sides2_y[1] = first2[:, 0, :]

    even8, odd8 = pl.ds(0, 8, stride=2), pl.ds(1, 8, stride=2)

    def level_three(field, part, weight):
        halves = field.reshape(8, 2, 16, LANES)
        small[...] = halves[:, 0] + halves[:, 1]
        summed = small[:, even8, :] + small[:, odd8, :]
        rule = square(lambda row, col: (row < 64) & (row // 2 == col - 32 * part))
        return spread(flat(summed), rule) * weight

    three = level_three(r2, 0, 0.5) + level_three(k2, 1, 0.125) + level_three(s2, 2, 0.5)
    whole[...] = three
    cubes = three.reshape(2, 4, 8, LANES)
    small[0:2, 0:8] = cubes[:, 0] + cubes[:, 1] + cubes[:, 2] + cubes[:, 3]
    quads = [small[0:2, pl.ds(j, 2, stride=4), :] for j in range(4)]
    quad = quads[0] + quads[1] + quads[2] + quads[3]
    small[2, 0:8] = jnp.zeros((8, LANES), F32)
    small[2, 0:2] = quad[0]
    small[2, 2:4] = quad[1]
    five = spread(small[2, 0:8], square(lambda row, col: (row < 96) & (row // 4 == col - 64)))
    lane8 = lanes_of((8, LANES))
    five = five * jnp.where((lane8 >= 72) & (lane8 < 80), 1.0 / 64.0, 0.25)
    fives[...] = five
    for out, start, tag in ((zp, 16, 1), (zm, 0, 2)):
        half = spread(
            three,
            square(
                lambda row, col, start=start: (col < 48)
                & (row == 32 * (col // 16) + start + col % 16)
            ),
        )
        face = spread(packed, square(lambda row, col, tag=tag: row == 4 * (col - 96) + tag))
        out[0:Z_SMALL] = half[0:32] + turn(half[32:64], 48, 1) + face
        face2 = spread(
            packed2, square(lambda row, col, tag=tag: (col < 16) & (row == 4 * col + tag))
        )
        out[Z_SMALL:Z_ROWS] = face2[0:8] + turn(face2[8:16], 16, 1) + five


def second(k_ref, f_ref, x, rows, k_rim, f_rim, lane, period, h):
    inside, pitch = pl.ds(8, rows), rows + 8
    k, e = k_ref[rows_of(x + 1, 0, pitch, rows)], f_ref[x + 1, inside]
    k_up, k_down = z_sides(k, k_rim, x, lane, period)
    e_up, e_down = z_sides(e, f_rim, x, lane, period)
    around = [
        (k_ref[rows_of(x, 0, pitch, rows)], f_ref[x, inside]),
        (k_ref[rows_of(x + 2, 0, pitch, rows)], f_ref[x + 2, inside]),
        (k_ref[rows_of(x + 1, -1, pitch, rows)], f_ref[x + 1, pl.ds(7, rows)]),
        (k_ref[rows_of(x + 1, 1, pitch, rows)], f_ref[x + 1, pl.ds(9, rows)]),
        (k_up, e_up),
        (k_down, e_down),
    ]
    total = k * sum(en for _, en in around) + sum(kn * en for kn, en in around)
    return 1.2 * e + 0.5 * h * total


def window_kernel(
    zlo, zhi, fives, whole, sides, sides2,
    own, xp, xm, ye, cf, cf2, blocks, small,
):
    lane = lanes_of((64, LANES))
    a_half, c_half = zlo[0:Z_SMALL], zhi[0:Z_SMALL]
    a = jnp.concatenate([a_half, turn(a_half, -48, 1)], 0)
    b = whole[...]
    c = jnp.concatenate([c_half, turn(c_half, -48, 1)], 0)

    def window(part):
        low = turn(a, BASE - 16 - 16 * part, 1)
        mid = turn(b, BASE - 32 * part, 1)
        high = turn(c, BASE + 32 - 16 * part, 1)
        value = jnp.where((lane < BASE) | (lane >= 112 + BASE), low, mid)
        value = jnp.where((lane >= BASE + 32) & (lane < BASE + 48), high, value)
        return jnp.where((lane >= BASE + 48) & (lane < 112 + BASE), 0.0, value)

    r, k, s = window(0), window(1), window(2)
    own[0], own[1], own[2] = r, k, s

    even, odd = pl.ds(0, 4, stride=2), pl.ds(1, 4, stride=2)

    def shrink(field, part, weight):
        halves = field.reshape(4, 2, 8, LANES)
        small[0:4] = halves[:, 0] + halves[:, 1]
        summed = small[0:4, even, :] + small[0:4, odd, :]
        for i in range(4):
            small[4 + i // 2, 4 * (i % 2) : 4 * (i % 2) + 4] = summed[i]

        def rule(row, col):
            cell = (row + 16 - BASE) % LANES
            return (cell < 64) & (cell // 2 == col - 32 * part)

        return spread(flat(small[4:6]), square(rule)) * weight

    four = shrink(r, 0, 0.5) + shrink(k, 1, 0.125) + shrink(s, 2, 0.5)
    lane8 = lanes_of((8, LANES))
    for n, ref in enumerate((zlo[Z_SMALL:Z_ROWS], fives[...], zhi[Z_SMALL:Z_ROWS])):
        small[4 + n // 2, 4 * (n % 2) : 4 * (n % 2) + 4] = turn(ref, 32, 1)[0:4]
    small[5, 4:8] = jnp.zeros((4, LANES), F32)
    lane4 = lanes_of((16, LANES))
    four = jnp.where((lane4 < 96) | (lane4 >= 120), four, flat(small[4:6]))
    for q in range(16):
        blocks[q] = four
    main = jnp.where(lane < 42, r, jnp.where(lane < 86, turn(k, 43, 1), turn(s, 86, 1)))
    low = jnp.where(lane == 127, r, jnp.where(lane == 126, k, turn(s, -2, 1)))
    high = jnp.where(lane == 42, r, jnp.where(lane == 43, k, turn(s, 2, 1)))
    ends = jnp.where(lane >= 64, low, turn(high, 86, 1))
    small[...] = ends.reshape(8, 8, LANES)
    ye[0] = small[:, 7, :]
    ye[1] = small[:, 0, :]
    for side, out, i in ((0, xp, 7), (1, xm, 0)):
        out[0:X_FACE] = main
        out[X_FACE:X_SEC] = sides[side]
        out[X_SEC:X_ENDS] = jnp.where(lane8 < 64, sides2[side, 0:8], sides2[side, 8:16])
        out[X_ENDS:X_ROWS] = ends[8 * i : 8 * i + 8]

    def rim(low, high, ready):
        below = spread(low, square(lambda row, col: ready(row) & (col == 4 * (row % 32) + 1)))
        above = spread(high, square(lambda row, col: ready(row) & (col == 4 * (row % 32) + 2)))
        return below + above

    cf[...] = rim(a_half, c_half, lambda row: row >= 96)

    def unfold(half):
        return jnp.concatenate([half, turn(half, -16, 1)], 0)

    cf2[...] = rim(unfold(zlo[Z_SMALL:Z_ROWS]), unfold(zhi[Z_SMALL:Z_ROWS]), lambda row: row < 16)


def second_kernel(kp2, ck2, scale2, first2, cf2, base2, edge2, fp2):
    rim_f2 = cf2[...]
    rim_k2 = ck2[...]
    lane2 = lanes_of((16, LANES))
    inner2 = pl.ds(8, 16)
    fp2[1:17, inner2] = first2[...]
    for x in (0, 17):
        fp2[x, inner2] = jnp.zeros((16, LANES), F32)
    fp2[:, 0:8] = jnp.zeros((18, 8, LANES), F32)
    fp2[:, 24:32] = jnp.zeros((18, 8, LANES), F32)
    def slab(x, carry):
        base2[x] = second(kp2, fp2, x, 16, rim_k2, rim_f2, lane2, 64, scale2[x])
        return carry

    lax.fori_loop(0, 16, slab, 0, unroll=8)
    for n, (x, step) in enumerate(((0, -1), (15, 1))):
        k = kp2[rows_of(x + 1, 0, 24, 16)] + kp2[rows_of(x + 1 + step, 0, 24, 16)]
        edge2[n] = 0.5 * scale2[x] * k
    for n, (y, step) in enumerate(((0, -1), (15, 1))):
        k = kp2[pl.ds(32 + y, 16, stride=24), :] + kp2[pl.ds(32 + y + step, 16, stride=24), :]
        edge2[2 + n] = 0.5 * scale2[:, y, :] * k


def columns_kernel(xlo, xhi, xp, sides, sides2, ye, after, after2, yp, ym):
    lane8 = lanes_of((8, LANES))
    for side, out in ((0, yp), (1, ym)):
        out[0:64] = xlo[0:64]
        out[64:128] = xp[0:64]
        out[128:192] = xhi[0:64]
        out[Y_FACE:Y_SEC] = sides[side]
        face = sides2.at[side]
        out[Y_SEC:Y_ENDS] = jnp.where(lane8 < 64, face[0:8], face[8:16])
        out[Y_ENDS:Y_ROWS] = ye[side]


def wrapped(value):
    last = value.shape[0] - 1
    return [
        jnp.concatenate([value[1:], value[:1]], 0),
        jnp.concatenate([value[last:], value[:last]], 0),
        turn(value, -1, 1),
        turn(value, 1, 1),
        turn(value, -1, 2),
        turn(value, 1, 2),
    ]


def periodic_setup(r, k, s, coefs):
    near = wrapped(k)
    diagonal = s + 3.0 * k + 0.5 * sum(near)
    h = WEIGHT / diagonal
    half = 0.5 * h
    for n in range(6):
        coefs[n] = half * (k + near[n])
    start = h * r
    coefs[6] = start
    return start


def periodic_sweep(e, coefs):
    total = 0.2 * e + coefs[6]
    for n, other in enumerate(wrapped(e)):
        total = total + coefs[n] * other
    return total


def ring_kernel(blocks, ring):
    for x in range(8):
        for n in range(3):
            start = 4 * n + 2 * (x % 2)
            pieces = [blocks[4 * (x // 2) + y, start : start + 2] for y in range(4)]
            ring[n, 8 * x : 8 * x + 8] = jnp.concatenate(pieces, 0)


def planes_kernel(
    place, blocks, ring, low, high, four_out, l4, l5, l6, c4, c5, c6, c7, w4
):
    gx, gy = place[0], place[1]
    for q in range(16):
        for i in range(4):
            l4[4 * (q // 4) + i, 4 * (q % 4) : 4 * (q % 4) + 4] = blocks[q, 4 * i : 4 * i + 4]
    lane = lanes_of((8, 8, LANES))

    def field(f):
        value = jnp.zeros((8, 8, LANES), F32)
        for ref, first in ((high, 2), (low, -4), (ring, -1)):
            for n in range(3):
                start = 8 * (first + n) % 64
                moved = turn(ref[n].reshape(8, 8, LANES), start - 96 - 8 * f, 2)
                value = jnp.where(lane // 8 == start // 8, moved, value)
        return jnp.where(lane < 64, value, turn(value, 64, 2))

    to_six = square(lambda row, col: (row < 64) & (row // 2 == col % 32))
    mean = square(lambda row, col: row < 32)

    def level_six(values, weight, n):
        pairs = values.reshape(4, 2, 8, LANES)
        l6[n] = pairs[:, 0] + pairs[:, 1]
        summed = l6[n, :, pl.ds(0, 4, stride=2), :] + l6[n, :, pl.ds(1, 4, stride=2), :]
        l6[n, :, 0:4] = summed
        l6[n, :, 4:8] = summed
        return (spread(flat(l6[n]), to_six) * weight).reshape(4, 8, LANES)

    def level_seven(values):
        return (spread(flat(values), mean) * (1.0 / 32.0)).reshape(4, 8, LANES)

    fields5 = [field(f) for f in range(3)]
    fields6 = [level_six(v, w, n) for n, (v, w) in enumerate(zip(fields5, (0.5, 0.125, 0.5)))]
    fields7 = [level_seven(v) for v in fields6]
    r4 = l4[0:16]
    e4 = periodic_setup(r4, turn(r4, 96, 2), turn(r4, 64, 2), c4)
    e5 = periodic_setup(*fields5, c5)
    e6 = periodic_setup(*fields6, c6)
    e7 = periodic_setup(*fields7, c7)

    def sweep(_, carry):
        a, b, c, d = carry
        return (
            periodic_sweep(a, c4), periodic_sweep(b, c5), periodic_sweep(c, c6),
            periodic_sweep(d, c7),
        )

    e4, e5, e6, e7 = lax.fori_loop(0, COARSE_SWEEPS - 1, sweep, (e4, e5, e6, e7))
    l6[0] = e6 + e7
    six = l6[0, gx, pl.ds(gy, 1)] + jnp.zeros((8, LANES), F32)
    six = spread(six, square(lambda row, col: row == col // 32))
    l5[0:8] = e5
    w4[0:16] = jnp.zeros((16, LANES), F32)
    w4[0:2] = l5[2 * gx, pl.ds(2 * gy, 2)]
    w4[2:4] = l5[2 * gx + 1, pl.ds(2 * gy, 2)]
    five = six + spread(w4[0:8], square(lambda row, col: row == col // 16))
    l4[0:16] = e4
    for i in range(4):
        w4[4 * i : 4 * i + 4] = l4[4 * gx + i, pl.ds(4 * gy, 4)]
    lane16 = lanes_of((16, LANES))
    four = jnp.where((lane16 >= 8) & (lane16 < 24), w4[0:16], 0.0)
    four = spread(four, square(lambda row, col: row == 8 + col // 8))
    for i in range(4):
        for j in range(2):
            row = 2 * (i // 2) + j
            w4[4 * i + 2 * j : 4 * i + 2 * j + 2] = jnp.broadcast_to(
                five[row : row + 1], (2, LANES)
            )
    four_out[...] = four + w4[0:16]


def fine_kernel(
    kp, ck, scale, first, cf, beside, base, edge, fp
):
    inner = pl.ds(8, 32)
    lane32 = lanes_of((32, LANES))
    for x in (0, 33):
        fp[x, inner] = jnp.zeros((32, LANES), F32)
    blank = jnp.zeros((8, LANES), F32)

    def fill(x, carry):
        fp[x + 1, inner] = first[x]
        fp[x + 1, 0:8] = blank
        fp[x + 1, 40:48] = blank
        return carry

    lax.fori_loop(0, 32, fill, 0, unroll=4)
    rim_k, rim_f = ck[...], cf[...]

    def slab(x, carry):
        base[x] = second(kp, fp, x, 32, rim_k, rim_f, lane32, LANES, scale[x])
        return carry

    lax.fori_loop(0, 32, slab, 0, unroll=4)
    for n, x in enumerate((0, 31)):
        edge[n] = 0.5 * scale[x] * (kp[rows_of(x + 1, 0, 40, 32)] + beside[n])
    for n, y in enumerate((0, 31)):
        k = kp[pl.ds(48 + y, 32, stride=40), :] + beside[2 + n]
        edge[2 + n] = 0.5 * scale[:, y, :] * k


def three_kernel(
    initial, own, xlo, xhi, ylo, yhi, base, base2, edge, edge2,
    three_out, two_out, fine_out,
    r3, s3, k3, c3, ea, eb, w2,
):
    lane8 = lanes_of((8, LANES))
    for ix in range(3):
        for iy, y_ref in enumerate((ylo, None, yhi)):
            for i in range(8):
                if ix == 1 and iy == 1:
                    r, k, s = [own[f, 8 * i : 8 * i + 8] for f in range(3)]
                else:
                    if iy == 1:
                        r = (xlo if ix == 0 else xhi)[8 * i : 8 * i + 8]
                    else:
                        r = y_ref[64 * ix + 8 * i : 64 * ix + 8 * i + 8]
                    k = turn(r, -43, 1)
                    s = turn(r, -86, 1)
                    if iy == 1 and ((ix == 0 and i == 7) or (ix == 2 and i == 0)):
                        low = (xlo if ix == 0 else xhi)[X_ENDS:X_ROWS]
                        high = turn(low, 42, 1)
                        r = jnp.where(lane8 == 127, low, jnp.where(lane8 == 42, high, r))
                        k = jnp.where(lane8 == 126, low, jnp.where(lane8 == 43, high, k))
                        low, high = turn(low, 2, 1), turn(high, -2, 1)
                        s = jnp.where(lane8 == 127, low, jnp.where(lane8 == 42, high, s))
                x, y = 8 * ix + i, 8 * iy
                r3[x, y : y + 8] = r
                k3[x, y + 8 : y + 16] = k
                s3[x, y : y + 8] = s
    lane1 = lanes_of((1, LANES))
    for y, y_ref in ((7, ylo), (16, yhi)):
        low = y_ref[Y_ENDS:Y_ROWS]
        high = turn(low, 42, 1)
        low_s, high_s = turn(low, 2, 1), turn(high, -2, 1)
        for i in range(8):
            row = slice(i, i + 1)

            def patch(ref, at, below, above, low_lane, high_lane):
                kept = jnp.where(lane1 == high_lane, above[row], ref[8 + i, at : at + 1])
                ref[8 + i, at : at + 1] = jnp.where(lane1 == low_lane, below[row], kept)

            patch(r3, y, low, high, 127, 42)
            patch(k3, y + 8, low, high, 126, 43)
            patch(s3, y, low_s, high_s, 127, 42)
    rim = jnp.zeros((24, 8, LANES), F32)
    for ref in (k3, ea, eb):
        ref[:, 0:8] = rim
        ref[:, 32:40] = rim
    mid = pl.ds(8, 24)

    def setup3(x, carry):
        k = k3[x, mid]
        near = [
            k3[x + 1, mid], k3[x - 1, mid], k3[x, pl.ds(9, 24)], k3[x, pl.ds(7, 24)],
            turn(k, -1, 1), turn(k, 1, 1),
        ]
        h = WEIGHT / (s3[x] + 3.0 * k + 0.5 * sum(near))
        half = 0.5 * h
        for n in range(6):
            c3[n, x] = half * (k + near[n])
        g = h * r3[x]
        c3[6, x] = g
        ea[x, mid] = g
        return carry

    lax.fori_loop(1, 23, setup3, 0, unroll=True)
    source, target = ea, eb
    for step in range(2, COARSE_SWEEPS + 1):

        def sweep3(x, carry, source=source, target=target):
            e = source[x, mid]
            near = [
                source[x + 1, mid], source[x - 1, mid],
                source[x, pl.ds(9, 24)], source[x, pl.ds(7, 24)],
                turn(e, -1, 1), turn(e, 1, 1),
            ]
            total = 0.2 * e + c3[6, x]
            for n in range(6):
                total = total + c3[n, x] * near[n]
            target[x, mid] = total
            return carry

        lax.fori_loop(step, 24 - step, sweep3, 0, unroll=True)
        source, target = target, source

    mine = source[8:16, 16:24]
    lane3 = lanes_of((8, 8, LANES))
    three = flat(jnp.where((lane3 >= BASE) & (lane3 < BASE + 32), mine, 0.0))
    three_out[...] = spread(three, square(lambda row, col: row == BASE + col // 4))

    def beyond(ref, start):
        half = ref[start : start + 8]
        other = turn(half, 64, 1)
        return jnp.concatenate(
            [jnp.where(lane8 < 64, half, other), jnp.where(lane8 < 64, other, half)], 0
        )

    w2[...] = base2[...]
    for n, (x, ref) in enumerate(((0, xlo), (15, xhi))):
        w2[x] = w2[x] + edge2[n] * beyond(ref, X_SEC)
    for n, (y, ref) in enumerate(((0, ylo), (15, yhi))):
        w2[:, y, :] = w2[:, y, :] + edge2[2 + n] * beyond(ref, Y_SEC)
    two_out[...] = spread(flat(w2[...]), square(lambda row, col: row == col // 2))

    def add(x, carry):
        fine_out[x] = initial[x] + base[x]
        return carry

    lax.fori_loop(0, 32, add, 0, unroll=8)
    for n, (x, ref) in enumerate(((0, xlo), (31, xhi))):
        fine_out[x] = fine_out[x] + edge[n] * ref[X_FACE:X_SEC]
    for n, (y, ref) in enumerate(((0, ylo), (31, yhi))):
        fine_out[:, y, :] = fine_out[:, y, :] + edge[2 + n] * ref[Y_FACE:Y_SEC]


def finish_kernel(
    three_in, two_in, four_in, fine_in, out_far, w3, w32, up, out, sems
):
    four = four_in[...]
    for i in range(8):
        block = four[4 * (i // 2) : 4 * (i // 2) + 4]
        w3[i, pl.ds(0, 4, stride=2), :] = block
        w3[i, pl.ds(1, 4, stride=2), :] = block
    three = three_in[...] + flat(w3[0:8])

    even8, odd8 = pl.ds(0, 8, stride=2), pl.ds(1, 8, stride=2)
    for i in range(16):
        block = three[8 * (i // 2) : 8 * (i // 2) + 8]
        w32[i, even8, :] = block
        w32[i, odd8, :] = block
    two = two_in[...].reshape(16, 16, LANES) + w32[...]
    up[:, pl.ds(0, 16, stride=2), :] = two
    up[:, pl.ds(1, 16, stride=2), :] = two

    depth = 32 // CHUNKS
    copies = []
    for c in range(CHUNKS):
        part = pl.ds(c * depth, depth)
        for x in range(c * depth, (c + 1) * depth):
            out[x] = fine_in[x] + up[x // 2]
        copy = pltpu.make_async_copy(out.at[part], out_far.at[part], sems.at[c])
        copy.start()
        copies.append(copy)
    for copy in copies:
        copy.wait()


VM = pl.BlockSpec(memory_space=pltpu.VMEM)
SM = pl.BlockSpec(memory_space=pltpu.SMEM)
FAR = pl.BlockSpec(memory_space=pltpu.HBM)


def shape(*dims):
    return pltpu.VMEM(dims, F32)


def local(kernel, outs, ins, scratch, name, sems=None, out_spec=VM):
    scratch = [pltpu.VMEM(dims, F32) for dims in scratch]
    if sems is not None:
        scratch.append(pltpu.SemaphoreType.DMA(sems))
    return pl.pallas_call(
        kernel,
        out_shape=outs,
        in_specs=ins,
        out_specs=[out_spec] * len(outs),
        scratch_shapes=scratch,
        compiler_params=pltpu.CompilerParams(vmem_limit_bytes=24 * 1024 * 1024),
        name=name,
    )


def on_device(initial, rhs, kappa, sigma):
    start = initial
    place = jnp.stack([lax.axis_index(axis) for axis in ("gx", "gy", "gz")]).astype(jnp.int32)

    def passed(value, axis, step):
        count = lax.axis_size(axis)
        return lax.ppermute(value, axis, [(i, (i + step) % count) for i in range(count)])

    block = (32, 32, LANES)
    block2 = (16, 16, LANES)
    edge = shape(3, 32, LANES)
    far = [
        pltpu.with_memory_space_constraint(value, pltpu.HBM)
        for value in (kappa, initial)
    ]
    xp, xm, yp, ym, zs, kappa, initial = local(
        faces_kernel,
        [edge, edge, edge, edge, shape(2, 32, LANES)] + [shape(*block)] * 2,
        [FAR] * 2, [], "faces", sems=(2, CHUNKS),
    )(*far)
    zlo, zhi = passed(zs, "gz", 1), passed(zs, "gz", -1)
    xlo, xhi = passed(xp, "gx", 1), passed(xm, "gx", -1)
    ylo, yhi = passed(yp, "gy", 1), passed(ym, "gy", -1)
    kp, ck, diagonal, rest, pair_k, pair_s = local(
        inside_kernel,
        [
            shape(1368, LANES), shape(32, LANES), shape(*block), shape(*block),
            shape(16, 32, LANES), shape(16, 32, LANES),
        ],
        [VM] * 6, [(34, 48, LANES)], "inside",
    )(kappa, initial, rhs, sigma, zlo, zhi)
    (
        scale, first, beside, zp, zm, fives, whole, sides_x, sides_y, kp2, ck2, scale2, first2,
        sides2_x, sides2_y,
    ) = local(
        residual_kernel,
        [
            shape(*block), shape(*block), shape(4, 32, LANES),
            shape(Z_ROWS, LANES), shape(Z_ROWS, LANES), shape(8, LANES),
            shape(64, LANES), shape(2, 32, LANES), shape(2, 32, LANES), shape(440, LANES),
            shape(16, LANES), shape(*block2), shape(*block2), shape(2, 16, LANES),
            shape(2, 16, LANES),
        ],
        [VM] * 11, [(16, 32, LANES), (4, 32, LANES), (8, 16, LANES), (5, 32, LANES)],
        "residual",
    )(kappa, initial, diagonal, rest, ck, pair_k, pair_s, xlo, xhi, ylo, yhi)

    zlo, zhi = passed(zp, "gz", 1), passed(zm, "gz", -1)
    own, xp, xm, ye, cf, cf2, blocks = local(
        window_kernel,
        [
            shape(3, 64, LANES), shape(X_ROWS, LANES), shape(X_ROWS, LANES),
            shape(2, 8, LANES), shape(32, LANES), shape(16, LANES),
            shape(16, 16, LANES),
        ],
        [VM] * 6, [(8, 8, LANES)], "window",
    )(zlo, zhi, fives, whole, sides_x, sides2_x)
    xlo, xhi = passed(xp, "gx", 1), passed(xm, "gx", -1)
    planes = lax.all_to_all(blocks, ("gx", "gy"), 0, 0)
    base, edge = local(
        fine_kernel,
        [shape(*block), shape(4, 32, LANES)], [VM] * 6, [(34, 48, LANES)], "fine",
    )(kp, ck, scale, first, cf, beside)
    base2, edge2 = local(
        second_kernel, [shape(*block2), shape(4, 16, LANES)], [VM] * 5, [(18, 32, LANES)],
        "second",
    )(kp2, ck2, scale2, first2, cf2)
    yp, ym = local(
        columns_kernel, [shape(Y_ROWS, LANES)] * 2, [VM] * 8, [], "columns"
    )(xlo, xhi, xp, sides_y, sides2_y, ye, edge, edge2)
    ylo, yhi = passed(yp, "gy", 1), passed(ym, "gy", -1)
    (ring,) = local(ring_kernel, [shape(3, 64, LANES)], [VM], [], "ring")(planes)
    ring_low, ring_high = passed(ring, "gz", 3), passed(ring, "gz", -3)
    padded3 = (24, 40, LANES)
    block3 = (24, 24, LANES)
    three, two, fine = local(
        three_kernel, [shape(64, LANES), shape(256, LANES), shape(*block)], [VM] * 10,
        [block3, block3, padded3, (7,) + block3, padded3, padded3, block2], "three",
    )(start, own, xlo, xhi, ylo, yhi, base, base2, edge, edge2)
    (four,) = local(
        planes_kernel, [shape(16, LANES)], [SM] + [VM] * 4,
        [
            (17, 16, LANES), (9, 8, LANES), (4, 4, 8, LANES), (7,) + block2,
            (7, 8, 8, LANES), (7, 4, 8, LANES), (7, 4, 8, LANES), (24, LANES),
        ],
        "planes",
    )(place, planes, ring, ring_low, ring_high)
    return local(
        finish_kernel, [pltpu.HBM(block, F32)], [VM] * 4,
        [(9, 8, LANES), block2, (16, 32, LANES), block],
        "finish", sems=(CHUNKS,), out_spec=FAR,
    )(three, two, four, fine)[0]


def solution(mesh):
    spec = P("gx", "gy", "gz")
    return jax.shard_map(
        on_device, mesh=mesh, in_specs=(spec,) * 4, out_specs=spec, check_vma=False
    )
```
